32 devices in a mesh: groups: 2 (over x), grid: 8 (over z, y), band: 2 (over core).
Axes of the slice: x: 2, y: 2, z: 4, core: 2. Of those that a mesh axis runs over, the one named last changes fastest.
Arguments:
- wavefunctions: bfloat16 [1024, 32768], P(('groups', 'grid', 'band')), parts along dimension 0, may hold values from -6 to 6
- tile_segment: int32 [3072], P('grid'), may hold values from 0 to 63
- tile_block: int32 [3072], P('grid'), may hold values from 0 to 31
- tile_count: int32 [8], P('grid'), may hold values from 48 to 384, as said below
- projectors: bfloat16 [3072, 64, 128], P('grid'), may hold values from -0.75 to 0.75
- coupling: float32 [32, 16, 8, 8], replicated, may hold values from -0.1875 to 0.1875
Outputs:
- applied_field: bfloat16 [1024, 32768], P(('groups', 'grid', 'band')), parts along dimension 0
The draws below stay inside these ranges and needn't reach their ends.
There are 2 independent parts, one for each index of `groups`. The reference program is written for one: setup_inputs(seed, part) draws one part's arguments, and reference() takes and returns one part's arrays. A program takes and returns all parts, laid end to end along the dimension named above; an argument that names none is the same for every part. Nothing has to cross between parts.
Inputs may be any that keep to these rules, and one draw needn't show every extreme that they name: `tile_count`: some grid index has exactly 384 live slots; every other has 48 to 192.
All inputs are finite; a program needn't handle non-finite values.
Results may differ from the reference program's by a relative error of at most 0.0063.
Values may be sent and summed in bfloat16 or wider, within the bound.
No kernel may reach another device: no remote copies, remote signals or barrier semaphores. Data moves between devices by JAX's collectives and lax.ppermute only.
A program may use at most 128 MiB of HBM per device.

```python
import jax
import jax.numpy as jnp
from jax import lax

PROJ = 128
APROJ = 8
ATOMS = 16
TILE = 64
NB = 512
PTS_DEV = 4096
TILES_DEV = 384
NABLK = 32
NPTS = 32768
NTILES = 3072
N_GRID = 8


def draw_tile_count(key, part):
    key = jax.random.fold_in(key, 11)
    low_key, full_key = jax.random.split(key)
    counts = jax.random.randint(low_key, (N_GRID,), TILES_DEV // 8, TILES_DEV // 2 + 1)
    busiest = jax.random.randint(full_key, (), 0, N_GRID)
    return jnp.where(jnp.arange(N_GRID) == busiest, TILES_DEV, counts).astype(jnp.int32)


def touch_ends(entries, stream_key, smallest, top_value):
    longest = entries.shape.index(max(entries.shape))
    spots = []
    for shift in (0, 1):
        where = [jax.random.randint(jax.random.fold_in(stream_key, axis), (), 0, length) for axis, length in enumerate(entries.shape)]
        where[longest] = (where[longest] + shift) % entries.shape[longest]
        spots.append(tuple(where))
    return entries.at[spots[0]].set(smallest).at[spots[1]].set(top_value)


def level_of(key, extent, cuts, low, top_value):
    factor_of = 1.0
    for position, shards_of in cuts:
        heights = jax.random.uniform(jax.random.fold_in(jax.random.fold_in(key, 6), position), (shards_of,), jnp.float32, low / len(cuts), top_value / len(cuts))
        factor_of = factor_of * jnp.repeat(jnp.exp(heights), extent[position] // shards_of).reshape((-1,) + (1,) * (len(extent) - 1 - position))
    return factor_of


def gaussian(key, dims, scale, bound, cuts=(), kind=jnp.bfloat16):
    array = scale * jax.random.normal(key, dims, jnp.float32)
    if cuts:
        array = array * level_of(key, dims, cuts, -0.22, 0.18)
    return jnp.clip(array, -bound, bound).astype(kind)


def setup_inputs(seed: int = 0, part: int = 0) -> dict:
    splits = jax.random.split(jax.random.key(seed), 7)
    part_splits = jax.random.split(jax.random.fold_in(splits[6], part), 7)
    return {
        "wavefunctions": gaussian(part_splits[0], (NB, NPTS), 1.0, 6.0, ((0, 16),)),
        "tile_segment": touch_ends(jax.random.randint(splits[1], (NTILES,), 0, PTS_DEV // TILE), jax.random.fold_in(splits[1], 1), 0, (PTS_DEV // TILE) - 1).astype(jnp.int32),
        "tile_block": touch_ends(jax.random.randint(splits[2], (NTILES,), 0, NABLK), jax.random.fold_in(splits[2], 1), 0, NABLK - 1).astype(jnp.int32),
        "tile_count": draw_tile_count(jax.random.fold_in(splits[6], 71), part),
        "projectors": gaussian(splits[4], (NTILES, TILE, PROJ), TILE ** -0.5, 0.75, ((0, 8),)),
        "coupling": gaussian(splits[5], (NABLK, ATOMS, APROJ, APROJ), (APROJ * PROJ * N_GRID * TILES_DEV * TILES_DEV // (NABLK * (PTS_DEV // TILE) * 640)) ** -0.5, 0.1875, (), jnp.float32),
    }


def settle(values):
    return lax.optimization_barrier(values.astype(jnp.bfloat16)).astype(jnp.float32)


def reference(wavefunctions, tile_segment, tile_block, tile_count, projectors, coupling):
    bands = wavefunctions.shape[0]
    seg_dev = PTS_DEV // TILE
    by_device = wavefunctions.reshape(bands, N_GRID, seg_dev, TILE).transpose(1, 0, 2, 3)
    segment_ids = tile_segment.reshape(N_GRID, TILES_DEV)
    block_ids = tile_block.reshape(N_GRID, TILES_DEV)
    tile_values = projectors.reshape(N_GRID, TILES_DEV, TILE, PROJ)
    live = (jnp.arange(TILES_DEV, dtype=jnp.int32)[None, :] < tile_count[:, None]).astype(jnp.float32)

    def forward(total, inputs):
        local, segment_row, block_row, values, alive = inputs
        gathered = jnp.take(local, segment_row, axis=1).astype(jnp.float32)
        contrib = jnp.einsum("btr,trp->tbp", gathered, values.astype(jnp.float32))
        contrib = settle(contrib) * alive[:, None, None]
        return total + jax.ops.segment_sum(contrib, block_row, num_segments=NABLK), None

    start = jnp.zeros((NABLK, bands, PROJ), jnp.float32)
    coefficients, unused = lax.scan(forward, start, (by_device, segment_ids, block_ids, tile_values, live))
    per_atom = coefficients.reshape(NABLK, bands, ATOMS, APROJ)
    applied = jnp.einsum("abmj,amjk->abmk", per_atom, coupling.astype(jnp.float32), precision=lax.Precision.HIGHEST)
    applied = applied.reshape(NABLK, bands, PROJ).astype(jnp.bfloat16)

    def backward(inputs):
        segment_row, block_row, values, alive = inputs
        picked = jnp.take(applied, block_row, axis=0).astype(jnp.float32)
        spread = jnp.einsum("tbp,trp->tbr", picked, values.astype(jnp.float32))
        spread = settle(spread) * alive[:, None, None]
        summed = jax.ops.segment_sum(spread, segment_row, num_segments=seg_dev)
        return summed.transpose(1, 0, 2).reshape(bands, PTS_DEV).astype(jnp.bfloat16)

    result = lax.map(backward, (segment_ids, block_ids, tile_values, live))
    return result.transpose(1, 0, 2).reshape(bands, N_GRID * PTS_DEV)
```

```python
import functools

import jax
import jax.numpy as jnp
from jax import lax
from jax.experimental import pallas as pl
from jax.experimental.pallas import tpu as pltpu
from jax.sharding import PartitionSpec as P

TILE = 64
PAIR = 2 * TILE
UNROLL = 8
VMEM_LIMIT = 56 * 1024 * 1024


def padded_tile(values, half):
    zero = jnp.zeros_like(values)
    return jnp.concatenate(
        [jnp.where(half == 0, values, zero), jnp.where(half == 1, values, zero)], axis=0
    )


def tile_loop(meta, proj_ref, chunk, tiles, step):
    base = pl.program_id(1) * chunk
    live = jnp.clip(meta[2 * tiles] - base, 0, chunk)

    def group(index, carry):
        for lane in range(UNROLL):
            local = index * UNROLL + lane
            slot = base + local
            segment = meta[slot]
            block = meta[tiles + slot]
            half = jnp.where(local < live, segment % 2, 2)
            points = pl.ds(pl.multiple_of((segment // 2) * PAIR, PAIR), PAIR)
            step(block, points, padded_tile(proj_ref[local], half))
        return carry

    lax.fori_loop(0, (live + UNROLL - 1) // UNROLL, group, 0)


def project_kernel(chunk, tiles, meta, wave_ref, proj_ref, *rest):
    out_ref = rest[-1]
    proj = proj_ref.shape[2]

    @pl.when(pl.program_id(1) == 0)
    def start():
        if len(rest) == 2:
            out_ref[...] = rest[0][...]
        else:
            out_ref[...] = jnp.zeros_like(out_ref)

    def step(block, points, tile):
        lanes = pl.ds(pl.multiple_of(block * proj, proj), proj)
        term = jnp.dot(wave_ref[:, points], tile, preferred_element_type=jnp.float32)
        out_ref[:, lanes] += term

    tile_loop(meta, proj_ref, chunk, tiles, step)


def spread_kernel(chunk, tiles, meta, applied_ref, proj_ref, out_ref, field):
    proj = proj_ref.shape[2]

    @pl.when(pl.program_id(1) == 0)
    def start():
        field[...] = jnp.zeros_like(field)

    def step(block, points, tile):
        lanes = pl.ds(pl.multiple_of(block * proj, proj), proj)
        term = lax.dot_general(
            applied_ref[:, lanes],
            tile,
            (((1,), (1,)), ((), ())),
            preferred_element_type=jnp.float32,
        )
        field[:, points] += term

    tile_loop(meta, proj_ref, chunk, tiles, step)

    @pl.when(pl.program_id(1) == pl.num_programs(1) - 1)
    def finish():
        out_ref[...] = field[...].astype(out_ref.dtype)


def row_block(rows):
    return rows if rows <= 256 else 256


def tile_chunk(tiles):
    for chunk in (96, 64, 48, 32, 16, 8):
        if tiles % chunk == 0:
            return chunk
    return tiles


def chunk_index(chunk, tiles):
    def index(row, step, meta):
        last = (meta[2 * tiles] + chunk - 1) // chunk - 1
        return (jnp.clip(step, 0, jnp.maximum(last, 0)), 0, 0)

    return index


def whole_rows(row, step, meta):
    return (row, 0)


def project(meta, wave, projectors, width, total=None):
    rows, points = wave.shape
    tiles, tile, proj = projectors.shape
    chunk, block = tile_chunk(tiles), row_block(rows)
    in_specs = [
        pl.BlockSpec((block, points), whole_rows),
        pl.BlockSpec((chunk, tile, proj), chunk_index(chunk, tiles)),
    ]
    operands = [meta, wave, projectors]
    if total is not None:
        in_specs.append(pl.BlockSpec((block, width), whole_rows))
        operands.append(total)
    return pl.pallas_call(
        functools.partial(project_kernel, chunk, tiles),
        grid_spec=pltpu.PrefetchScalarGridSpec(
            num_scalar_prefetch=1,
            grid=(rows // block, tiles // chunk),
            in_specs=in_specs,
            out_specs=pl.BlockSpec((block, width), whole_rows),
        ),
        out_shape=jax.ShapeDtypeStruct((rows, width), jnp.float32),
        compiler_params=pltpu.CompilerParams(vmem_limit_bytes=VMEM_LIMIT),
        cost_estimate=pl.CostEstimate(
            flops=2 * rows * tiles * tile * proj,
            bytes_accessed=projectors.size * 2 + wave.size * 2 + rows * width * 4,
            transcendentals=0,
        ),
    )(*operands)


def spread(meta, applied, projectors, points):
    rows, width = applied.shape
    tiles, tile, proj = projectors.shape
    chunk, block = tile_chunk(tiles), row_block(rows)
    return pl.pallas_call(
        functools.partial(spread_kernel, chunk, tiles),
        grid_spec=pltpu.PrefetchScalarGridSpec(
            num_scalar_prefetch=1,
            grid=(rows // block, tiles // chunk),
            in_specs=[
                pl.BlockSpec((block, width), whole_rows),
                pl.BlockSpec((chunk, tile, proj), chunk_index(chunk, tiles)),
            ],
            out_specs=pl.BlockSpec((block, points), whole_rows),
            scratch_shapes=[pltpu.VMEM((block, points), jnp.float32)],
        ),
        out_shape=jax.ShapeDtypeStruct((rows, points), jnp.bfloat16),
        compiler_params=pltpu.CompilerParams(vmem_limit_bytes=VMEM_LIMIT),
        cost_estimate=pl.CostEstimate(
            flops=2 * rows * tiles * tile * proj,
            bytes_accessed=projectors.size * 2 + applied.size * 2 + rows * points * 2,
            transcendentals=0,
        ),
    )(meta, applied, projectors)


def couple_kernel(parts_ref, matrix_ref, out_ref):
    blocks, proj, unused = matrix_ref.shape
    for block in range(blocks):
        lanes = slice(block * proj, (block + 1) * proj)
        total = jnp.sum(parts_ref[:, :, lanes].astype(jnp.float32), axis=0)
        out_ref[:, lanes] = jnp.dot(
            total,
            matrix_ref[block],
            precision=lax.Precision.HIGHEST,
            preferred_element_type=jnp.float32,
        ).astype(out_ref.dtype)


def couple(parts, matrix):
    count, rows, width = parts.shape
    return pl.pallas_call(
        couple_kernel,
        out_shape=jax.ShapeDtypeStruct((rows, width), jnp.bfloat16),
        compiler_params=pltpu.CompilerParams(vmem_limit_bytes=VMEM_LIMIT),
        cost_estimate=pl.CostEstimate(
            flops=12 * rows * width * matrix.shape[1],
            bytes_accessed=parts.size * 2 + matrix.size * 4,
            transcendentals=0,
        ),
    )(parts, matrix)


def coupling_matrix(coupling):
    blocks, atoms, width, unused = coupling.shape
    proj = atoms * width
    wide = jnp.tile(coupling.reshape(blocks, proj, width), (1, 1, atoms))
    same = jnp.arange(proj)[:, None] // width == jnp.arange(proj)[None, :] // width
    return jnp.where(same[None], wide, 0.0)


def body(n_grid, n_copies, wavefunctions, tile_segment, tile_block, tile_count, projectors, coupling):
    half = n_grid // 2
    bands, npts = wavefunctions.shape
    points = npts // n_grid
    tiles = projectors.shape[0]
    width = coupling.shape[0] * projectors.shape[2]
    side = lax.axis_index("grid") // half
    pools = [list(range(half)), list(range(half, n_grid))]
    partners = [(index, (index + half) % n_grid) for index in range(n_grid)]

    meta = jnp.concatenate([tile_segment, tile_block, tile_count])
    other_meta = lax.ppermute(meta, "grid", partners)

    share = tiles // n_copies
    mine = lax.dynamic_slice_in_dim(
        projectors, lax.axis_index(("groups", "band")) * share, share, 0
    )
    arrived = lax.ppermute(mine, "grid", partners)
    other_projectors = lax.all_gather(arrived, ("groups", "band"), axis=0, tiled=True)

    def to_bricks(which):
        part = lax.dynamic_slice_in_dim(wavefunctions, which * half * points, half * points, 1)
        return lax.all_to_all(
            part, "grid", split_axis=1, concat_axis=0, tiled=True, axis_index_groups=pools
        )

    own_wave = to_bricks(side)
    other_wave = to_bricks(1 - side)
    matrix = coupling_matrix(coupling)

    total = project(meta, own_wave, projectors, width)
    total = project(other_meta, other_wave, other_projectors, width, total)

    partial = total.astype(jnp.bfloat16).reshape(half, bands, width)
    parts = lax.all_to_all(
        partial, "grid", split_axis=0, concat_axis=0, tiled=True, axis_index_groups=pools
    )
    applied = lax.all_gather(
        couple(parts, matrix), "grid", axis=0, tiled=True, axis_index_groups=pools
    )

    def to_bands(field):
        return lax.all_to_all(
            field, "grid", split_axis=0, concat_axis=1, tiled=True, axis_index_groups=pools
        )

    other_field = to_bands(spread(other_meta, applied, other_projectors, points))
    own_field = to_bands(spread(meta, applied, projectors, points))
    return jnp.where(
        side == 0,
        jnp.concatenate([own_field, other_field], axis=1),
        jnp.concatenate([other_field, own_field], axis=1),
    )


def solution(mesh):
    in_specs = (
        P(("groups", "grid", "band"), None),
        P("grid"),
        P("grid"),
        P("grid"),
        P("grid", None, None),
        P(),
    )
    out_specs = P(("groups", "grid", "band"), None)
    n_copies = mesh.shape["groups"] * mesh.shape["band"]
    return jax.shard_map(
        functools.partial(body, mesh.shape["grid"], n_copies),
        mesh=mesh,
        in_specs=in_specs,
        out_specs=out_specs,
        check_vma=False,
    )
```

```python
import functools

import jax
import jax.numpy as jnp
from jax import lax
from jax.experimental import pallas as pl
from jax.experimental.pallas import tpu as pltpu
from jax.sharding import PartitionSpec as P

TILE = 64
PAIR = 2 * TILE
UNROLL = 8
VMEM_LIMIT = 56 * 1024 * 1024


def padded_tile(values, half):
    zero = jnp.zeros_like(values)
    return jnp.concatenate(
        [jnp.where(half == 0, values, zero), jnp.where(half == 1, values, zero)], axis=0
    )


def tile_loop(meta, tiles, ref, offset, base, size, step):
    live = jnp.clip(meta[2 * tiles] - base, 0, size)

    def group(index, carry):
        for lane in range(UNROLL):
            local = index * UNROLL + lane
            segment = meta[base + local]
            block = meta[tiles + base + local]
            half = jnp.where(local < live, segment % 2, 2)
            points = pl.ds(pl.multiple_of((segment // 2) * PAIR, PAIR), PAIR)
            step(block, points, padded_tile(ref[offset + local], half))
        return carry

    lax.fori_loop(0, (live + UNROLL - 1) // UNROLL, group, 0)


def all_tiles(meta, tiles, pieces, step):
    if len(pieces) == 1:
        size = pieces[0].shape[0]
        tile_loop(meta, tiles, pieces[0], 0, pl.program_id(1) * size, size, step)
        return
    for number, ref in enumerate(pieces):
        size = ref.shape[0] // 2

        def share(which, carry, number=number, ref=ref, size=size):
            base = meta[2 * tiles + 1 + 2 * number + which]
            tile_loop(meta, tiles, ref, which * size, base, size, step)
            return carry

        lax.fori_loop(0, 2, share, 0)


def project_kernel(tiles, count, last, meta, wave_ref, *rest):
    pieces, rest = rest[:count], rest[count:]
    total = rest[-1]
    out_ref = rest[-2] if last else None
    proj = pieces[0].shape[2]

    @pl.when(pl.program_id(1) == 0)
    def start():
        if len(rest) == (3 if last else 2):
            total[...] = rest[0][...]
        else:
            total[...] = jnp.zeros_like(total)

    def step(block, points, tile):
        lanes = pl.ds(pl.multiple_of(block * proj, proj), proj)
        term = jnp.dot(wave_ref[:, points], tile, preferred_element_type=jnp.float32)
        total[:, lanes] += term

    all_tiles(meta, tiles, pieces, step)
    if last:

        @pl.when(pl.program_id(1) == pl.num_programs(1) - 1)
        def finish():
            out_ref[...] = total[...].astype(out_ref.dtype)


def spread_kernel(tiles, count, meta, applied_ref, *rest):
    pieces, (out_ref, field) = rest[:count], rest[count:]
    proj = pieces[0].shape[2]

    @pl.when(pl.program_id(1) == 0)
    def start():
        field[...] = jnp.zeros_like(field)

    def step(block, points, tile):
        lanes = pl.ds(pl.multiple_of(block * proj, proj), proj)
        term = lax.dot_general(
            applied_ref[:, lanes],
            tile,
            (((1,), (1,)), ((), ())),
            preferred_element_type=jnp.float32,
        )
        field[:, points] += term

    all_tiles(meta, tiles, pieces, step)

    @pl.when(pl.program_id(1) == pl.num_programs(1) - 1)
    def finish():
        out_ref[...] = field[...].astype(out_ref.dtype)


def row_block(rows):
    return rows if rows <= 256 else 256


def tile_chunk(tiles):
    for chunk in (96, 64, 48, 32, 16, 8):
        if tiles % chunk == 0:
            return chunk
    return tiles


def whole_rows(row, step, meta):
    return (row, 0)


def piece_specs(tiles, pieces):
    if len(pieces) > 1:
        return 1, [pl.BlockSpec(piece.shape, lambda row, step, meta: (0, 0, 0)) for piece in pieces]
    chunk = tile_chunk(tiles)

    def index(row, step, meta):
        last = (meta[2 * tiles] + chunk - 1) // chunk - 1
        return (jnp.clip(step, 0, jnp.maximum(last, 0)), 0, 0)

    return tiles // chunk, [pl.BlockSpec((chunk,) + pieces[0].shape[1:], index)]


def cost(rows, pieces, data):
    size = sum(piece.size for piece in pieces)
    return pl.CostEstimate(flops=2 * rows * size, bytes_accessed=2 * size + data, transcendentals=0)


def project(tiles, meta, wave, pieces, width, total=None, last=False):
    rows, points = wave.shape
    block = row_block(rows)
    steps, specs = piece_specs(tiles, pieces)
    in_specs = [pl.BlockSpec((block, points), whole_rows)] + specs
    operands = [meta, wave] + pieces
    if total is not None:
        in_specs.append(pl.BlockSpec((block, width), whole_rows))
        operands.append(total)
    return pl.pallas_call(
        functools.partial(project_kernel, tiles, len(pieces), last),
        grid_spec=pltpu.PrefetchScalarGridSpec(
            num_scalar_prefetch=1,
            grid=(rows // block, steps),
            in_specs=in_specs,
            out_specs=pl.BlockSpec((block, width), whole_rows),
            scratch_shapes=[pltpu.VMEM((block, width), jnp.float32)] if last else [],
        ),
        out_shape=jax.ShapeDtypeStruct((rows, width), jnp.bfloat16 if last else jnp.float32),
        compiler_params=pltpu.CompilerParams(vmem_limit_bytes=VMEM_LIMIT),
        cost_estimate=cost(rows, pieces, wave.size * 2 + rows * width * 4),
    )(*operands)


def spread(tiles, meta, applied, pieces, points):
    rows, width = applied.shape
    block = row_block(rows)
    steps, specs = piece_specs(tiles, pieces)
    return pl.pallas_call(
        functools.partial(spread_kernel, tiles, len(pieces)),
        grid_spec=pltpu.PrefetchScalarGridSpec(
            num_scalar_prefetch=1,
            grid=(rows // block, steps),
            in_specs=[pl.BlockSpec((block, width), whole_rows)] + specs,
            out_specs=pl.BlockSpec((block, points), whole_rows),
            scratch_shapes=[pltpu.VMEM((block, points), jnp.float32)],
        ),
        out_shape=jax.ShapeDtypeStruct((rows, points), jnp.bfloat16),
        compiler_params=pltpu.CompilerParams(vmem_limit_bytes=VMEM_LIMIT),
        cost_estimate=cost(rows, pieces, applied.size * 2 + rows * points * 2),
    )(meta, applied, *pieces)


def two_parts(values):
    high = values.astype(jnp.bfloat16)
    return high, (values - high.astype(jnp.float32)).astype(jnp.bfloat16)


def couple_kernel(parts_ref, high_ref, low_ref, out_ref):
    blocks, proj, unused = high_ref.shape
    for block in range(blocks):
        lanes = slice(block * proj, (block + 1) * proj)
        total = jnp.sum(parts_ref[:, :, lanes].astype(jnp.float32), axis=0)
        high, low = two_parts(total)
        result = jnp.dot(high, high_ref[block], preferred_element_type=jnp.float32)
        result += jnp.dot(high, low_ref[block], preferred_element_type=jnp.float32)
        result += jnp.dot(low, high_ref[block], preferred_element_type=jnp.float32)
        out_ref[:, lanes] = result.astype(out_ref.dtype)


def couple(parts, matrix):
    count, rows, width = parts.shape
    high, low = two_parts(matrix)
    return pl.pallas_call(
        couple_kernel,
        out_shape=jax.ShapeDtypeStruct((rows, width), jnp.bfloat16),
        compiler_params=pltpu.CompilerParams(vmem_limit_bytes=VMEM_LIMIT),
        cost_estimate=pl.CostEstimate(
            flops=6 * rows * width * matrix.shape[1],
            bytes_accessed=parts.size * 2 + matrix.size * 4,
            transcendentals=0,
        ),
    )(parts, high, low)


def coupling_matrix(coupling):
    blocks, atoms, width, unused = coupling.shape
    proj = atoms * width
    wide = jnp.tile(coupling.reshape(blocks, proj, width), (1, 1, atoms))
    same = jnp.arange(proj)[:, None] // width == jnp.arange(proj)[None, :] // width
    return jnp.where(same[None], wide, 0.0)


def body(n_grid, wavefunctions, tile_segment, tile_block, tile_count, projectors, coupling):
    half = n_grid // 2
    bands, npts = wavefunctions.shape
    points = npts // n_grid
    tiles = projectors.shape[0]
    width = coupling.shape[0] * projectors.shape[2]
    side = lax.axis_index("grid") // half
    group, core = lax.axis_index("groups"), lax.axis_index("band")
    pools = [list(range(half)), list(range(half, n_grid))]
    partners = [(index, (index + half) % n_grid) for index in range(n_grid)]
    swap = [(0, 1), (1, 0)]

    meta = jnp.concatenate([tile_segment, tile_block, tile_count])

    def to_bricks(which):
        part = lax.dynamic_slice_in_dim(wavefunctions, which * half * points, half * points, 1)
        return lax.all_to_all(
            part, "grid", split_axis=1, concat_axis=0, tiled=True, axis_index_groups=pools
        )

    own_wave = to_bricks(side)
    other_wave = to_bricks(1 - side)

    pieces, bases = [], []
    start = 0
    for size in (tiles // 2, tiles // 4, tiles // 4):
        share = size // 4
        quarter = 2 * group + core
        mine = lax.dynamic_slice_in_dim(projectors, start + quarter * share, share, 0)
        mine = lax.ppermute(mine, "grid", partners)
        both = jnp.concatenate([mine, lax.ppermute(mine, "groups", swap)])
        pieces += [both, lax.ppermute(both, "band", swap)]
        for other_core in (core, 1 - core):
            for other_group in (group, 1 - group):
                bases.append(start + (2 * other_group + other_core) * share)
        start += size
    other_meta = lax.ppermute(meta, "grid", partners)
    metas = [jnp.concatenate([other_meta, jnp.stack(bases[i : i + 4])]) for i in (0, 4, 8)]
    other_meta = jnp.concatenate([other_meta, jnp.stack(bases)])

    matrix = coupling_matrix(coupling)

    total = project(tiles, meta, own_wave, [projectors], width)
    total = project(tiles, metas[0], other_wave, pieces[0:2], width, total)
    total = project(tiles, metas[1], other_wave, pieces[2:4], width, total)
    partial = project(tiles, metas[2], other_wave, pieces[4:6], width, total, last=True)

    parts = lax.all_to_all(
        partial.reshape(half, bands, width),
        "grid",
        split_axis=0,
        concat_axis=0,
        tiled=True,
        axis_index_groups=pools,
    )
    applied = couple(parts, matrix)
    applied = lax.all_to_all(
        jnp.broadcast_to(applied[None], (half, bands, width)),
        "grid",
        split_axis=0,
        concat_axis=0,
        tiled=True,
        axis_index_groups=pools,
    ).reshape(half * bands, width)

    def to_bands(field):
        return lax.all_to_all(
            field, "grid", split_axis=0, concat_axis=1, tiled=True, axis_index_groups=pools
        )

    other_field = to_bands(spread(tiles, other_meta, applied, pieces, points))
    own_field = to_bands(spread(tiles, meta, applied, [projectors], points))
    return jnp.where(
        side == 0,
        jnp.concatenate([own_field, other_field], axis=1),
        jnp.concatenate([other_field, own_field], axis=1),
    )


def solution(mesh):
    in_specs = (
        P(("groups", "grid", "band"), None),
        P("grid"),
        P("grid"),
        P("grid"),
        P("grid", None, None),
        P(),
    )
    out_specs = P(("groups", "grid", "band"), None)
    return jax.shard_map(
        functools.partial(body, mesh.shape["grid"]),
        mesh=mesh,
        in_specs=in_specs,
        out_specs=out_specs,
        check_vma=False,
    )
```

```python
import functools

import jax
import jax.numpy as jnp
from jax import lax
from jax.experimental import pallas as pl
from jax.experimental.pallas import tpu as pltpu
from jax.sharding import PartitionSpec as P

TILE = 64
PAIR = 2 * TILE
UNROLL = 8
VMEM_LIMIT = 24 * 1024 * 1024


def padded_tile(values, half):
    zero = jnp.zeros_like(values)
    return jnp.concatenate(
        [jnp.where(half == 0, values, zero), jnp.where(half == 1, values, zero)], axis=0
    )


def diagonal(first, second):
    zero = jnp.zeros_like(first)
    return jnp.concatenate(
        [jnp.concatenate([first, zero], axis=1), jnp.concatenate([zero, second], axis=1)], axis=0
    )


def tile_loop(meta, tiles, ref, offset, base, size, step):
    live = jnp.clip(meta[2 * tiles] - base, 0, size)

    def group(index, carry):
        for pair in range(0, UNROLL, 2):
            places = []
            for lane in (pair, pair + 1):
                local = index * UNROLL + lane
                segment = meta[base + local]
                block = meta[tiles + base + local]
                half = jnp.where(local < live, segment % 2, 2)
                points = pl.ds(pl.multiple_of((segment // 2) * PAIR, PAIR), PAIR)
                places.append((block, points, padded_tile(ref[offset + local], half)))
            step(*places)
        return carry

    lax.fori_loop(0, (live + UNROLL - 1) // UNROLL, group, 0)


def all_tiles(meta, tiles, pieces, step):
    if len(pieces) == 1:
        size = pieces[0].shape[0]
        tile_loop(meta, tiles, pieces[0], 0, pl.program_id(0) * size, size, step)
        return
    for number, ref in enumerate(pieces):
        size = ref.shape[0] // 2

        def share(which, carry, number=number, ref=ref, size=size):
            base = meta[2 * tiles + 1 + 2 * number + which]
            tile_loop(meta, tiles, ref, which * size, base, size, step)
            return carry

        lax.fori_loop(0, 2, share, 0)


def project_kernel(tiles, count, last, meta, wave_ref, *rest):
    pieces, rest = rest[:count], rest[count:]
    total = rest[-1]
    out_ref = rest[-2] if last else None
    proj = pieces[0].shape[2]

    @pl.when(pl.program_id(0) == 0)
    def start():
        if len(rest) == (3 if last else 2):
            total[...] = rest[0][...]
        else:
            total[...] = jnp.zeros_like(total)

    def step(first, second):
        waves = jnp.concatenate([wave_ref[:, first[1]], wave_ref[:, second[1]]], axis=1)
        terms = jnp.dot(waves, diagonal(first[2], second[2]), preferred_element_type=jnp.float32)
        for index, place in enumerate((first, second)):
            lanes = pl.ds(pl.multiple_of(place[0] * proj, proj), proj)
            total[:, lanes] += terms[:, index * proj : (index + 1) * proj]

    all_tiles(meta, tiles, pieces, step)
    if last:

        @pl.when(pl.program_id(0) == pl.num_programs(0) - 1)
        def finish():
            out_ref[...] = total[...].astype(out_ref.dtype)


def spread_kernel(tiles, count, meta, applied_ref, *rest):
    pieces, (out_ref, field) = rest[:count], rest[count:]
    proj = pieces[0].shape[2]

    @pl.when(pl.program_id(0) == 0)
    def start():
        field[...] = jnp.zeros_like(field)

    def step(first, second):
        lanes = [pl.ds(pl.multiple_of(place[0] * proj, proj), proj) for place in (first, second)]
        terms = lax.dot_general(
            jnp.concatenate([applied_ref[:, lanes[0]], applied_ref[:, lanes[1]]], axis=1),
            diagonal(first[2], second[2]),
            (((1,), (1,)), ((), ())),
            preferred_element_type=jnp.float32,
        )
        for index, place in enumerate((first, second)):
            field[:, place[1]] += terms[:, index * PAIR : (index + 1) * PAIR]

    all_tiles(meta, tiles, pieces, step)

    @pl.when(pl.program_id(0) == pl.num_programs(0) - 1)
    def finish():
        out_ref[...] = field[...].astype(out_ref.dtype)


def tile_chunk(tiles):
    for chunk in (96, 64, 48, 32, 16, 8):
        if tiles % chunk == 0:
            return chunk
    return tiles


WHOLE = pl.BlockSpec(memory_space=pltpu.VMEM)


def piece_specs(tiles, pieces):
    if len(pieces) > 1:
        return 1, [WHOLE] * len(pieces)
    chunk = tile_chunk(tiles)

    def index(step, meta):
        last = (meta[2 * tiles] + chunk - 1) // chunk - 1
        return (jnp.clip(step, 0, jnp.maximum(last, 0)), 0, 0)

    return tiles // chunk, [pl.BlockSpec((chunk,) + pieces[0].shape[1:], index)]


COST = pl.CostEstimate(flops=1, bytes_accessed=1, transcendentals=0)


def project(tiles, meta, wave, pieces, width, total=None, last=False):
    rows, points = wave.shape
    steps, specs = piece_specs(tiles, pieces)
    in_specs = [WHOLE] + specs
    operands = [meta, wave] + pieces
    if total is not None:
        in_specs.append(WHOLE)
        operands.append(total)
    return pl.pallas_call(
        functools.partial(project_kernel, tiles, len(pieces), last),
        grid_spec=pltpu.PrefetchScalarGridSpec(
            num_scalar_prefetch=1,
            grid=(steps,),
            in_specs=in_specs,
            out_specs=WHOLE,
            scratch_shapes=[pltpu.VMEM((rows, width), jnp.float32)] if last else [],
        ),
        out_shape=jax.ShapeDtypeStruct((rows, width), jnp.bfloat16 if last else jnp.float32),
        compiler_params=pltpu.CompilerParams(vmem_limit_bytes=VMEM_LIMIT),
        cost_estimate=COST,
    )(*operands)


def spread(tiles, meta, applied, pieces, points):
    rows, width = applied.shape
    steps, specs = piece_specs(tiles, pieces)
    return pl.pallas_call(
        functools.partial(spread_kernel, tiles, len(pieces)),
        grid_spec=pltpu.PrefetchScalarGridSpec(
            num_scalar_prefetch=1,
            grid=(steps,),
            in_specs=[WHOLE] + specs,
            out_specs=WHOLE,
            scratch_shapes=[pltpu.VMEM((rows, points), jnp.float32)],
        ),
        out_shape=jax.ShapeDtypeStruct((rows, points), jnp.bfloat16),
        compiler_params=pltpu.CompilerParams(vmem_limit_bytes=VMEM_LIMIT),
        cost_estimate=COST,
    )(meta, applied, *pieces)


def two_parts(values):
    high = values.astype(jnp.bfloat16)
    return high, (values - high.astype(jnp.float32)).astype(jnp.bfloat16)


def couple_kernel(parts_ref, high_ref, low_ref, out_ref):
    blocks, proj, unused = high_ref.shape
    for block in range(blocks):
        lanes = slice(block * proj, (block + 1) * proj)
        total = jnp.sum(parts_ref[:, :, lanes].astype(jnp.float32), axis=0)
        high, low = two_parts(total)
        result = jnp.dot(high, high_ref[block], preferred_element_type=jnp.float32)
        result += jnp.dot(high, low_ref[block], preferred_element_type=jnp.float32)
        result += jnp.dot(low, high_ref[block], preferred_element_type=jnp.float32)
        out_ref[:, lanes] = result.astype(out_ref.dtype)


def couple(parts, matrix):
    count, rows, width = parts.shape
    high, low = two_parts(matrix)
    return pl.pallas_call(
        couple_kernel,
        in_specs=[WHOLE] * 3,
        out_specs=WHOLE,
        out_shape=jax.ShapeDtypeStruct((rows, width), jnp.bfloat16),
        compiler_params=pltpu.CompilerParams(vmem_limit_bytes=VMEM_LIMIT),
        cost_estimate=COST,
    )(parts, high, low)


def coupling_matrix(coupling):
    blocks, atoms, width, unused = coupling.shape
    proj = atoms * width
    wide = jnp.tile(coupling.reshape(blocks, proj, width), (1, 1, atoms))
    same = jnp.arange(proj)[:, None] // width == jnp.arange(proj)[None, :] // width
    return jnp.where(same[None], wide, 0.0)


def body(n_grid, wavefunctions, tile_segment, tile_block, tile_count, projectors, coupling):
    half = n_grid // 2
    bands, npts = wavefunctions.shape
    points = npts // n_grid
    tiles = projectors.shape[0]
    width = coupling.shape[0] * projectors.shape[2]
    side = lax.axis_index("grid") // half
    group, core = lax.axis_index("groups"), lax.axis_index("band")
    pools = [list(range(half)), list(range(half, n_grid))]
    partners = [(index, (index + half) % n_grid) for index in range(n_grid)]
    swap = [(0, 1), (1, 0)]

    meta = jnp.concatenate([tile_segment, tile_block, tile_count])

    def to_bricks(which):
        part = lax.dynamic_slice_in_dim(wavefunctions, which * half * points, half * points, 1)
        return lax.all_to_all(
            part, "grid", split_axis=1, concat_axis=0, tiled=True, axis_index_groups=pools
        )

    own_wave = to_bricks(side)
    other_wave = to_bricks(1 - side)

    total = project(tiles, meta, own_wave, [projectors], width)

    pieces, bases = [], []
    start = 0
    for size in (tiles // 2, tiles // 4, tiles // 4):
        share = size // 4
        quarter = 2 * group + core
        mine = lax.dynamic_slice_in_dim(projectors, start + quarter * share, share, 0)
        mine = lax.ppermute(mine, "grid", partners)
        if start == 0:
            mine, total = lax.optimization_barrier((mine, total))
        both = jnp.concatenate([mine, lax.ppermute(mine, "groups", swap)])
        pieces += [both, lax.ppermute(both, "band", swap)]
        for other_core in (core, 1 - core):
            for other_group in (group, 1 - group):
                bases.append(start + (2 * other_group + other_core) * share)
        start += size
    other_meta = lax.ppermute(meta, "grid", partners)
    metas = [jnp.concatenate([other_meta, jnp.stack(bases[i : i + 4])]) for i in (0, 4, 8)]
    other_meta = jnp.concatenate([other_meta, jnp.stack(bases)])

    matrix = coupling_matrix(coupling)

    total = project(tiles, metas[0], other_wave, pieces[0:2], width, total)
    total = project(tiles, metas[1], other_wave, pieces[2:4], width, total)
    partial = project(tiles, metas[2], other_wave, pieces[4:6], width, total, last=True)

    parts = lax.all_to_all(
        partial.reshape(half, bands, width),
        "grid",
        split_axis=0,
        concat_axis=0,
        tiled=True,
        axis_index_groups=pools,
    )
    applied = couple(parts, matrix)
    applied = lax.all_to_all(
        jnp.broadcast_to(applied[None], (half, bands, width)),
        "grid",
        split_axis=0,
        concat_axis=0,
        tiled=True,
        axis_index_groups=pools,
    ).reshape(half * bands, width)

    def to_bands(field):
        return lax.all_to_all(
            field, "grid", split_axis=0, concat_axis=1, tiled=True, axis_index_groups=pools
        )

    other_field = to_bands(spread(tiles, other_meta, applied, pieces, points))
    own_field = to_bands(spread(tiles, meta, applied, [projectors], points))
    return jnp.where(
        side == 0,
        jnp.concatenate([own_field, other_field], axis=1),
        jnp.concatenate([other_field, own_field], axis=1),
    )


def solution(mesh):
    in_specs = (
        P(("groups", "grid", "band"), None),
        P("grid"),
        P("grid"),
        P("grid"),
        P("grid", None, None),
        P(),
    )
    out_specs = P(("groups", "grid", "band"), None)
    return jax.shard_map(
        functools.partial(body, mesh.shape["grid"]),
        mesh=mesh,
        in_specs=in_specs,
        out_specs=out_specs,
        check_vma=False,
    )
```

```python
import functools

import jax
import jax.numpy as jnp
from jax import lax
from jax.experimental import pallas as pl
from jax.experimental.pallas import tpu as pltpu
from jax.sharding import PartitionSpec as P

TILE = 64
PAIR = 2 * TILE
UNROLL = 8
VMEM_LIMIT = 24 * 1024 * 1024


def padded_tile(values, half):
    zero = jnp.zeros_like(values)
    return jnp.concatenate(
        [jnp.where(half == 0, values, zero), jnp.where(half == 1, values, zero)], axis=0
    )


def diagonal(first, second):
    zero = jnp.zeros_like(first)
    return jnp.concatenate(
        [jnp.concatenate([first, zero], axis=1), jnp.concatenate([zero, second], axis=1)], axis=0
    )


def tile_loop(meta, tiles, ref, offset, base, size, step):
    live = jnp.clip(meta[2 * tiles] - base, 0, size)

    def group(index, carry):
        for pair in range(0, UNROLL, 2):
            places = []
            for lane in (pair, pair + 1):
                local = index * UNROLL + lane
                segment = meta[base + local]
                block = meta[tiles + base + local]
                half = jnp.where(local < live, segment % 2, 2)
                points = pl.ds(pl.multiple_of((segment // 2) * PAIR, PAIR), PAIR)
                places.append((block, points, padded_tile(ref[offset + local], half)))
            step(*places)
        return carry

    lax.fori_loop(0, (live + UNROLL - 1) // UNROLL, group, 0)


def all_tiles(meta, tiles, pieces, step):
    if len(pieces) == 1:
        size = pieces[0].shape[0]
        tile_loop(meta, tiles, pieces[0], 0, pl.program_id(0) * size, size, step)
        return
    for number, ref in enumerate(pieces):
        size = ref.shape[0] // 2

        def share(which, carry, number=number, ref=ref, size=size):
            base = meta[2 * tiles + 1 + 2 * number + which]
            tile_loop(meta, tiles, ref, which * size, base, size, step)
            return carry

        lax.fori_loop(0, 2, share, 0)


def project_kernel(tiles, count, last, meta, wave_ref, *rest):
    pieces, rest = rest[:count], rest[count:]
    total = rest[-1]
    out_ref = rest[-2] if last else None
    proj = pieces[0].shape[2]

    @pl.when(pl.program_id(0) == 0)
    def start():
        if len(rest) == (3 if last else 2):
            total[...] = rest[0][...]
        else:
            total[...] = jnp.zeros_like(total)

    def step(first, second):
        waves = jnp.concatenate([wave_ref[:, first[1]], wave_ref[:, second[1]]], axis=1)
        terms = jnp.dot(waves, diagonal(first[2], second[2]), preferred_element_type=jnp.float32)
        for index, place in enumerate((first, second)):
            lanes = pl.ds(pl.multiple_of(place[0] * proj, proj), proj)
            total[:, lanes] += terms[:, index * proj : (index + 1) * proj]

    all_tiles(meta, tiles, pieces, step)
    if last:

        @pl.when(pl.program_id(0) == pl.num_programs(0) - 1)
        def finish():
            out_ref[...] = total[...].astype(out_ref.dtype)


def spread_kernel(tiles, count, meta, applied_ref, *rest):
    pieces, (out_ref, field) = rest[:count], rest[count:]
    proj = pieces[0].shape[2]

    @pl.when(pl.program_id(0) == 0)
    def start():
        field[...] = jnp.zeros_like(field)

    def step(first, second):
        lanes = [pl.ds(pl.multiple_of(place[0] * proj, proj), proj) for place in (first, second)]
        terms = lax.dot_general(
            jnp.concatenate([applied_ref[:, lanes[0]], applied_ref[:, lanes[1]]], axis=1),
            diagonal(first[2], second[2]),
            (((1,), (1,)), ((), ())),
            preferred_element_type=jnp.float32,
        )
        for index, place in enumerate((first, second)):
            field[:, place[1]] += terms[:, index * PAIR : (index + 1) * PAIR]

    all_tiles(meta, tiles, pieces, step)

    @pl.when(pl.program_id(0) == pl.num_programs(0) - 1)
    def finish():
        out_ref[...] = field[...].astype(out_ref.dtype)


def tile_chunk(tiles):
    for chunk in (96, 64, 48, 32, 16, 8):
        if tiles % chunk == 0:
            return chunk
    return tiles


WHOLE = pl.BlockSpec(memory_space=pltpu.VMEM)


def piece_specs(tiles, pieces):
    if len(pieces) > 1:
        return 1, [WHOLE] * len(pieces)
    chunk = tile_chunk(tiles)

    def index(step, meta):
        last = (meta[2 * tiles] + chunk - 1) // chunk - 1
        return (jnp.clip(step, 0, jnp.maximum(last, 0)), 0, 0)

    return tiles // chunk, [pl.BlockSpec((chunk,) + pieces[0].shape[1:], index)]


COST = pl.CostEstimate(flops=1, bytes_accessed=1, transcendentals=0)


def project(tiles, meta, wave, pieces, width, total=None, last=False):
    rows, points = wave.shape
    steps, specs = piece_specs(tiles, pieces)
    in_specs = [WHOLE] + specs
    operands = [meta, wave] + pieces
    if total is not None:
        in_specs.append(WHOLE)
        operands.append(total)
    return pl.pallas_call(
        functools.partial(project_kernel, tiles, len(pieces), last),
        grid_spec=pltpu.PrefetchScalarGridSpec(
            num_scalar_prefetch=1,
            grid=(steps,),
            in_specs=in_specs,
            out_specs=WHOLE,
            scratch_shapes=[pltpu.VMEM((rows, width), jnp.float32)] if last else [],
        ),
        out_shape=jax.ShapeDtypeStruct((rows, width), jnp.bfloat16 if last else jnp.float32),
        compiler_params=pltpu.CompilerParams(vmem_limit_bytes=VMEM_LIMIT),
        cost_estimate=COST,
    )(*operands)


def spread(tiles, meta, applied, pieces, points):
    rows, width = applied.shape
    steps, specs = piece_specs(tiles, pieces)
    return pl.pallas_call(
        functools.partial(spread_kernel, tiles, len(pieces)),
        grid_spec=pltpu.PrefetchScalarGridSpec(
            num_scalar_prefetch=1,
            grid=(steps,),
            in_specs=[WHOLE] + specs,
            out_specs=WHOLE,
            scratch_shapes=[pltpu.VMEM((rows, points), jnp.float32)],
        ),
        out_shape=jax.ShapeDtypeStruct((rows, points), jnp.bfloat16),
        compiler_params=pltpu.CompilerParams(vmem_limit_bytes=VMEM_LIMIT),
        cost_estimate=COST,
    )(meta, applied, *pieces)


def two_parts(values):
    high = values.astype(jnp.bfloat16)
    return high, (values - high.astype(jnp.float32)).astype(jnp.bfloat16)


def couple_kernel(parts_ref, high_ref, low_ref, out_ref):
    blocks, proj, unused = high_ref.shape
    for block in range(blocks):
        lanes = slice(block * proj, (block + 1) * proj)
        total = jnp.sum(parts_ref[:, :, lanes].astype(jnp.float32), axis=0)
        high, low = two_parts(total)
        result = jnp.dot(high, high_ref[block], preferred_element_type=jnp.float32)
        result += jnp.dot(high, low_ref[block], preferred_element_type=jnp.float32)
        result += jnp.dot(low, high_ref[block], preferred_element_type=jnp.float32)
        out_ref[:, lanes] = result.astype(out_ref.dtype)


def couple(parts, matrix):
    count, rows, width = parts.shape
    high, low = two_parts(matrix)
    return pl.pallas_call(
        couple_kernel,
        in_specs=[WHOLE] * 3,
        out_specs=WHOLE,
        out_shape=jax.ShapeDtypeStruct((rows, width), jnp.bfloat16),
        compiler_params=pltpu.CompilerParams(vmem_limit_bytes=VMEM_LIMIT),
        cost_estimate=COST,
    )(parts, high, low)


def coupling_matrix(coupling):
    blocks, atoms, width, unused = coupling.shape
    proj = atoms * width
    wide = jnp.tile(coupling.reshape(blocks, proj, width), (1, 1, atoms))
    same = jnp.arange(proj)[:, None] // width == jnp.arange(proj)[None, :] // width
    return jnp.where(same[None], wide, 0.0)


def body(n_grid, wavefunctions, tile_segment, tile_block, tile_count, projectors, coupling):
    half = n_grid // 2
    bands, npts = wavefunctions.shape
    points = npts // n_grid
    tiles = projectors.shape[0]
    width = coupling.shape[0] * projectors.shape[2]
    side = lax.axis_index("grid") // half
    group, core = lax.axis_index("groups"), lax.axis_index("band")
    pools = [list(range(half)), list(range(half, n_grid))]
    partners = [(index, (index + half) % n_grid) for index in range(n_grid)]
    swap = [(0, 1), (1, 0)]

    meta = jnp.concatenate([tile_segment, tile_block, tile_count])

    def to_bricks(which):
        part = lax.dynamic_slice_in_dim(wavefunctions, which * half * points, half * points, 1)
        return lax.all_to_all(
            part, "grid", split_axis=1, concat_axis=0, tiled=True, axis_index_groups=pools
        )

    own_wave = to_bricks(side)
    other_wave = to_bricks(1 - side)

    total = project(tiles, meta, own_wave, [projectors], width)

    other_meta = lax.ppermute(meta, "grid", partners)

    pieces, bases = [], []
    start = 0
    for size in [tiles // 4] * 4:
        share = size // 4
        quarter = 2 * group + core
        mine = lax.dynamic_slice_in_dim(projectors, start + quarter * share, share, 0)
        mine = lax.ppermute(mine, "grid", partners)
        if start == 0:
            mine, total, other_meta = lax.optimization_barrier((mine, total, other_meta))
        both = jnp.concatenate([mine, lax.ppermute(mine, "groups", swap)])
        pieces += [both, lax.ppermute(both, "band", swap)]
        for other_core in (core, 1 - core):
            for other_group in (group, 1 - group):
                bases.append(start + (2 * other_group + other_core) * share)
        start += size
    ranges = ((0, 2), (2, 3), (3, 4))
    metas = [
        jnp.concatenate([other_meta, jnp.stack(bases[4 * first : 4 * end])])
        for first, end in ranges
    ]
    other_meta = jnp.concatenate([other_meta, jnp.stack(bases)])

    matrix = coupling_matrix(coupling)

    for (first, end), piece_meta in zip(ranges, metas):
        total = project(
            tiles, piece_meta, other_wave, pieces[2 * first : 2 * end], width, total, last=end == 4
        )
    partial = total

    parts = lax.all_to_all(
        partial.reshape(half, bands, width),
        "grid",
        split_axis=0,
        concat_axis=0,
        tiled=True,
        axis_index_groups=pools,
    )
    applied = couple(parts, matrix)
    applied = lax.all_to_all(
        jnp.broadcast_to(applied[None], (half, bands, width)),
        "grid",
        split_axis=0,
        concat_axis=0,
        tiled=True,
        axis_index_groups=pools,
    ).reshape(half * bands, width)

    def to_bands(field):
        return lax.all_to_all(
            field, "grid", split_axis=0, concat_axis=1, tiled=True, axis_index_groups=pools
        )

    other_field = to_bands(spread(tiles, other_meta, applied, pieces, points))
    own_field = to_bands(spread(tiles, meta, applied, [projectors], points))
    return jnp.where(
        side == 0,
        jnp.concatenate([own_field, other_field], axis=1),
        jnp.concatenate([other_field, own_field], axis=1),
    )


def solution(mesh):
    in_specs = (
        P(("groups", "grid", "band"), None),
        P("grid"),
        P("grid"),
        P("grid"),
        P("grid", None, None),
        P(),
    )
    out_specs = P(("groups", "grid", "band"), None)
    return jax.shard_map(
        functools.partial(body, mesh.shape["grid"]),
        mesh=mesh,
        in_specs=in_specs,
        out_specs=out_specs,
        check_vma=False,
    )
```

```python
import functools

import jax
import jax.numpy as jnp
from jax import lax
from jax.experimental import pallas as pl
from jax.experimental.pallas import tpu as pltpu
from jax.sharding import PartitionSpec as P

TILE = 64
PAIR = 2 * TILE
UNROLL = 8
HEAD = 3
VMEM_LIMIT = 24 * 1024 * 1024


def padded_tile(values, half):
    zero = jnp.zeros_like(values)
    return jnp.concatenate(
        [jnp.where(half == 0, values, zero), jnp.where(half == 1, values, zero)], axis=0
    )


def diagonal(first, second):
    zero = jnp.zeros_like(first)
    return jnp.concatenate(
        [jnp.concatenate([first, zero], axis=1), jnp.concatenate([zero, second], axis=1)], axis=0
    )


def tile_loop(meta, tiles, ref, base, size, step):
    live = jnp.clip(meta[2 * tiles] - base, 0, size)

    def group(index, carry):
        for pair in range(0, UNROLL, 2):
            places = []
            for lane in (pair, pair + 1):
                local = index * UNROLL + lane
                segment = meta[base + local]
                block = meta[tiles + base + local]
                half = jnp.where(local < live, segment % 2, 2)
                places.append((block, segment // 2, padded_tile(ref[local], half)))
            step(*places)
        return carry

    lax.fori_loop(0, (live + UNROLL - 1) // UNROLL, group, 0)


def tile_points(place, column):
    return pl.ds(pl.multiple_of(column + place[1] * PAIR, PAIR), PAIR)


def all_tiles(meta, tiles, pieces, step):
    if len(pieces) == 1:
        size = pieces[0].shape[0]
        tile_loop(meta, tiles, pieces[0], pl.program_id(0) * size, size, step)
        return
    for number, ref in enumerate(pieces):
        tile_loop(meta, tiles, ref, meta[2 * tiles + HEAD + number], ref.shape[0], step)


def rows_of(refs, lanes):
    return jnp.concatenate([ref[:, lanes] for ref in refs], axis=0)


def store_rows(refs, values):
    start = 0
    for ref in refs:
        rows = ref.shape[0]
        ref[...] = values[start : start + rows].astype(ref.dtype)
        start += rows


def project_kernel(tiles, n_pieces, first, last, meta, wave, *refs):
    pieces, refs = refs[:n_pieces], refs[n_pieces:]
    total = refs[-1]
    proj = pieces[0].shape[2]
    side, place = meta[2 * tiles + 1], meta[2 * tiles + 2]
    column = side * (wave.shape[1] // 2)

    @pl.when(pl.program_id(0) == 0)
    def start():
        total[...] = jnp.zeros_like(total) if first else refs[0][...]

    def step(first, second):
        values = jnp.concatenate([wave[:, tile_points(place, column)] for place in (first, second)], axis=1)
        terms = jnp.dot(values, diagonal(first[2], second[2]), preferred_element_type=jnp.float32)
        for index, place in enumerate((first, second)):
            lanes = pl.ds(pl.multiple_of(place[0] * proj, proj), proj)
            total[:, lanes] += terms[:, index * proj : (index + 1) * proj]

    all_tiles(meta, tiles, pieces, step)
    if last:
        outs = refs[1:-1]
        rows = outs[0].shape[0]
        for d, out in enumerate(outs):
            start = 0 if len(outs) == 1 else pl.multiple_of((place ^ d) * rows, rows)
            out[...] = total[pl.ds(start, rows), :].astype(out.dtype)


def spread_kernel(tiles, n_rows, n_pieces, meta, *refs):
    applied, refs = refs[:n_rows], refs[n_rows:]
    pieces, refs = refs[:n_pieces], refs[n_pieces:]
    outs, field = refs[:-1], refs[-1]
    proj = pieces[0].shape[2]

    @pl.when(pl.program_id(0) == 0)
    def start():
        field[...] = jnp.zeros_like(field)

    def step(first, second):
        lanes = [pl.ds(pl.multiple_of(place[0] * proj, proj), proj) for place in (first, second)]
        terms = lax.dot_general(
            jnp.concatenate([rows_of(applied, lanes[0]), rows_of(applied, lanes[1])], axis=1),
            diagonal(first[2], second[2]),
            (((1,), (1,)), ((), ())),
            preferred_element_type=jnp.float32,
        )
        for index, place in enumerate((first, second)):
            field[:, tile_points(place, 0)] += terms[:, index * PAIR : (index + 1) * PAIR]

    all_tiles(meta, tiles, pieces, step)

    @pl.when(pl.program_id(0) == pl.num_programs(0) - 1)
    def finish():
        store_rows(outs, field)


def tile_chunk(tiles):
    for chunk in (96, 64, 48, 32, 16, 8):
        if tiles % chunk == 0:
            return chunk
    return tiles


WHOLE = pl.BlockSpec(memory_space=pltpu.VMEM)


def piece_specs(tiles, pieces):
    if len(pieces) > 1:
        return 1, [WHOLE] * len(pieces)
    chunk = tile_chunk(tiles)

    def index(step, meta):
        last = (meta[2 * tiles] + chunk - 1) // chunk - 1
        return (jnp.clip(step, 0, jnp.maximum(last, 0)), 0, 0)

    return tiles // chunk, [pl.BlockSpec((chunk,) + pieces[0].shape[1:], index)]


COST = pl.CostEstimate(flops=1, bytes_accessed=1, transcendentals=0)


def join_small(blocks):
    return blocks if blocks[0].shape[0] % 16 == 0 else [jnp.concatenate(blocks)]


def split_small(blocks, count):
    return blocks if len(blocks) == count else jnp.split(blocks[0], count)


def project(tiles, meta, wave, pieces, count, width, total=None, last=False):
    rows = wave.shape[0]
    bands = rows // count
    split = bands % 16 == 0
    steps, specs = piece_specs(tiles, pieces)
    operands = [wave, *pieces] + ([] if total is None else [total])
    in_specs = [WHOLE] + specs + [WHOLE] * (total is not None)
    outs = count if split else 1
    out_shape = [jax.ShapeDtypeStruct((rows // outs, width), jnp.bfloat16)] * outs
    return pl.pallas_call(
        functools.partial(project_kernel, tiles, len(pieces), total is None, last),
        grid_spec=pltpu.PrefetchScalarGridSpec(
            num_scalar_prefetch=1,
            grid=(steps,),
            in_specs=in_specs,
            out_specs=[WHOLE] * outs if last else WHOLE,
            scratch_shapes=[pltpu.VMEM((rows, width), jnp.float32)] if last else [],
        ),
        out_shape=out_shape if last else jax.ShapeDtypeStruct((rows, width), jnp.float32),
        compiler_params=pltpu.CompilerParams(vmem_limit_bytes=VMEM_LIMIT),
        cost_estimate=COST,
    )(meta, *operands)


def spread(tiles, meta, applied, pieces, points):
    count = len(applied)
    applied = join_small(applied)
    rows = sum(block.shape[0] for block in applied)
    steps, specs = piece_specs(tiles, pieces)
    result = pl.pallas_call(
        functools.partial(spread_kernel, tiles, len(applied), len(pieces)),
        grid_spec=pltpu.PrefetchScalarGridSpec(
            num_scalar_prefetch=1,
            grid=(steps,),
            in_specs=[WHOLE] * len(applied) + specs,
            out_specs=[WHOLE] * len(applied),
            scratch_shapes=[pltpu.VMEM((rows, points), jnp.float32)],
        ),
        out_shape=[
            jax.ShapeDtypeStruct((block.shape[0], points), jnp.bfloat16) for block in applied
        ],
        compiler_params=pltpu.CompilerParams(vmem_limit_bytes=VMEM_LIMIT),
        cost_estimate=COST,
    )(meta, *applied, *pieces)
    return split_small(result, count)


def two_parts(values):
    high = values.astype(jnp.bfloat16)
    return high, (values - high.astype(jnp.float32)).astype(jnp.bfloat16)


def couple_kernel(high_ref, low_ref, *refs):
    parts, out_ref = refs[:-1], refs[-1]
    blocks, proj, unused = high_ref.shape
    for block in range(blocks):
        lanes = slice(block * proj, (block + 1) * proj)
        total = parts[0][:, lanes].astype(jnp.float32)
        for part in parts[1:]:
            total += part[:, lanes].astype(jnp.float32)
        high, low = two_parts(total)
        result = jnp.dot(high, high_ref[block], preferred_element_type=jnp.float32)
        result += jnp.dot(high, low_ref[block], preferred_element_type=jnp.float32)
        result += jnp.dot(low, high_ref[block], preferred_element_type=jnp.float32)
        out_ref[:, lanes] = result.astype(out_ref.dtype)


def couple(parts, high, low):
    return pl.pallas_call(
        couple_kernel,
        in_specs=[WHOLE] * (2 + len(parts)),
        out_specs=WHOLE,
        out_shape=jax.ShapeDtypeStruct(parts[0].shape, jnp.bfloat16),
        compiler_params=pltpu.CompilerParams(vmem_limit_bytes=VMEM_LIMIT),
        cost_estimate=COST,
    )(high, low, *parts)


def coupling_matrix(coupling):
    blocks, atoms, width, unused = coupling.shape
    proj = atoms * width
    wide = jnp.tile(coupling.reshape(blocks, proj, width), (1, 1, atoms))
    same = jnp.arange(proj)[:, None] // width == jnp.arange(proj)[None, :] // width
    return jnp.where(same[None], wide, 0.0)


def body(n_grid, wavefunctions, tile_segment, tile_block, tile_count, projectors, coupling):
    half = n_grid // 2
    bands, npts = wavefunctions.shape
    points = npts // n_grid
    tiles = projectors.shape[0]
    width = coupling.shape[0] * projectors.shape[2]
    index = lax.axis_index("grid")
    side, place = index // half, index % half
    group, core = lax.axis_index("groups"), lax.axis_index("band")
    partners = [(i, (i + half) % n_grid) for i in range(n_grid)]
    swap = [(0, 1), (1, 0)]

    def exchange(blocks):
        return [blocks[0]] + [
            lax.ppermute(
                blocks[d], "grid", [(i, i // half * half + (i % half ^ d)) for i in range(n_grid)]
            )
            for d in range(1, half)
        ]

    waves = wavefunctions.reshape(bands, 2, half, points).transpose(2, 0, 1, 3)
    waves = lax.all_to_all(
        waves.reshape(half, bands, 2 * points),
        "grid",
        split_axis=0,
        concat_axis=0,
        tiled=True,
        axis_index_groups=[list(range(half)), list(range(half, n_grid))],
    ).reshape(half * bands, 2 * points)

    lists = jnp.concatenate([tile_segment, tile_block, tile_count])
    other_lists = lax.ppermute(lists, "grid", partners)
    meta = jnp.concatenate([lists, jnp.stack([side, place])])
    total = project(tiles, meta, waves, [projectors], half, width)

    pieces, bases = [], []
    parts = 4
    size = tiles // parts
    share = size // 4
    for part in range(parts):
        mine = lax.dynamic_slice_in_dim(
            projectors, part * size + (2 * group + core) * share, share, 0
        )
        mine = lax.ppermute(mine, "grid", partners)
        if part > 0:
            mine, total, other_lists = lax.optimization_barrier((mine, total, other_lists))
        across = lax.ppermute(mine, "groups", swap)
        pieces += [mine, across, lax.ppermute(mine, "band", swap), lax.ppermute(across, "band", swap)]
        for other_core in (core, 1 - core):
            for other_group in (group, 1 - group):
                bases.append(part * size + (2 * other_group + other_core) * share)

    matrix = two_parts(coupling_matrix(coupling))
    other_meta = jnp.concatenate([other_lists, jnp.stack([1 - side, place] + bases)])
    for first, end in ((0, 2), (2, 3), (3, 4)):
        skip = 2 * tiles + HEAD
        piece_meta = jnp.concatenate(
            [other_meta[:skip], other_meta[skip + 4 * first : skip + 4 * end]]
        )
        total = project(
            tiles,
            piece_meta,
            waves,
            pieces[4 * first : 4 * end],
            half,
            width,
            total,
            last=end == parts,
        )
    if len(total) < half:
        total = [lax.dynamic_slice_in_dim(total[0], (place ^ d) * bands, bands, 0) for d in range(half)]

    applied = couple(exchange(total), *matrix)
    applied = exchange([applied] * half)

    result = jnp.zeros((bands, npts), jnp.bfloat16)
    for which, field in (
        (1 - side, spread(tiles, other_meta, applied, pieces, points)),
        (side, spread(tiles, meta, applied, [projectors], points)),
    ):
        for d, block in enumerate(exchange(field)):
            start = (which * half + (place ^ d)) * points
            result = lax.dynamic_update_slice_in_dim(result, block, start, 1)
    return result


def solution(mesh):
    in_specs = (
        P(("groups", "grid", "band"), None),
        P("grid"),
        P("grid"),
        P("grid"),
        P("grid", None, None),
        P(),
    )
    out_specs = P(("groups", "grid", "band"), None)
    return jax.shard_map(
        functools.partial(body, mesh.shape["grid"]),
        mesh=mesh,
        in_specs=in_specs,
        out_specs=out_specs,
        check_vma=False,
    )
```

```python
import functools

import jax
import jax.numpy as jnp
from jax import lax
from jax.experimental import pallas as pl
from jax.experimental.pallas import tpu as pltpu
from jax.sharding import PartitionSpec as P

TILE = 64
PAIR = 2 * TILE
UNROLL = 8
HEAD = 2
VMEM_LIMIT = 12 * 1024 * 1024


def padded_tile(values, half):
    zero = jnp.zeros_like(values)
    return jnp.concatenate(
        [jnp.where(half == 0, values, zero), jnp.where(half == 1, values, zero)], axis=0
    )


def diagonal(first, second):
    zero = jnp.zeros_like(first)
    return jnp.concatenate(
        [jnp.concatenate([first, zero], axis=1), jnp.concatenate([zero, second], axis=1)], axis=0
    )


def tile_loop(meta, tiles, ref, base, size, step):
    live = jnp.clip(meta[2 * tiles] - base, 0, size)

    def group(index, carry):
        for pair in range(0, UNROLL, 2):
            places = []
            for lane in (pair, pair + 1):
                local = index * UNROLL + lane
                segment = meta[base + local]
                block = meta[tiles + base + local]
                half = jnp.where(local < live, segment % 2, 2)
                places.append((block, segment // 2, padded_tile(ref[local], half)))
            step(*places)
        return carry

    lax.fori_loop(0, (live + UNROLL - 1) // UNROLL, group, 0)


def tile_points(place):
    return pl.ds(pl.multiple_of(place[1] * PAIR, PAIR), PAIR)


def all_tiles(meta, tiles, pieces, step):
    if len(pieces) == 1:
        tile_loop(meta, tiles, pieces[0], 0, tiles, step)
        return
    for number, ref in enumerate(pieces):
        size = ref.shape[0] // 2

        def share(which, carry, number=number, ref=ref, size=size):
            base = meta[2 * tiles + HEAD + 2 * number + which]
            tile_loop(meta, tiles, ref.at[pl.ds(which * size, size)], base, size, step)
            return carry

        lax.fori_loop(0, 2, share, 0)


def rows_of(refs, lanes):
    return jnp.concatenate([ref[:, lanes] for ref in refs], axis=0)


def store_rows(refs, values):
    start = 0
    for ref in refs:
        rows = ref.shape[0]
        ref[...] = values[start : start + rows].astype(ref.dtype)
        start += rows


def project_kernel(tiles, n_pieces, first, last, meta, wave, *refs):
    pieces, refs = refs[:n_pieces], refs[n_pieces:]
    total = refs[-1]
    proj = pieces[0].shape[2]
    place = meta[2 * tiles + 1]

    total[...] = jnp.zeros_like(total) if first else refs[0][...]

    def step(first, second):
        values = jnp.concatenate([wave[:, tile_points(at)] for at in (first, second)], axis=1)
        terms = jnp.dot(values, diagonal(first[2], second[2]), preferred_element_type=jnp.float32)
        for index, place in enumerate((first, second)):
            lanes = pl.ds(pl.multiple_of(place[0] * proj, proj), proj)
            total[:, lanes] += terms[:, index * proj : (index + 1) * proj]

    all_tiles(meta, tiles, pieces, step)
    if last:
        outs = refs[1:-1]
        rows = outs[0].shape[0]
        for d, out in enumerate(outs):
            start = 0 if len(outs) == 1 else pl.multiple_of((place ^ d) * rows, rows)
            out[...] = total[pl.ds(start, rows), :].astype(out.dtype)


def spread_kernel(tiles, n_rows, n_pieces, meta, *refs):
    applied, refs = refs[:n_rows], refs[n_rows:]
    pieces, refs = refs[:n_pieces], refs[n_pieces:]
    outs, field = refs[:-1], refs[-1]
    proj = pieces[0].shape[2]

    field[...] = jnp.zeros_like(field)

    def step(first, second):
        lanes = [pl.ds(pl.multiple_of(place[0] * proj, proj), proj) for place in (first, second)]
        terms = lax.dot_general(
            jnp.concatenate([rows_of(applied, lanes[0]), rows_of(applied, lanes[1])], axis=1),
            diagonal(first[2], second[2]),
            (((1,), (1,)), ((), ())),
            preferred_element_type=jnp.float32,
        )
        for index, place in enumerate((first, second)):
            field[:, tile_points(place)] += terms[:, index * PAIR : (index + 1) * PAIR]

    all_tiles(meta, tiles, pieces, step)

    store_rows(outs, field)


WHOLE = pl.BlockSpec(memory_space=pltpu.VMEM)


COST = pl.CostEstimate(flops=1, bytes_accessed=1, transcendentals=0)


def join_small(blocks):
    return blocks if blocks[0].shape[0] % 16 == 0 else [jnp.concatenate(blocks)]


def split_small(blocks, count):
    return blocks if len(blocks) == count else jnp.split(blocks[0], count)


def project(tiles, meta, wave, pieces, count, width, total=None, last=False):
    rows = wave.shape[0]
    bands = rows // count
    split = bands % 16 == 0
    operands = [wave, *pieces] + ([] if total is None else [total])
    outs = count if split else 1
    out_shape = [jax.ShapeDtypeStruct((rows // outs, width), jnp.bfloat16)] * outs
    return pl.pallas_call(
        functools.partial(project_kernel, tiles, len(pieces), total is None, last),
        grid_spec=pltpu.PrefetchScalarGridSpec(
            num_scalar_prefetch=1,
            grid=(1,),
            in_specs=[WHOLE] * len(operands),
            out_specs=[WHOLE] * outs if last else WHOLE,
            scratch_shapes=[pltpu.VMEM((rows, width), jnp.float32)] if last else [],
        ),
        out_shape=out_shape if last else jax.ShapeDtypeStruct((rows, width), jnp.float32),
        compiler_params=pltpu.CompilerParams(vmem_limit_bytes=VMEM_LIMIT),
        cost_estimate=COST,
    )(meta, *operands)


def spread(tiles, meta, applied, pieces, points):
    count = len(applied)
    applied = join_small(applied)
    rows = sum(block.shape[0] for block in applied)
    result = pl.pallas_call(
        functools.partial(spread_kernel, tiles, len(applied), len(pieces)),
        grid_spec=pltpu.PrefetchScalarGridSpec(
            num_scalar_prefetch=1,
            grid=(1,),
            in_specs=[WHOLE] * (len(applied) + len(pieces)),
            out_specs=[WHOLE] * len(applied),
            scratch_shapes=[pltpu.VMEM((rows, points), jnp.float32)],
        ),
        out_shape=[
            jax.ShapeDtypeStruct((block.shape[0], points), jnp.bfloat16) for block in applied
        ],
        compiler_params=pltpu.CompilerParams(vmem_limit_bytes=VMEM_LIMIT),
        cost_estimate=COST,
    )(meta, *applied, *pieces)
    return split_small(result, count)


def two_parts(values):
    high = values.astype(jnp.bfloat16)
    return high, (values - high.astype(jnp.float32)).astype(jnp.bfloat16)


def couple_kernel(high_ref, low_ref, *refs):
    parts, out_ref = refs[:-1], refs[-1]
    blocks, proj, unused = high_ref.shape
    for block in range(blocks):
        lanes = slice(block * proj, (block + 1) * proj)
        total = parts[0][:, lanes].astype(jnp.float32)
        for part in parts[1:]:
            total += part[:, lanes].astype(jnp.float32)
        high, low = two_parts(total)
        result = jnp.dot(high, high_ref[block], preferred_element_type=jnp.float32)
        result += jnp.dot(high, low_ref[block], preferred_element_type=jnp.float32)
        result += jnp.dot(low, high_ref[block], preferred_element_type=jnp.float32)
        out_ref[:, lanes] = result.astype(out_ref.dtype)


def couple(parts, high, low):
    return pl.pallas_call(
        couple_kernel,
        in_specs=[WHOLE] * (2 + len(parts)),
        out_specs=WHOLE,
        out_shape=jax.ShapeDtypeStruct(parts[0].shape, jnp.bfloat16),
        compiler_params=pltpu.CompilerParams(vmem_limit_bytes=VMEM_LIMIT),
        cost_estimate=COST,
    )(high, low, *parts)


def coupling_matrix(coupling):
    blocks, atoms, width, unused = coupling.shape
    proj = atoms * width
    wide = jnp.tile(coupling.reshape(blocks, proj, width), (1, 1, atoms))
    same = jnp.arange(proj)[:, None] // width == jnp.arange(proj)[None, :] // width
    return jnp.where(same[None], wide, 0.0)


def body(n_grid, wavefunctions, tile_segment, tile_block, tile_count, projectors, coupling):
    half = n_grid // 2
    bands, npts = wavefunctions.shape
    points = npts // n_grid
    tiles = projectors.shape[0]
    width = coupling.shape[0] * projectors.shape[2]
    index = lax.axis_index("grid")
    side, place = index // half, index % half
    group, core = lax.axis_index("groups"), lax.axis_index("band")
    partners = [(i, (i + half) % n_grid) for i in range(n_grid)]
    pools = [list(range(half)), list(range(half, n_grid))]
    swap = [(0, 1), (1, 0)]

    def exchange(blocks):
        return [blocks[0]] + [
            lax.ppermute(
                blocks[d], "grid", [(i, i // half * half + (i % half ^ d)) for i in range(n_grid)]
            )
            for d in range(1, half)
        ]

    def to_bricks(which):
        part = lax.dynamic_slice_in_dim(wavefunctions, which * half * points, half * points, 1)
        return lax.all_to_all(
            part, "grid", split_axis=1, concat_axis=0, tiled=True, axis_index_groups=pools
        )

    lists = jnp.concatenate([tile_segment, tile_block, tile_count])
    other_lists = lax.ppermute(lists, "grid", partners)
    own_wave = to_bricks(side)
    other_wave = to_bricks(1 - side)
    meta = jnp.concatenate([lists, jnp.stack([place])])
    total = project(tiles, meta, own_wave, [projectors], half, width)
    matrix = two_parts(coupling_matrix(coupling))

    pieces, bases = [], []
    parts = 4
    size = tiles // parts
    share = size // 4
    for part in range(parts):
        mine = lax.dynamic_slice_in_dim(
            projectors, part * size + (2 * group + core) * share, share, 0
        )
        mine = lax.ppermute(mine, "grid", partners)
        if part == 0:
            mine, matrix, other_lists = lax.optimization_barrier((mine, matrix, other_lists))
        both = jnp.concatenate([mine, lax.ppermute(mine, "groups", swap)])
        if part == 0:
            both, total, other_wave = lax.optimization_barrier((both, total, other_wave))
        pieces += [both, lax.ppermute(both, "band", swap)]
        for other_core in (core, 1 - core):
            for other_group in (group, 1 - group):
                bases.append(part * size + (2 * other_group + other_core) * share)

    other_meta = jnp.concatenate([other_lists, jnp.stack([place] + bases)])
    for first, end in ((0, 2), (2, 3), (3, 4)):
        skip = 2 * tiles + HEAD
        piece_meta = jnp.concatenate(
            [other_meta[:skip], other_meta[skip + 4 * first : skip + 4 * end]]
        )
        total = project(
            tiles,
            piece_meta,
            other_wave,
            pieces[2 * first : 2 * end],
            half,
            width,
            total,
            last=end == parts,
        )
    if len(total) < half:
        total = [lax.dynamic_slice_in_dim(total[0], (place ^ d) * bands, bands, 0) for d in range(half)]

    applied = couple(exchange(total), *matrix)
    applied = exchange([applied] * half)

    result = jnp.zeros((bands, npts), jnp.bfloat16)
    for which, field in (
        (1 - side, spread(tiles, other_meta, applied, pieces, points)),
        (side, spread(tiles, meta, applied, [projectors], points)),
    ):
        for d, block in enumerate(exchange(field)):
            start = (which * half + (place ^ d)) * points
            result = lax.dynamic_update_slice_in_dim(result, block, start, 1)
    return result


def solution(mesh):
    in_specs = (
        P(("groups", "grid", "band"), None),
        P("grid"),
        P("grid"),
        P("grid"),
        P("grid", None, None),
        P(),
    )
    out_specs = P(("groups", "grid", "band"), None)
    return jax.shard_map(
        functools.partial(body, mesh.shape["grid"]),
        mesh=mesh,
        in_specs=in_specs,
        out_specs=out_specs,
        check_vma=False,
    )
```

```python
import functools

import jax
import jax.numpy as jnp
from jax import lax
from jax.experimental import pallas as pl
from jax.experimental.pallas import tpu as pltpu
from jax.sharding import PartitionSpec as P

TILE = 64
PAIR = 2 * TILE
UNROLL = 4
VMEM_LIMIT = 16 * 1024 * 1024
PARTS = 4
RANGES = ((0, 2), (2, 3), (3, 4))
OWN_FORWARD, OWN_BACKWARD, OTHER_FORWARD, OTHER_BACKWARD = range(4)
BOUNDS = 3
STEPS = len(RANGES) + 1
LISTS = BOUNDS + 4 * STEPS


def bits(count):
    return max(1, (count - 1).bit_length())


def pair_lists(codes, keys, live, blocks, absent):
    n_lists, tiles = codes.shape
    n_keys = len(RANGES) * blocks
    order = jnp.arange(tiles, dtype=jnp.int32)
    key_range = jnp.arange(n_keys, dtype=jnp.int32)
    mine = (keys[:, None, :] == key_range[None, :, None]) & live[:, None, :]
    pairs = (jnp.sum(mine, axis=2, dtype=jnp.int32) + 1) // 2
    lower = key_range[None, :, None] < key_range[None, None, :]
    starts = jnp.sum(jnp.where(lower, pairs[:, :, None], 0), axis=1, dtype=jnp.int32)
    before = (
        (keys[:, :, None] == keys[:, None, :]) & live[:, :, None] & (order[:, None] < order[None, :])
    )
    entry = jnp.sum(before, axis=1, dtype=jnp.int32) + 2 * jnp.sum(
        jnp.where(mine, starts[:, :, None], 0), axis=1, dtype=jnp.int32
    )
    entry = jnp.where(live, entry, -1)
    found = entry[:, :, None] == jnp.arange(tiles + n_keys, dtype=jnp.int32)
    entries = absent + jnp.sum(
        jnp.where(found, codes[:, :, None] - absent, 0), axis=1, dtype=jnp.int32
    )
    ends = jnp.arange(STEPS, dtype=jnp.int32) * blocks
    bounds = jnp.sum(
        jnp.where(key_range[None, :, None] < ends, pairs[:, :, None], 0), axis=1, dtype=jnp.int32
    )
    return jnp.concatenate([bounds.reshape(-1), entries.reshape(-1)])


def padded_tile(values, half):
    zero = jnp.zeros_like(values)
    return jnp.concatenate(
        [jnp.where(half == 0, values, zero), jnp.where(half == 1, values, zero)], axis=0
    )


def pair_loop(sizes, meta, ref, proj, which, first, last, origin, step):
    tiles, segments, blocks = sizes
    begin, end = (meta[BOUNDS + STEPS * which + number] for number in (first, last))
    base = LISTS + which * (tiles + len(RANGES) * blocks)

    def tile(entry, live):
        code = meta[base + entry]
        index = jnp.where(live, (code & ((1 << bits(tiles)) - 1)) - origin, 0)
        code = code >> bits(tiles)
        segment = code & ((1 << bits(segments)) - 1)
        code = code >> bits(segments)
        block = code & ((1 << bits(blocks)) - 1)
        half = jnp.where(live, (segment & 1) + 2 * (code >> bits(blocks)), 2)
        points = pl.ds(pl.multiple_of((segment >> 1) * PAIR, PAIR), PAIR)
        lanes = pl.ds(pl.multiple_of(block * proj, proj), proj)
        return points, lanes, padded_tile(ref[jnp.maximum(index, 0)], half)

    def group(index, carry):
        for lane in range(UNROLL):
            pair = begin + index * UNROLL + lane
            live = pair < end
            pair = jnp.minimum(pair, end - 1)
            step(tile(2 * pair, live), tile(2 * pair + 1, live))
        return carry

    lax.fori_loop(0, (end - begin + UNROLL - 1) // UNROLL, group, 0)


def join_pieces(meta, pieces, joined, first):
    size = pieces[0].shape[0]
    for number, ref in enumerate(pieces):

        @pl.when(meta[2] > first + number // 2 * 2 * size)
        def copy(number=number, ref=ref):
            joined[number * size : (number + 1) * size] = ref[...]


def rows_of(refs, lanes):
    return jnp.concatenate([ref[:, lanes] for ref in refs], axis=0)


def store_rows(refs, values):
    start = 0
    for ref in refs:
        rows = ref.shape[0]
        ref[...] = values[start : start + rows].astype(ref.dtype)
        start += rows


def project_kernel(sizes, n_pieces, spot, first, last, meta, wave, *refs):
    pieces, refs = refs[:n_pieces], refs[n_pieces:]
    proj = pieces[0].shape[2]
    values = pieces[0]
    if n_pieces > 1:
        values, refs = refs[-1], refs[:-1]
        join_pieces(meta, pieces, values, spot[-1])
    total = refs[-1]
    total[...] = jnp.zeros_like(total) if first else refs[0][...]

    def step(one, two):
        waves = jnp.concatenate([wave[:, one[0]], wave[:, two[0]]], axis=1)
        tiles = jnp.concatenate([one[2], two[2]], axis=0)
        total[:, one[1]] += jnp.dot(waves, tiles, preferred_element_type=jnp.float32)

    pair_loop(sizes, meta, values, proj, *spot, step)
    if last:
        outs = refs[1:-1]
        rows = outs[0].shape[0]
        for d, out in enumerate(outs):
            start = 0 if len(outs) == 1 else pl.multiple_of((meta[0] ^ d) * rows, rows)
            out[...] = total[pl.ds(start, rows), :].astype(out.dtype)


def spread_kernel(sizes, n_rows, n_pieces, which, meta, *refs):
    applied, refs = refs[:n_rows], refs[n_rows:]
    pieces, refs = refs[:n_pieces], refs[n_pieces:]
    proj = pieces[0].shape[2]
    values = pieces[0]
    if n_pieces > 1:
        values, refs = refs[-1], refs[:-1]
        join_pieces(meta, pieces, values, 0)
    outs, field = refs[:-1], refs[-1]
    field[...] = jnp.zeros_like(field)

    def step(one, two):
        rows = jnp.concatenate([rows_of(applied, one[1]), rows_of(applied, two[1])], axis=1)
        tiles = jnp.concatenate([one[2], two[2]], axis=1)
        field[:, one[0]] += lax.dot_general(
            rows, tiles, (((1,), (1,)), ((), ())), preferred_element_type=jnp.float32
        )

    pair_loop(sizes, meta, values, proj, which, 0, len(RANGES), 0, step)
    store_rows(outs, field)


WHOLE = pl.BlockSpec(memory_space=pltpu.VMEM)


COST = pl.CostEstimate(flops=1, bytes_accessed=1, transcendentals=0)


def join_small(blocks):
    return blocks if blocks[0].shape[0] % 16 == 0 else [jnp.concatenate(blocks)]


def split_small(blocks, count):
    return blocks if len(blocks) == count else jnp.split(blocks[0], count)


def joined_shape(pieces):
    if len(pieces) == 1:
        return []
    shape = pieces[0].shape
    return [pltpu.VMEM((len(pieces) * shape[0],) + shape[1:], jnp.bfloat16)]


def project(sizes, meta, wave, pieces, count, width, spot, total=None, last=False):
    rows = wave.shape[0]
    bands = rows // count
    split = bands % 16 == 0
    operands = [wave, *pieces] + ([] if total is None else [total])
    outs = count if split else 1
    out_shape = [jax.ShapeDtypeStruct((rows // outs, width), jnp.bfloat16)] * outs
    return pl.pallas_call(
        functools.partial(
            project_kernel, sizes, len(pieces), spot, total is None, last
        ),
        grid_spec=pltpu.PrefetchScalarGridSpec(
            num_scalar_prefetch=1,
            grid=(1,),
            in_specs=[WHOLE] * len(operands),
            out_specs=[WHOLE] * outs if last else WHOLE,
            scratch_shapes=([pltpu.VMEM((rows, width), jnp.float32)] if last else [])
            + joined_shape(pieces),
        ),
        out_shape=out_shape if last else jax.ShapeDtypeStruct((rows, width), jnp.float32),
        compiler_params=pltpu.CompilerParams(vmem_limit_bytes=VMEM_LIMIT),
        cost_estimate=COST,
    )(meta, *operands)


def spread(sizes, meta, applied, pieces, points, which):
    count = len(applied)
    applied = join_small(applied)
    rows = sum(block.shape[0] for block in applied)
    result = pl.pallas_call(
        functools.partial(spread_kernel, sizes, len(applied), len(pieces), which),
        grid_spec=pltpu.PrefetchScalarGridSpec(
            num_scalar_prefetch=1,
            grid=(1,),
            in_specs=[WHOLE] * (len(applied) + len(pieces)),
            out_specs=[WHOLE] * len(applied),
            scratch_shapes=[pltpu.VMEM((rows, points), jnp.float32)] + joined_shape(pieces),
        ),
        out_shape=[
            jax.ShapeDtypeStruct((block.shape[0], points), jnp.bfloat16) for block in applied
        ],
        compiler_params=pltpu.CompilerParams(vmem_limit_bytes=VMEM_LIMIT),
        cost_estimate=COST,
    )(meta, *applied, *pieces)
    return split_small(result, count)


def two_parts(values):
    high = values.astype(jnp.bfloat16)
    return high, (values - high.astype(jnp.float32)).astype(jnp.bfloat16)


def couple_kernel(high_ref, low_ref, *refs):
    parts, out_ref = refs[:-1], refs[-1]
    blocks, proj, unused = high_ref.shape
    for block in range(blocks):
        lanes = slice(block * proj, (block + 1) * proj)
        total = parts[0][:, lanes].astype(jnp.float32)
        for part in parts[1:]:
            total += part[:, lanes].astype(jnp.float32)
        high, low = two_parts(total)
        result = jnp.dot(high, high_ref[block], preferred_element_type=jnp.float32)
        result += jnp.dot(high, low_ref[block], preferred_element_type=jnp.float32)
        result += jnp.dot(low, high_ref[block], preferred_element_type=jnp.float32)
        out_ref[:, lanes] = result.astype(out_ref.dtype)


def couple(parts, high, low):
    return pl.pallas_call(
        couple_kernel,
        in_specs=[WHOLE] * (2 + len(parts)),
        out_specs=WHOLE,
        out_shape=jax.ShapeDtypeStruct(parts[0].shape, jnp.bfloat16),
        compiler_params=pltpu.CompilerParams(vmem_limit_bytes=VMEM_LIMIT),
        cost_estimate=COST,
    )(high, low, *parts)


def coupling_matrix(coupling):
    blocks, atoms, width, unused = coupling.shape
    proj = atoms * width
    wide = jnp.tile(coupling.reshape(blocks, proj, width), (1, 1, atoms))
    same = jnp.arange(proj)[:, None] // width == jnp.arange(proj)[None, :] // width
    return jnp.where(same[None], wide, 0.0)


def body(n_grid, wavefunctions, tile_segment, tile_block, tile_count, projectors, coupling):
    half = n_grid // 2
    bands, npts = wavefunctions.shape
    points = npts // n_grid
    tiles = projectors.shape[0]
    width = coupling.shape[0] * projectors.shape[2]
    index = lax.axis_index("grid")
    side, place = index // half, index % half
    group, core = lax.axis_index("groups"), lax.axis_index("band")
    partners = [(i, (i + half) % n_grid) for i in range(n_grid)]
    pools = [list(range(half)), list(range(half, n_grid))]
    swap = [(0, 1), (1, 0)]

    def exchange(blocks):
        return [blocks[0]] + [
            lax.ppermute(
                blocks[d], "grid", [(i, i // half * half + (i % half ^ d)) for i in range(n_grid)]
            )
            for d in range(1, half)
        ]

    def to_bricks(which):
        part = lax.dynamic_slice_in_dim(wavefunctions, which * half * points, half * points, 1)
        return lax.all_to_all(
            part, "grid", split_axis=1, concat_axis=0, tiled=True, axis_index_groups=pools
        )

    segments, blocks = points // TILE, coupling.shape[0]
    sizes = (tiles, segments, blocks)
    size = tiles // PARTS
    share = size // 4
    slots = jnp.arange(tiles, dtype=jnp.int32)
    part, quarter = slots // size, slots % size // share
    held = part * size + slots % share
    held += share * ((quarter // 2 ^ group) + 2 * (quarter % 2 ^ core))

    numbers = jnp.stack([tile_segment, tile_block, jnp.broadcast_to(tile_count, (tiles,))])
    others = lax.ppermute(numbers, "grid", partners)
    absent = 1 << (bits(tiles) + bits(segments) + bits(blocks))
    segment, block = (jnp.stack([numbers[i], others[i]]) for i in (0, 1))
    codes = jnp.stack([slots, held]) + ((segment + (block << bits(segments))) << bits(tiles))
    live = slots < jnp.stack([numbers[2], others[2]])
    group_of = sum(jnp.where(part >= first, 1, 0) for first, end in RANGES[1:])
    keys = jnp.stack([block + blocks * jnp.stack([0 * part, group_of]), segment // 2], axis=1)
    codes, live = (jnp.stack([values] * 2, axis=1) for values in (codes, live))
    meta = jnp.concatenate(
        [
            jnp.stack([place, numbers[2, 0], others[2, 0]]),
            pair_lists(*(v.reshape(4, tiles) for v in (codes, keys, live)), blocks, absent),
        ]
    )

    own_wave = to_bricks(side)
    other_wave = to_bricks(1 - side)
    spot = (OWN_FORWARD, 0, len(RANGES), 0)
    own_total = project(sizes, meta, own_wave, [projectors], half, width, spot)
    matrix = two_parts(coupling_matrix(coupling))

    pieces = []
    for part in range(PARTS):
        mine = lax.dynamic_slice_in_dim(
            projectors, part * size + (2 * group + core) * share, share, 0
        )
        mine = lax.ppermute(mine, "grid", partners)
        if part == 0:
            mine, total, matrix = lax.optimization_barrier((mine, own_total, matrix))
        else:
            mine = lax.optimization_barrier((mine, own_total))[0]
        both = jnp.concatenate([mine, lax.ppermute(mine, "groups", swap)])
        if part == 0:
            both, other_wave = lax.optimization_barrier((both, other_wave))
        pieces += [both, lax.ppermute(both, "band", swap)]

    for number, (first, end) in enumerate(RANGES):
        total = project(
            sizes,
            meta,
            other_wave,
            pieces[2 * first : 2 * end],
            half,
            width,
            (OTHER_FORWARD, number, number + 1, first * size),
            total,
            last=end == PARTS,
        )
    if len(total) < half:
        total = [lax.dynamic_slice_in_dim(total[0], (place ^ d) * bands, bands, 0) for d in range(half)]

    applied = couple(exchange(total), *matrix)
    applied = exchange([applied] * half)

    result = jnp.zeros((bands, npts), jnp.bfloat16)
    for which, field in (
        (1 - side, spread(sizes, meta, applied, pieces, points, OTHER_BACKWARD)),
        (side, spread(sizes, meta, applied, [projectors], points, OWN_BACKWARD)),
    ):
        for d, block in enumerate(exchange(field)):
            start = (which * half + (place ^ d)) * points
            result = lax.dynamic_update_slice_in_dim(result, block, start, 1)
    return result


def solution(mesh):
    in_specs = (
        P(("groups", "grid", "band"), None),
        P("grid"),
        P("grid"),
        P("grid"),
        P("grid", None, None),
        P(),
    )
    out_specs = P(("groups", "grid", "band"), None)
    return jax.shard_map(
        functools.partial(body, mesh.shape["grid"]),
        mesh=mesh,
        in_specs=in_specs,
        out_specs=out_specs,
        check_vma=False,
    )
```

```python
import functools

import jax
import jax.numpy as jnp
from jax import lax
from jax.experimental import pallas as pl
from jax.experimental.pallas import tpu as pltpu
from jax.sharding import PartitionSpec as P

TILE = 64
PAIR = 2 * TILE
UNROLL = 4
VMEM_LIMIT = 16 * 1024 * 1024
PARTS = 3
RANGES = ((0, 2), (2, 3))
OWN_FORWARD, OWN_BACKWARD, OTHER_FORWARD, OTHER_BACKWARD = range(4)
BOUNDS = 3
STEPS = len(RANGES) + 1
LISTS = BOUNDS + 4 * STEPS


def bits(count):
    return max(1, (count - 1).bit_length())


def pair_lists(codes, keys, live, blocks, absent):
    n_lists, tiles = codes.shape
    n_keys = len(RANGES) * blocks
    order = jnp.arange(tiles, dtype=jnp.int32)
    key_range = jnp.arange(n_keys, dtype=jnp.int32)
    mine = (keys[:, None, :] == key_range[None, :, None]) & live[:, None, :]
    pairs = (jnp.sum(mine, axis=2, dtype=jnp.int32) + 1) // 2
    lower = key_range[None, :, None] < key_range[None, None, :]
    starts = jnp.sum(jnp.where(lower, pairs[:, :, None], 0), axis=1, dtype=jnp.int32)
    before = (
        (keys[:, :, None] == keys[:, None, :]) & live[:, :, None] & (order[:, None] < order[None, :])
    )
    entry = jnp.sum(before, axis=1, dtype=jnp.int32) + 2 * jnp.sum(
        jnp.where(mine, starts[:, :, None], 0), axis=1, dtype=jnp.int32
    )
    entry = jnp.where(live, entry, -1)
    found = entry[:, :, None] == jnp.arange(tiles + n_keys, dtype=jnp.int32)
    entries = absent + jnp.sum(
        jnp.where(found, codes[:, :, None] - absent, 0), axis=1, dtype=jnp.int32
    )
    ends = jnp.arange(STEPS, dtype=jnp.int32) * blocks
    bounds = jnp.sum(
        jnp.where(key_range[None, :, None] < ends, pairs[:, :, None], 0), axis=1, dtype=jnp.int32
    )
    return jnp.concatenate([bounds.reshape(-1), entries.reshape(-1)])


def padded_tile(values, half):
    zero = jnp.zeros_like(values)
    return jnp.concatenate(
        [jnp.where(half == 0, values, zero), jnp.where(half == 1, values, zero)], axis=0
    )


def pair_loop(sizes, meta, ref, proj, which, first, last, origin, product, sums):
    tiles, segments, blocks = sizes
    begin, end = (meta[BOUNDS + STEPS * which + number] for number in (first, last))
    base = LISTS + which * (tiles + len(RANGES) * blocks)

    def tile(entry, live):
        code = meta[base + entry]
        index = jnp.where(live, (code & ((1 << bits(tiles)) - 1)) - origin, 0)
        code = code >> bits(tiles)
        segment = code & ((1 << bits(segments)) - 1)
        code = code >> bits(segments)
        block = code & ((1 << bits(blocks)) - 1)
        half = jnp.where(live, (segment & 1) + 2 * (code >> bits(blocks)), 2)
        points = pl.ds(pl.multiple_of((segment >> 1) * PAIR, PAIR), PAIR)
        lanes = pl.ds(pl.multiple_of(block * proj, proj), proj)
        return points, lanes, padded_tile(ref[jnp.maximum(index, 0)], half)

    def group(index, carry):
        terms = []
        for lane in range(UNROLL):
            pair = begin + index * UNROLL + lane
            live = pair < end
            pair = jnp.minimum(pair, end - 1)
            terms.append(product(tile(2 * pair, live), tile(2 * pair + 1, live)))
        for lanes, term in terms:
            sums[:, lanes] += term
        return carry

    lax.fori_loop(0, (end - begin + UNROLL - 1) // UNROLL, group, 0)


def join_pieces(meta, pieces, joined, first):
    size = pieces[0].shape[0]
    for number, ref in enumerate(pieces):

        @pl.when(meta[2] > first + number // 2 * 2 * size)
        def copy(number=number, ref=ref):
            joined[number * size : (number + 1) * size] = ref[...]


def rows_of(refs, lanes):
    return jnp.concatenate([ref[:, lanes] for ref in refs], axis=0)


def store_rows(refs, values):
    start = 0
    for ref in refs:
        rows = ref.shape[0]
        ref[...] = values[start : start + rows].astype(ref.dtype)
        start += rows


def project_kernel(sizes, n_pieces, spot, first, last, meta, wave, *refs):
    pieces, refs = refs[:n_pieces], refs[n_pieces:]
    proj = pieces[0].shape[2]
    values = pieces[0]
    if n_pieces > 1:
        values, refs = refs[-1], refs[:-1]
        join_pieces(meta, pieces, values, spot[-1])
    total = refs[-1]
    total[...] = jnp.zeros_like(total) if first else refs[0][...]

    def product(one, two):
        waves = jnp.concatenate([wave[:, one[0]], wave[:, two[0]]], axis=1)
        tiles = jnp.concatenate([one[2], two[2]], axis=0)
        return one[1], jnp.dot(waves, tiles, preferred_element_type=jnp.float32)

    pair_loop(sizes, meta, values, proj, *spot, product, total)
    if last:
        outs = refs[1:-1]
        rows = outs[0].shape[0]
        for d, out in enumerate(outs):
            start = 0 if len(outs) == 1 else pl.multiple_of((meta[0] ^ d) * rows, rows)
            out[...] = total[pl.ds(start, rows), :].astype(out.dtype)


def spread_kernel(sizes, n_rows, n_pieces, which, meta, *refs):
    applied, refs = refs[:n_rows], refs[n_rows:]
    pieces, refs = refs[:n_pieces], refs[n_pieces:]
    proj = pieces[0].shape[2]
    values = pieces[0]
    if n_pieces > 1:
        values, refs = refs[-1], refs[:-1]
        join_pieces(meta, pieces, values, 0)
    outs, field = refs[:-1], refs[-1]
    field[...] = jnp.zeros_like(field)

    def product(one, two):
        rows = jnp.concatenate([rows_of(applied, one[1]), rows_of(applied, two[1])], axis=1)
        tiles = jnp.concatenate([one[2], two[2]], axis=1)
        return one[0], lax.dot_general(
            rows, tiles, (((1,), (1,)), ((), ())), preferred_element_type=jnp.float32
        )

    pair_loop(sizes, meta, values, proj, which, 0, len(RANGES), 0, product, field)
    store_rows(outs, field)


WHOLE = pl.BlockSpec(memory_space=pltpu.VMEM)


def cost(us):
    return pl.CostEstimate(flops=1 + us * 10**9, bytes_accessed=1, transcendentals=0)


def join_small(blocks):
    return blocks if blocks[0].shape[0] % 16 == 0 else [jnp.concatenate(blocks)]


def split_small(blocks, count):
    return blocks if len(blocks) == count else jnp.split(blocks[0], count)


def joined_shape(pieces):
    if len(pieces) == 1:
        return []
    shape = pieces[0].shape
    return [pltpu.VMEM((len(pieces) * shape[0],) + shape[1:], jnp.bfloat16)]


def project(sizes, meta, wave, pieces, count, width, spot, total=None, last=False, us=0):
    rows = wave.shape[0]
    bands = rows // count
    split = bands % 16 == 0
    operands = [wave, *pieces] + ([] if total is None else [total])
    outs = count if split else 1
    out_shape = [jax.ShapeDtypeStruct((rows // outs, width), jnp.bfloat16)] * outs
    return pl.pallas_call(
        functools.partial(
            project_kernel, sizes, len(pieces), spot, total is None, last
        ),
        grid_spec=pltpu.PrefetchScalarGridSpec(
            num_scalar_prefetch=1,
            grid=(1,),
            in_specs=[WHOLE] * len(operands),
            out_specs=[WHOLE] * outs if last else WHOLE,
            scratch_shapes=([pltpu.VMEM((rows, width), jnp.float32)] if last else [])
            + joined_shape(pieces),
        ),
        out_shape=out_shape if last else jax.ShapeDtypeStruct((rows, width), jnp.float32),
        compiler_params=pltpu.CompilerParams(vmem_limit_bytes=VMEM_LIMIT),
        cost_estimate=cost(us),
    )(meta, *operands)


def spread(sizes, meta, applied, pieces, points, which):
    count = len(applied)
    applied = join_small(applied)
    rows = sum(block.shape[0] for block in applied)
    result = pl.pallas_call(
        functools.partial(spread_kernel, sizes, len(applied), len(pieces), which),
        grid_spec=pltpu.PrefetchScalarGridSpec(
            num_scalar_prefetch=1,
            grid=(1,),
            in_specs=[WHOLE] * (len(applied) + len(pieces)),
            out_specs=[WHOLE] * len(applied),
            scratch_shapes=[pltpu.VMEM((rows, points), jnp.float32)] + joined_shape(pieces),
        ),
        out_shape=[
            jax.ShapeDtypeStruct((block.shape[0], points), jnp.bfloat16) for block in applied
        ],
        compiler_params=pltpu.CompilerParams(vmem_limit_bytes=VMEM_LIMIT),
        cost_estimate=cost(0),
    )(meta, *applied, *pieces)
    return split_small(result, count)


def two_parts(values):
    high = values.astype(jnp.bfloat16)
    return high, (values - high.astype(jnp.float32)).astype(jnp.bfloat16)


def couple_kernel(high_ref, low_ref, *refs):
    parts, out_ref = refs[:-1], refs[-1]
    blocks, proj, unused = high_ref.shape
    for block in range(blocks):
        lanes = slice(block * proj, (block + 1) * proj)
        total = parts[0][:, lanes].astype(jnp.float32)
        for part in parts[1:]:
            total += part[:, lanes].astype(jnp.float32)
        high, low = two_parts(total)
        result = jnp.dot(high, high_ref[block], preferred_element_type=jnp.float32)
        result += jnp.dot(high, low_ref[block], preferred_element_type=jnp.float32)
        result += jnp.dot(low, high_ref[block], preferred_element_type=jnp.float32)
        out_ref[:, lanes] = result.astype(out_ref.dtype)


def couple(parts, high, low):
    return pl.pallas_call(
        couple_kernel,
        in_specs=[WHOLE] * (2 + len(parts)),
        out_specs=WHOLE,
        out_shape=jax.ShapeDtypeStruct(parts[0].shape, jnp.bfloat16),
        compiler_params=pltpu.CompilerParams(vmem_limit_bytes=VMEM_LIMIT),
        cost_estimate=cost(0),
    )(high, low, *parts)


def coupling_matrix(coupling):
    blocks, atoms, width, unused = coupling.shape
    proj = atoms * width
    wide = jnp.tile(coupling.reshape(blocks, proj, width), (1, 1, atoms))
    same = jnp.arange(proj)[:, None] // width == jnp.arange(proj)[None, :] // width
    return jnp.where(same[None], wide, 0.0)


def body(n_grid, wavefunctions, tile_segment, tile_block, tile_count, projectors, coupling):
    half = n_grid // 2
    bands, npts = wavefunctions.shape
    points = npts // n_grid
    tiles = projectors.shape[0]
    width = coupling.shape[0] * projectors.shape[2]
    index = lax.axis_index("grid")
    side, place = index // half, index % half
    group, core = lax.axis_index("groups"), lax.axis_index("band")
    partners = [(i, (i + half) % n_grid) for i in range(n_grid)]
    pools = [list(range(half)), list(range(half, n_grid))]
    swap = [(0, 1), (1, 0)]

    def exchange(blocks):
        return [blocks[0]] + [
            lax.ppermute(
                blocks[d], "grid", [(i, i // half * half + (i % half ^ d)) for i in range(n_grid)]
            )
            for d in range(1, half)
        ]

    def to_bricks(which):
        part = lax.dynamic_slice_in_dim(wavefunctions, which * half * points, half * points, 1)
        return lax.all_to_all(
            part, "grid", split_axis=1, concat_axis=0, tiled=True, axis_index_groups=pools
        )

    segments, blocks = points // TILE, coupling.shape[0]
    sizes = (tiles, segments, blocks)
    size = tiles // PARTS
    share = size // 4
    slots = jnp.arange(tiles, dtype=jnp.int32)
    part, quarter = slots // size, slots % size // share
    held = part * size + slots % share
    held += share * ((quarter // 2 ^ group) + 2 * (quarter % 2 ^ core))

    numbers = jnp.stack([tile_segment, tile_block, jnp.broadcast_to(tile_count, (tiles,))])
    others = lax.ppermute(numbers, "grid", partners)
    absent = 1 << (bits(tiles) + bits(segments) + bits(blocks))
    segment, block = (jnp.stack([numbers[i], others[i]]) for i in (0, 1))
    codes = jnp.stack([slots, held]) + ((segment + (block << bits(segments))) << bits(tiles))
    live = slots < jnp.stack([numbers[2], others[2]])
    group_of = sum(jnp.where(part >= first, 1, 0) for first, end in RANGES[1:])
    keys = jnp.stack([block + blocks * jnp.stack([0 * part, group_of]), segment // 2], axis=1)
    codes, live = (jnp.stack([values] * 2, axis=1) for values in (codes, live))
    meta = jnp.concatenate(
        [
            jnp.stack([place, numbers[2, 0], others[2, 0]]),
            pair_lists(*(v.reshape(4, tiles) for v in (codes, keys, live)), blocks, absent),
        ]
    )

    own_wave = to_bricks(side)
    other_wave = to_bricks(1 - side)
    spot = (OWN_FORWARD, 0, len(RANGES), 0)
    own_total = project(sizes, meta, own_wave, [projectors], half, width, spot, us=10)
    matrix = two_parts(coupling_matrix(coupling))

    pieces, mine, across = [], None, None
    for part in range(PARTS):
        start = part * size + (2 * group + core) * share
        sent = lax.dynamic_slice_in_dim(projectors, start, share, 0)
        if part > 0:
            sent = lax.optimization_barrier((sent, mine))[0]
        mine = lax.ppermute(sent, "grid", partners)
        sent = mine
        if part == 0:
            sent, matrix, meta = lax.optimization_barrier((sent, matrix, meta))
        else:
            sent = lax.optimization_barrier((sent, across))[0]
        across = lax.ppermute(sent, "groups", swap)
        both = jnp.concatenate([mine, across])
        if part == 0:
            both, total = lax.optimization_barrier((both, own_total))
        pieces += [both, lax.ppermute(both, "band", swap)]

    for number, (first, end) in enumerate(RANGES):
        total = project(
            sizes,
            meta,
            other_wave,
            pieces[2 * first : 2 * end],
            half,
            width,
            (OTHER_FORWARD, number, number + 1, first * size),
            total,
            last=end == PARTS,
            us=8 if end < PARTS else 0,
        )
    if len(total) < half:
        total = [lax.dynamic_slice_in_dim(total[0], (place ^ d) * bands, bands, 0) for d in range(half)]

    applied = couple(exchange(total), *matrix)
    applied = exchange([applied] * half)

    result = jnp.zeros((bands, npts), jnp.bfloat16)
    for which, field in (
        (1 - side, spread(sizes, meta, applied, pieces, points, OTHER_BACKWARD)),
        (side, spread(sizes, meta, applied, [projectors], points, OWN_BACKWARD)),
    ):
        for d, block in enumerate(exchange(field)):
            start = (which * half + (place ^ d)) * points
            result = lax.dynamic_update_slice_in_dim(result, block, start, 1)
    return result


def solution(mesh):
    in_specs = (
        P(("groups", "grid", "band"), None),
        P("grid"),
        P("grid"),
        P("grid"),
        P("grid", None, None),
        P(),
    )
    out_specs = P(("groups", "grid", "band"), None)
    return jax.shard_map(
        functools.partial(body, mesh.shape["grid"]),
        mesh=mesh,
        in_specs=in_specs,
        out_specs=out_specs,
        check_vma=False,
    )
```

```python
import functools

import jax
import jax.numpy as jnp
from jax import lax
from jax.experimental import pallas as pl
from jax.experimental.pallas import tpu as pltpu
from jax.sharding import PartitionSpec as P

TILE = 64
PAIR = 2 * TILE
UNROLL = 4
OWN_COPIES = 8
VMEM_LIMIT = 24 * 1024 * 1024
PARTS = 3
RANGES = ((0, 2), (2, 3))
OWN_FORWARD, OWN_BACKWARD, OTHER_FORWARD, OTHER_BACKWARD = range(4)
BOUNDS = 3
STEPS = len(RANGES) + 1
LISTS = BOUNDS + 4 * STEPS


def bits(count):
    return max(1, (count - 1).bit_length())


def list_length(tiles, blocks):
    return tiles + len(RANGES) * (blocks + 2 * UNROLL)


def pair_lists(codes, keys, live, blocks, absent):
    n_lists, tiles = codes.shape
    n_keys = len(RANGES) * blocks
    order = jnp.arange(tiles, dtype=jnp.int32)
    key_range = jnp.arange(n_keys, dtype=jnp.int32)
    ranges = jnp.arange(STEPS, dtype=jnp.int32)
    mine = (keys[:, None, :] == key_range[None, :, None]) & live[:, None, :]
    pairs = (jnp.sum(mine, axis=2, dtype=jnp.int32) + 1) // 2
    in_range = key_range[:, None] // blocks == ranges[None, :]
    totals = jnp.sum(jnp.where(in_range, pairs[:, :, None], 0), axis=1, dtype=jnp.int32)
    totals = (totals + UNROLL - 1) // UNROLL * UNROLL
    bounds = jnp.sum(
        jnp.where(ranges[:, None] < ranges[None, :], totals[:, :, None], 0), axis=1, dtype=jnp.int32
    )
    lower = (key_range[:, None] < key_range[None, :]) & (
        key_range[:, None] // blocks == key_range[None, :] // blocks
    )
    starts = jnp.sum(jnp.where(lower, pairs[:, :, None], 0), axis=1, dtype=jnp.int32)
    starts += jnp.sum(jnp.where(in_range, bounds[:, None, :], 0), axis=2, dtype=jnp.int32)
    before = (
        (keys[:, :, None] == keys[:, None, :]) & live[:, :, None] & (order[:, None] < order[None, :])
    )
    entry = jnp.sum(before, axis=1, dtype=jnp.int32) + 2 * jnp.sum(
        jnp.where(mine, starts[:, :, None], 0), axis=1, dtype=jnp.int32
    )
    entry = jnp.where(live, entry, -1)
    found = entry[:, :, None] == jnp.arange(list_length(tiles, blocks), dtype=jnp.int32)
    entries = absent + jnp.sum(
        jnp.where(found, codes[:, :, None] - absent, 0), axis=1, dtype=jnp.int32
    )
    return jnp.concatenate([bounds.reshape(-1), entries.reshape(-1)])


def pair_loop(sizes, meta, held, proj, which, first, last, origin, product, sums):
    tiles, segments, blocks = sizes
    begin, end = (meta[BOUNDS + STEPS * which + number] for number in (first, last))
    base = LISTS + which * list_length(tiles, blocks)
    final = 2 * (held.shape[0] - 1)

    def tile(entry):
        code = meta[base + entry]
        window = jnp.minimum((code & ((1 << bits(2 * tiles + 1)) - 1)) - 2 * origin, final)
        code = code >> bits(2 * tiles + 1)
        points = pl.ds(pl.multiple_of((code & ((1 << bits(segments // 2)) - 1)) * PAIR, PAIR), PAIR)
        lanes = pl.ds(pl.multiple_of((code >> bits(segments // 2)) * proj, proj), proj)
        values = [held[at >> 1, at & 1] for at in (window, window + 1)]
        return points, lanes, jnp.concatenate(values, axis=0)

    def group(index, carry):
        terms = []
        for lane in range(UNROLL):
            pair = begin + index * UNROLL + lane
            terms.append(product(tile(2 * pair), tile(2 * pair + 1)))
        for lanes, term in terms:
            sums[:, lanes] += term
        return carry

    lax.fori_loop(0, (end - begin) // UNROLL, group, 0)


def hold_pieces(meta, pieces, held, first):
    size = pieces[0].shape[0]
    for number, ref in enumerate(pieces):
        held[number * size, 0] = jnp.zeros(held.shape[2:], held.dtype)

        @pl.when(meta[2] > first + number // 2 * 2 * size)
        def copy(number=number, ref=ref):
            at = slice(number * size, (number + 1) * size)
            held[at, 0] = jnp.zeros_like(ref)
            held[at, 1] = ref[...]

    held[held.shape[0] - 1] = jnp.zeros(held.shape[1:], held.dtype)


def hold_own(meta, projectors, held, sems):
    tiles = projectors.shape[0]
    size = tiles // OWN_COPIES
    copies = []
    for number in range(OWN_COPIES):
        at = pl.ds(number * size, size)
        copies.append(
            pltpu.make_async_copy(projectors.at[at], held.at[at, 1], sems.at[number])
        )
        pl.when(meta[1] > number * size)(copies[number].start)
    for number in range(OWN_COPIES):
        at = slice(number * size, (number + 1) * size)
        held[number * size, 0] = jnp.zeros(held.shape[2:], held.dtype)

        @pl.when(meta[1] > number * size)
        def fill(at=at):
            held[at, 0] = jnp.zeros((size,) + held.shape[2:], held.dtype)

    held[tiles] = jnp.zeros(held.shape[1:], held.dtype)
    return copies, size


def wait_own(meta, copies, size):
    for number, copy in enumerate(copies):
        pl.when(meta[1] > number * size)(copy.wait)


def rows_of(refs, lanes):
    return jnp.concatenate([ref[:, lanes] for ref in refs], axis=0)


def store_rows(refs, values):
    start = 0
    for ref in refs:
        rows = ref.shape[0]
        ref[...] = values[start : start + rows].astype(ref.dtype)
        start += rows


def project_kernel(sizes, n_pieces, spot, first, last, meta, wave, *refs):
    pieces, refs = refs[:n_pieces], refs[n_pieces:]
    proj = pieces[0].shape[2]
    if n_pieces > 1:
        held, refs = refs[-1], refs[:-1]
        hold_pieces(meta, pieces, held, spot[-1])
    else:
        (held, sems), refs = refs[-2:], refs[:-2]
        copies = hold_own(meta, pieces[0], held, sems)
    total = refs[-1]
    total[...] = jnp.zeros_like(total) if first else refs[0][...]
    if n_pieces == 1:
        wait_own(meta, *copies)

    def product(one, two):
        waves = jnp.concatenate([wave[:, one[0]], wave[:, two[0]]], axis=1)
        tiles = jnp.concatenate([one[2], two[2]], axis=0)
        return one[1], jnp.dot(waves, tiles, preferred_element_type=jnp.float32)

    pair_loop(sizes, meta, held, proj, *spot, product, total)
    if last:
        outs = refs[1:-1]
        rows = outs[0].shape[0]
        for d, out in enumerate(outs):
            start = 0 if len(outs) == 1 else pl.multiple_of((meta[0] ^ d) * rows, rows)
            out[...] = total[pl.ds(start, rows), :].astype(out.dtype)


def spread_kernel(sizes, n_rows, n_pieces, which, meta, *refs):
    applied, refs = refs[:n_rows], refs[n_rows:]
    pieces, refs = refs[:n_pieces], refs[n_pieces:]
    proj = pieces[0].shape[2]
    if n_pieces > 1:
        held, refs = refs[-1], refs[:-1]
        hold_pieces(meta, pieces, held, 0)
    else:
        (held, sems), refs = refs[-2:], refs[:-2]
        copies = hold_own(meta, pieces[0], held, sems)
    outs, field = refs[:-1], refs[-1]
    field[...] = jnp.zeros_like(field)
    if n_pieces == 1:
        wait_own(meta, *copies)

    def product(one, two):
        rows = jnp.concatenate([rows_of(applied, one[1]), rows_of(applied, two[1])], axis=1)
        tiles = jnp.concatenate([one[2], two[2]], axis=1)
        return one[0], lax.dot_general(
            rows, tiles, (((1,), (1,)), ((), ())), preferred_element_type=jnp.float32
        )

    pair_loop(sizes, meta, held, proj, which, 0, len(RANGES), 0, product, field)
    store_rows(outs, field)


WHOLE = pl.BlockSpec(memory_space=pltpu.VMEM)


def cost(us):
    return pl.CostEstimate(flops=1 + us * 10**9, bytes_accessed=1, transcendentals=0)


def join_small(blocks):
    return blocks if blocks[0].shape[0] % 16 == 0 else [jnp.concatenate(blocks)]


def split_small(blocks, count):
    return blocks if len(blocks) == count else jnp.split(blocks[0], count)


def held_shape(pieces):
    shape = pieces[0].shape
    shape = (len(pieces) * shape[0] + 1, 2) + shape[1:]
    sems = [pltpu.SemaphoreType.DMA((OWN_COPIES,))] if len(pieces) == 1 else []
    return [pltpu.VMEM(shape, jnp.bfloat16)] + sems


def piece_specs(pieces):
    return [pl.BlockSpec(memory_space=pltpu.HBM) if len(pieces) == 1 else WHOLE] * len(pieces)


def project(sizes, meta, wave, pieces, count, width, spot, total=None, last=False, us=0):
    rows = wave.shape[0]
    bands = rows // count
    split = bands % 16 == 0
    operands = [wave, *pieces] + ([] if total is None else [total])
    outs = count if split else 1
    out_shape = [jax.ShapeDtypeStruct((rows // outs, width), jnp.bfloat16)] * outs
    return pl.pallas_call(
        functools.partial(
            project_kernel, sizes, len(pieces), spot, total is None, last
        ),
        grid_spec=pltpu.PrefetchScalarGridSpec(
            num_scalar_prefetch=1,
            grid=(1,),
            in_specs=[WHOLE] + piece_specs(pieces) + [WHOLE] * (total is not None),
            out_specs=[WHOLE] * outs if last else WHOLE,
            scratch_shapes=([pltpu.VMEM((rows, width), jnp.float32)] if last else [])
            + held_shape(pieces),
        ),
        out_shape=out_shape if last else jax.ShapeDtypeStruct((rows, width), jnp.float32),
        compiler_params=pltpu.CompilerParams(vmem_limit_bytes=VMEM_LIMIT),
        cost_estimate=cost(us),
    )(meta, *operands)


def spread(sizes, meta, applied, pieces, points, which):
    count = len(applied)
    applied = join_small(applied)
    rows = sum(block.shape[0] for block in applied)
    result = pl.pallas_call(
        functools.partial(spread_kernel, sizes, len(applied), len(pieces), which),
        grid_spec=pltpu.PrefetchScalarGridSpec(
            num_scalar_prefetch=1,
            grid=(1,),
            in_specs=[WHOLE] * len(applied) + piece_specs(pieces),
            out_specs=[WHOLE] * len(applied),
            scratch_shapes=[pltpu.VMEM((rows, points), jnp.float32)] + held_shape(pieces),
        ),
        out_shape=[
            jax.ShapeDtypeStruct((block.shape[0], points), jnp.bfloat16) for block in applied
        ],
        compiler_params=pltpu.CompilerParams(vmem_limit_bytes=VMEM_LIMIT),
        cost_estimate=cost(0),
    )(meta, *applied, *pieces)
    return split_small(result, count)


def two_parts(values):
    high = values.astype(jnp.bfloat16)
    return high, (values - high.astype(jnp.float32)).astype(jnp.bfloat16)


def couple_kernel(high_ref, low_ref, *refs):
    parts, out_ref = refs[:-1], refs[-1]
    blocks, proj, unused = high_ref.shape
    for block in range(blocks):
        lanes = slice(block * proj, (block + 1) * proj)
        total = parts[0][:, lanes].astype(jnp.float32)
        for part in parts[1:]:
            total += part[:, lanes].astype(jnp.float32)
        high, low = two_parts(total)
        result = jnp.dot(high, high_ref[block], preferred_element_type=jnp.float32)
        result += jnp.dot(high, low_ref[block], preferred_element_type=jnp.float32)
        result += jnp.dot(low, high_ref[block], preferred_element_type=jnp.float32)
        out_ref[:, lanes] = result.astype(out_ref.dtype)


def couple(parts, high, low):
    return pl.pallas_call(
        couple_kernel,
        in_specs=[WHOLE] * (2 + len(parts)),
        out_specs=WHOLE,
        out_shape=jax.ShapeDtypeStruct(parts[0].shape, jnp.bfloat16),
        compiler_params=pltpu.CompilerParams(vmem_limit_bytes=VMEM_LIMIT),
        cost_estimate=cost(0),
    )(high, low, *parts)


def coupling_matrix(coupling):
    blocks, atoms, width, unused = coupling.shape
    proj = atoms * width
    wide = jnp.tile(coupling.reshape(blocks, proj, width), (1, 1, atoms))
    same = jnp.arange(proj)[:, None] // width == jnp.arange(proj)[None, :] // width
    return jnp.where(same[None], wide, 0.0)


def body(n_grid, wavefunctions, tile_segment, tile_block, tile_count, projectors, coupling):
    half = n_grid // 2
    bands, npts = wavefunctions.shape
    points = npts // n_grid
    tiles = projectors.shape[0]
    width = coupling.shape[0] * projectors.shape[2]
    index = lax.axis_index("grid")
    side, place = index // half, index % half
    group, core = lax.axis_index("groups"), lax.axis_index("band")
    partners = [(i, (i + half) % n_grid) for i in range(n_grid)]
    pools = [list(range(half)), list(range(half, n_grid))]
    swap = [(0, 1), (1, 0)]

    def exchange(blocks):
        return [blocks[0]] + [
            lax.ppermute(
                blocks[d], "grid", [(i, i // half * half + (i % half ^ d)) for i in range(n_grid)]
            )
            for d in range(1, half)
        ]

    def to_bricks(which):
        part = lax.dynamic_slice_in_dim(wavefunctions, which * half * points, half * points, 1)
        return lax.all_to_all(
            part, "grid", split_axis=1, concat_axis=0, tiled=True, axis_index_groups=pools
        )

    segments, blocks = points // TILE, coupling.shape[0]
    sizes = (tiles, segments, blocks)
    size = tiles // PARTS
    share = size // 4
    slots = jnp.arange(tiles, dtype=jnp.int32)
    part, quarter = slots // size, slots % size // share
    held = part * size + slots % share
    held += share * ((quarter // 2 ^ group) + 2 * (quarter % 2 ^ core))

    numbers = jnp.stack([tile_segment, tile_block, jnp.broadcast_to(tile_count, (tiles,))])
    others = lax.ppermute(numbers, "grid", partners)
    absent = 2 * tiles
    segment, block = (jnp.stack([numbers[i], others[i]]) for i in (0, 1))
    codes = 2 * jnp.stack([slots, held]) + 1 - segment % 2
    places = segment // 2 + (block << bits(segments // 2))
    codes += places << bits(2 * tiles + 1)
    live = slots < jnp.stack([numbers[2], others[2]])
    group_of = sum(jnp.where(part >= first, 1, 0) for first, end in RANGES[1:])
    keys = jnp.stack([block + blocks * jnp.stack([0 * part, group_of]), segment // 2], axis=1)
    codes, live = (jnp.stack([values] * 2, axis=1) for values in (codes, live))
    meta = jnp.concatenate(
        [
            jnp.stack([place, numbers[2, 0], others[2, 0]]),
            pair_lists(*(v.reshape(4, tiles) for v in (codes, keys, live)), blocks, absent),
        ]
    )

    own_wave = to_bricks(side)
    other_wave = to_bricks(1 - side)
    spot = (OWN_FORWARD, 0, len(RANGES), 0)
    own_total = project(sizes, meta, own_wave, [projectors], half, width, spot, us=10)
    matrix = two_parts(coupling_matrix(coupling))

    pieces, mine, across = [], None, None
    for part in range(PARTS):
        start = part * size + (2 * group + core) * share
        sent = lax.dynamic_slice_in_dim(projectors, start, share, 0)
        if part > 0:
            sent = lax.optimization_barrier((sent, mine))[0]
        mine = lax.ppermute(sent, "grid", partners)
        sent = mine
        if part == 0:
            sent, matrix, meta = lax.optimization_barrier((sent, matrix, meta))
        else:
            sent = lax.optimization_barrier((sent, across))[0]
        across = lax.ppermute(sent, "groups", swap)
        both = jnp.concatenate([mine, across])
        if part == 0:
            both, total = lax.optimization_barrier((both, own_total))
        pieces += [both, lax.ppermute(both, "band", swap)]

    for number, (first, end) in enumerate(RANGES):
        total = project(
            sizes,
            meta,
            other_wave,
            pieces[2 * first : 2 * end],
            half,
            width,
            (OTHER_FORWARD, number, number + 1, first * size),
            total,
            last=end == PARTS,
            us=8 if end < PARTS else 0,
        )
    if len(total) < half:
        total = [lax.dynamic_slice_in_dim(total[0], (place ^ d) * bands, bands, 0) for d in range(half)]

    applied = couple(exchange(total), *matrix)
    applied = exchange([applied] * half)

    result = jnp.zeros((bands, npts), jnp.bfloat16)
    for which, field in (
        (1 - side, spread(sizes, meta, applied, pieces, points, OTHER_BACKWARD)),
        (side, spread(sizes, meta, applied, [projectors], points, OWN_BACKWARD)),
    ):
        for d, block in enumerate(exchange(field)):
            start = (which * half + (place ^ d)) * points
            result = lax.dynamic_update_slice_in_dim(result, block, start, 1)
    return result


def solution(mesh):
    in_specs = (
        P(("groups", "grid", "band"), None),
        P("grid"),
        P("grid"),
        P("grid"),
        P("grid", None, None),
        P(),
    )
    out_specs = P(("groups", "grid", "band"), None)
    return jax.shard_map(
        functools.partial(body, mesh.shape["grid"]),
        mesh=mesh,
        in_specs=in_specs,
        out_specs=out_specs,
        check_vma=False,
    )
```

```python
import functools

import jax
import jax.numpy as jnp
from jax import lax
from jax.experimental import pallas as pl
from jax.experimental.pallas import tpu as pltpu
from jax.sharding import PartitionSpec as P

TILE = 64
PAIR = 2 * TILE
GROUP = 4
UNROLL = 2
VMEM_LIMIT = 20 * 1024 * 1024
PARTS = 3
RANGES = ((0, 2), (2, 3))
OWN, OTHER = range(2)
BOUNDS = 3
STEPS = len(RANGES) + 1
LISTS = BOUNDS + 2 * STEPS


def bits(count):
    return max(1, (count - 1).bit_length())


def list_length(tiles, blocks):
    return tiles + len(RANGES) * ((GROUP - 1) * blocks + GROUP * UNROLL)


def group_lists(codes, keys, live, blocks, absent):
    n_lists, tiles = codes.shape
    n_keys = len(RANGES) * blocks
    order = jnp.arange(tiles, dtype=jnp.int32)
    key_range = jnp.arange(n_keys, dtype=jnp.int32)
    ranges = jnp.arange(STEPS, dtype=jnp.int32)
    mine = (keys[:, None, :] == key_range[None, :, None]) & live[:, None, :]
    groups = (jnp.sum(mine, axis=2, dtype=jnp.int32) + GROUP - 1) // GROUP
    in_range = key_range[:, None] // blocks == ranges[None, :]
    totals = jnp.sum(jnp.where(in_range, groups[:, :, None], 0), axis=1, dtype=jnp.int32)
    totals = (totals + UNROLL - 1) // UNROLL * UNROLL
    bounds = jnp.sum(
        jnp.where(ranges[:, None] < ranges[None, :], totals[:, :, None], 0), axis=1, dtype=jnp.int32
    )
    lower = (key_range[:, None] < key_range[None, :]) & (
        key_range[:, None] // blocks == key_range[None, :] // blocks
    )
    starts = jnp.sum(jnp.where(lower, groups[:, :, None], 0), axis=1, dtype=jnp.int32)
    starts += jnp.sum(jnp.where(in_range, bounds[:, None, :], 0), axis=2, dtype=jnp.int32)
    before = (
        (keys[:, :, None] == keys[:, None, :]) & live[:, :, None] & (order[:, None] < order[None, :])
    )
    entry = jnp.sum(before, axis=1, dtype=jnp.int32) + GROUP * jnp.sum(
        jnp.where(mine, starts[:, :, None], 0), axis=1, dtype=jnp.int32
    )
    entry = jnp.where(live, entry, -1)
    found = entry[:, :, None] == jnp.arange(list_length(tiles, blocks), dtype=jnp.int32)
    entries = absent + jnp.sum(
        jnp.where(found, codes[:, :, None] - absent, 0), axis=1, dtype=jnp.int32
    )
    return jnp.concatenate([bounds.reshape(-1), entries.reshape(-1)])


def group_loop(sizes, meta, values, proj, which, first, last, origin, product):
    tiles, segments, blocks = sizes
    begin, end = (meta[BOUNDS + STEPS * which + number] for number in (first, last))
    base = LISTS + which * list_length(tiles, blocks)

    def group(number):
        places = []
        for entry in range(GROUP):
            code = meta[base + GROUP * number + entry]
            index = jnp.maximum((code & ((1 << bits(tiles)) - 1)) - origin, 0)
            code = code >> bits(tiles)
            places.append((code & ((1 << bits(segments + 1)) - 1), values[index]))
            if entry == 0:
                block = code >> bits(segments + 1)
        lanes = pl.ds(pl.multiple_of(block * proj, proj), proj)
        return product(lanes, [at for at, tile in places], [tile for at, tile in places])

    def step(index, carry):
        sums = [group(begin + index * UNROLL + lane) for lane in range(UNROLL)]
        for additions in sums:
            for ref, rows, lanes, term in additions:
                ref[rows, lanes] += term
        return carry

    lax.fori_loop(0, (end - begin) // UNROLL, step, 0)


def join_pieces(meta, pieces, joined, first):
    size = pieces[0].shape[0]
    for number, ref in enumerate(pieces):

        @pl.when(meta[2] > first + number // 2 * 2 * size)
        def copy(number=number, ref=ref):
            joined[number * size : (number + 1) * size] = ref[...]


def rows_of(refs, lanes):
    return jnp.concatenate([ref[:, lanes] for ref in refs], axis=0)


def turn_waves(wave, turned, segments):
    for pair in range(segments // 2):
        values = wave[:, pair * PAIR : (pair + 1) * PAIR]
        turned[0, pair] = values
        turned[1, pair] = pltpu.roll(values.astype(jnp.float32), TILE, 1).astype(values.dtype)
    for way in range(2):
        turned[way, segments // 2] = jnp.zeros(turned.shape[2:], turned.dtype)


def project_kernel(sizes, n_pieces, spot, first, last, meta, wave, *refs):
    pieces, refs = refs[:n_pieces], refs[n_pieces:]
    turned, refs = refs[-1], refs[:-1]
    proj = pieces[0].shape[2]
    values = pieces[0]
    if n_pieces > 1:
        values, refs = refs[-1], refs[:-1]
        join_pieces(meta, pieces, values, spot[-1])
    total = refs[-1]
    total[...] = jnp.zeros_like(total) if first else refs[0][...]
    every = slice(None)

    def product(lanes, segments, tiles):
        low = lax.broadcasted_iota(jnp.int32, turned.shape[2:], 1) < TILE
        waves = [
            jnp.where(
                low,
                turned[segments[at] & 1, segments[at] >> 1],
                turned[1 - (segments[at + 1] & 1), segments[at + 1] >> 1],
            )
            for at in range(0, GROUP, 2)
        ]
        term = jnp.dot(
            jnp.concatenate(waves, axis=1),
            jnp.concatenate(tiles, axis=0),
            preferred_element_type=jnp.float32,
        )
        return [(total, every, lanes, term)]

    @pl.when(meta[1 + spot[0]] > spot[-1])
    def loop():
        turn_waves(wave, turned, sizes[1])
        group_loop(sizes, meta, values, proj, *spot, product)

    if last:
        outs = refs[1:-1]
        rows = outs[0].shape[0]
        for d, out in enumerate(outs):
            start = 0 if len(outs) == 1 else pl.multiple_of((meta[0] ^ d) * rows, rows)
            out[...] = total[pl.ds(start, rows), :].astype(out.dtype)


def spread_kernel(sizes, n_rows, n_pieces, which, meta, *refs):
    applied, refs = refs[:n_rows], refs[n_rows:]
    pieces, refs = refs[:n_pieces], refs[n_pieces:]
    proj = pieces[0].shape[2]
    values = pieces[0]
    if n_pieces > 1:
        values, refs = refs[-1], refs[:-1]
        join_pieces(meta, pieces, values, 0)
    outs, field = refs[:-1], refs[-1]
    field[...] = jnp.zeros_like(field)
    every = slice(None)

    def product(lanes, segments, tiles):
        terms = lax.dot_general(
            jnp.concatenate(tiles, axis=0),
            rows_of(applied, lanes),
            (((1,), (1,)), ((), ())),
            preferred_element_type=jnp.float32,
        )
        return [
            (
                field,
                pl.ds(pl.multiple_of(at * TILE, TILE), TILE),
                every,
                terms[number * TILE : (number + 1) * TILE],
            )
            for number, at in enumerate(segments)
        ]

    group_loop(sizes, meta, values, proj, which, 0, len(RANGES), 0, product)
    for pair in range(sizes[1] // 2):
        points = slice(pair * PAIR, (pair + 1) * PAIR)
        values, start = field[points, :].T, 0
        for out in outs:
            out[:, points] = values[start : start + out.shape[0]].astype(out.dtype)
            start += out.shape[0]


WHOLE = pl.BlockSpec(memory_space=pltpu.VMEM)


def cost(us):
    return pl.CostEstimate(flops=1 + us * 10**9, bytes_accessed=1, transcendentals=0)


def join_small(blocks):
    return blocks if blocks[0].shape[0] % 16 == 0 else [jnp.concatenate(blocks)]


def split_small(blocks, count):
    return blocks if len(blocks) == count else jnp.split(blocks[0], count)


def joined_shape(pieces):
    if len(pieces) == 1:
        return []
    shape = pieces[0].shape
    return [pltpu.VMEM((len(pieces) * shape[0],) + shape[1:], jnp.bfloat16)]


def project(sizes, meta, wave, pieces, count, width, spot, total=None, last=False, us=0):
    rows = wave.shape[0]
    bands = rows // count
    split = bands % 16 == 0
    operands = [wave, *pieces] + ([] if total is None else [total])
    outs = count if split else 1
    out_shape = [jax.ShapeDtypeStruct((rows // outs, width), jnp.bfloat16)] * outs
    return pl.pallas_call(
        functools.partial(
            project_kernel, sizes, len(pieces), spot, total is None, last
        ),
        grid_spec=pltpu.PrefetchScalarGridSpec(
            num_scalar_prefetch=1,
            grid=(1,),
            in_specs=[WHOLE] * len(operands),
            out_specs=[WHOLE] * outs if last else WHOLE,
            scratch_shapes=([pltpu.VMEM((rows, width), jnp.float32)] if last else [])
            + joined_shape(pieces)
            + [pltpu.VMEM((2, sizes[1] // 2 + 1, rows, PAIR), jnp.bfloat16)],
        ),
        out_shape=out_shape if last else jax.ShapeDtypeStruct((rows, width), jnp.float32),
        compiler_params=pltpu.CompilerParams(vmem_limit_bytes=VMEM_LIMIT),
        cost_estimate=cost(us),
    )(meta, *operands)


def spread(sizes, meta, applied, pieces, points, which):
    count = len(applied)
    applied = join_small(applied)
    rows = sum(block.shape[0] for block in applied)
    result = pl.pallas_call(
        functools.partial(spread_kernel, sizes, len(applied), len(pieces), which),
        grid_spec=pltpu.PrefetchScalarGridSpec(
            num_scalar_prefetch=1,
            grid=(1,),
            in_specs=[WHOLE] * (len(applied) + len(pieces)),
            out_specs=[WHOLE] * len(applied),
            scratch_shapes=[pltpu.VMEM((points + TILE, rows), jnp.float32)] + joined_shape(pieces),
        ),
        out_shape=[
            jax.ShapeDtypeStruct((block.shape[0], points), jnp.bfloat16) for block in applied
        ],
        compiler_params=pltpu.CompilerParams(vmem_limit_bytes=VMEM_LIMIT),
        cost_estimate=cost(0),
    )(meta, *applied, *pieces)
    return split_small(result, count)


def two_parts(values):
    high = values.astype(jnp.bfloat16)
    return high, (values - high.astype(jnp.float32)).astype(jnp.bfloat16)


def couple_kernel(high_ref, low_ref, *refs):
    parts, out_ref = refs[:-1], refs[-1]
    blocks, proj, unused = high_ref.shape
    for block in range(blocks):
        lanes = slice(block * proj, (block + 1) * proj)
        total = parts[0][:, lanes].astype(jnp.float32)
        for part in parts[1:]:
            total += part[:, lanes].astype(jnp.float32)
        high, low = two_parts(total)
        result = jnp.dot(high, high_ref[block], preferred_element_type=jnp.float32)
        result += jnp.dot(high, low_ref[block], preferred_element_type=jnp.float32)
        result += jnp.dot(low, high_ref[block], preferred_element_type=jnp.float32)
        out_ref[:, lanes] = result.astype(out_ref.dtype)


def couple(parts, high, low):
    return pl.pallas_call(
        couple_kernel,
        in_specs=[WHOLE] * (2 + len(parts)),
        out_specs=WHOLE,
        out_shape=jax.ShapeDtypeStruct(parts[0].shape, jnp.bfloat16),
        compiler_params=pltpu.CompilerParams(vmem_limit_bytes=VMEM_LIMIT),
        cost_estimate=cost(0),
    )(high, low, *parts)


def coupling_matrix(coupling):
    blocks, atoms, width, unused = coupling.shape
    proj = atoms * width
    wide = jnp.tile(coupling.reshape(blocks, proj, width), (1, 1, atoms))
    same = jnp.arange(proj)[:, None] // width == jnp.arange(proj)[None, :] // width
    return jnp.where(same[None], wide, 0.0)


def body(n_grid, wavefunctions, tile_segment, tile_block, tile_count, projectors, coupling):
    half = n_grid // 2
    bands, npts = wavefunctions.shape
    points = npts // n_grid
    tiles = projectors.shape[0]
    width = coupling.shape[0] * projectors.shape[2]
    index = lax.axis_index("grid")
    side, place = index // half, index % half
    group, core = lax.axis_index("groups"), lax.axis_index("band")
    partners = [(i, (i + half) % n_grid) for i in range(n_grid)]
    pools = [list(range(half)), list(range(half, n_grid))]
    swap = [(0, 1), (1, 0)]

    def exchange(blocks):
        return [blocks[0]] + [
            lax.ppermute(
                blocks[d], "grid", [(i, i // half * half + (i % half ^ d)) for i in range(n_grid)]
            )
            for d in range(1, half)
        ]

    def to_bricks(which):
        part = lax.dynamic_slice_in_dim(wavefunctions, which * half * points, half * points, 1)
        return lax.all_to_all(
            part, "grid", split_axis=1, concat_axis=0, tiled=True, axis_index_groups=pools
        )

    segments, blocks = points // TILE, coupling.shape[0]
    sizes = (tiles, segments, blocks)
    size = tiles // PARTS
    share = size // 4
    slots = jnp.arange(tiles, dtype=jnp.int32)
    part, quarter = slots // size, slots % size // share
    held = part * size + slots % share
    held += share * ((quarter // 2 ^ group) + 2 * (quarter % 2 ^ core))

    numbers = jnp.stack([tile_segment, tile_block, jnp.broadcast_to(tile_count, (tiles,))])
    others = lax.ppermute(numbers, "grid", partners)
    absent = segments << bits(tiles)
    segment, block = (jnp.stack([numbers[i], others[i]]) for i in (0, 1))
    codes = jnp.stack([slots, held])
    codes += (segment + (block << bits(segments + 1))) << bits(tiles)
    live = slots < jnp.stack([numbers[2], others[2]])
    range_of = sum(jnp.where(part >= first, 1, 0) for first, end in RANGES[1:])
    keys = block + blocks * jnp.stack([0 * part, range_of])
    meta = jnp.concatenate(
        [
            jnp.stack([place, numbers[2, 0], others[2, 0]]),
            group_lists(codes, keys, live, blocks, absent),
        ]
    )

    own_wave = to_bricks(side)
    other_wave = to_bricks(1 - side)
    spot = (OWN, 0, len(RANGES), 0)
    own_total = project(sizes, meta, own_wave, [projectors], half, width, spot, us=10)
    matrix = two_parts(coupling_matrix(coupling))

    pieces, mine, across = [], None, None
    for part in range(PARTS):
        start = part * size + (2 * group + core) * share
        sent = lax.dynamic_slice_in_dim(projectors, start, share, 0)
        if part > 0:
            sent = lax.optimization_barrier((sent, mine))[0]
        mine = lax.ppermute(sent, "grid", partners)
        sent = mine
        if part == 0:
            sent, matrix, meta = lax.optimization_barrier((sent, matrix, meta))
        else:
            sent = lax.optimization_barrier((sent, across))[0]
        across = lax.ppermute(sent, "groups", swap)
        both = jnp.concatenate([mine, across])
        if part == 0:
            both, total = lax.optimization_barrier((both, own_total))
        pieces += [both, lax.ppermute(both, "band", swap)]

    for number, (first, end) in enumerate(RANGES):
        total = project(
            sizes,
            meta,
            other_wave,
            pieces[2 * first : 2 * end],
            half,
            width,
            (OTHER, number, number + 1, first * size),
            total,
            last=end == PARTS,
            us=8 if end < PARTS else 0,
        )
    if len(total) < half:
        total = [lax.dynamic_slice_in_dim(total[0], (place ^ d) * bands, bands, 0) for d in range(half)]

    applied = couple(exchange(total), *matrix)
    applied = exchange([applied] * half)

    result = jnp.zeros((bands, npts), jnp.bfloat16)
    for which, field in (
        (1 - side, spread(sizes, meta, applied, pieces, points, OTHER)),
        (side, spread(sizes, meta, applied, [projectors], points, OWN)),
    ):
        for d, block in enumerate(exchange(field)):
            start = (which * half + (place ^ d)) * points
            result = lax.dynamic_update_slice_in_dim(result, block, start, 1)
    return result


def solution(mesh):
    in_specs = (
        P(("groups", "grid", "band"), None),
        P("grid"),
        P("grid"),
        P("grid"),
        P("grid", None, None),
        P(),
    )
    out_specs = P(("groups", "grid", "band"), None)
    return jax.shard_map(
        functools.partial(body, mesh.shape["grid"]),
        mesh=mesh,
        in_specs=in_specs,
        out_specs=out_specs,
        check_vma=False,
    )
```

```python
import functools

import jax
import jax.numpy as jnp
from jax import lax
from jax.experimental import pallas as pl
from jax.experimental.pallas import tpu as pltpu
from jax.sharding import PartitionSpec as P

TILE = 64
PAIR = 2 * TILE
GROUP = 4
UNROLL = 4
VMEM_LIMIT = 14 * 1024 * 1024
PARTS = (3, 5, 4)
RANGES = ((0, 2), (2, 3))
OWN, OTHER = range(2)
BOUNDS = 3
STEPS = len(RANGES) + 1
LISTS = BOUNDS + 2 * STEPS


def bits(count):
    return max(1, (count - 1).bit_length())


def list_length(tiles, blocks):
    return tiles + len(RANGES) * ((GROUP - 1) * blocks + GROUP * UNROLL)


def group_lists(codes, keys, live, blocks, absent):
    n_lists, tiles = codes.shape
    n_keys = len(RANGES) * blocks
    order = jnp.arange(tiles, dtype=jnp.int32)
    key_range = jnp.arange(n_keys, dtype=jnp.int32)
    ranges = jnp.arange(STEPS, dtype=jnp.int32)
    mine = (keys[:, None, :] == key_range[None, :, None]) & live[:, None, :]
    groups = (jnp.sum(mine, axis=2, dtype=jnp.int32) + GROUP - 1) // GROUP
    in_range = key_range[:, None] // blocks == ranges[None, :]
    totals = jnp.sum(jnp.where(in_range, groups[:, :, None], 0), axis=1, dtype=jnp.int32)
    totals = (totals + UNROLL - 1) // UNROLL * UNROLL
    bounds = jnp.sum(
        jnp.where(ranges[:, None] < ranges[None, :], totals[:, :, None], 0), axis=1, dtype=jnp.int32
    )
    lower = (key_range[:, None] < key_range[None, :]) & (
        key_range[:, None] // blocks == key_range[None, :] // blocks
    )
    starts = jnp.sum(jnp.where(lower, groups[:, :, None], 0), axis=1, dtype=jnp.int32)
    starts += jnp.sum(jnp.where(in_range, bounds[:, None, :], 0), axis=2, dtype=jnp.int32)
    before = (
        (keys[:, :, None] == keys[:, None, :]) & live[:, :, None] & (order[:, None] < order[None, :])
    )
    entry = jnp.sum(before, axis=1, dtype=jnp.int32) + GROUP * jnp.sum(
        jnp.where(mine, starts[:, :, None], 0), axis=1, dtype=jnp.int32
    )
    entry = jnp.where(live, entry, -1)
    found = entry[:, :, None] == jnp.arange(list_length(tiles, blocks), dtype=jnp.int32)
    entries = absent + jnp.sum(
        jnp.where(found, codes[:, :, None] - absent, 0), axis=1, dtype=jnp.int32
    )
    return jnp.concatenate([bounds.reshape(-1), entries.reshape(-1)])


def group_loop(sizes, meta, values, proj, which, first, last, origin, product):
    tiles, segments, blocks = sizes
    begin, end = (meta[BOUNDS + STEPS * which + number] for number in (first, last))
    base = LISTS + which * list_length(tiles, blocks)

    def group(number):
        places = []
        for entry in range(GROUP):
            code = meta[base + GROUP * number + entry]
            index = jnp.maximum((code & ((1 << bits(tiles)) - 1)) - origin, 0)
            code = code >> bits(tiles)
            places.append((code & ((1 << bits(segments + 1)) - 1), values[index]))
            if entry == 0:
                block = code >> bits(segments + 1)
        lanes = pl.ds(pl.multiple_of(block * proj, proj), proj)
        return product(lanes, [at for at, tile in places], [tile for at, tile in places])

    def step(index, carry):
        sums = [group(begin + index * UNROLL + lane) for lane in range(UNROLL)]
        for additions in sums:
            for ref, rows, lanes, term in additions:
                ref[rows, lanes] += term
        return carry

    lax.fori_loop(0, (end - begin) // UNROLL, step, 0)


def join_pieces(meta, pieces, joined, first):
    end = 0
    for number, ref in enumerate(pieces):
        start, end = end, end + ref.shape[0]

        @pl.when(meta[2] > first + (start if number % 2 == 0 else start - ref.shape[0]))
        def copy(start=start, end=end, ref=ref):
            joined[start:end] = ref[...]


def rows_of(refs, lanes):
    return jnp.concatenate([ref[:, lanes] for ref in refs], axis=0)


def turn_waves(wave, turned, segments):
    for pair in range(segments // 2):
        values = wave[:, pair * PAIR : (pair + 1) * PAIR]
        turned[0, pair] = values
        turned[1, pair] = pltpu.roll(values.astype(jnp.float32), TILE, 1).astype(values.dtype)
    for way in range(2):
        turned[way, segments // 2] = jnp.zeros(turned.shape[2:], turned.dtype)


def project_kernel(sizes, n_pieces, spot, first, last, meta, wave, *refs):
    pieces, refs = refs[:n_pieces], refs[n_pieces:]
    turned, refs = refs[-1], refs[:-1]
    proj = pieces[0].shape[2]
    values = pieces[0]
    if n_pieces > 1:
        values, refs = refs[-1], refs[:-1]
        join_pieces(meta, pieces, values, spot[-1])
    total = refs[-1]
    total[...] = jnp.zeros_like(total) if first else refs[0][...]
    every = slice(None)

    def product(lanes, segments, tiles):
        low = lax.broadcasted_iota(jnp.int32, turned.shape[2:], 1) < TILE
        waves = [
            jnp.where(
                low,
                turned[segments[at] & 1, segments[at] >> 1],
                turned[1 - (segments[at + 1] & 1), segments[at + 1] >> 1],
            )
            for at in range(0, GROUP, 2)
        ]
        term = jnp.dot(
            jnp.concatenate(waves, axis=1),
            jnp.concatenate(tiles, axis=0),
            preferred_element_type=jnp.float32,
        )
        return [(total, every, lanes, term)]

    @pl.when(meta[1 + spot[0]] > spot[-1])
    def loop():
        turn_waves(wave, turned, sizes[1])
        group_loop(sizes, meta, values, proj, *spot, product)

    if last:
        outs = refs[1:-1]
        rows = outs[0].shape[0]
        for d, out in enumerate(outs):
            start = 0 if len(outs) == 1 else pl.multiple_of((meta[0] ^ d) * rows, rows)
            out[...] = total[pl.ds(start, rows), :].astype(out.dtype)


def spread_kernel(sizes, n_rows, n_pieces, which, meta, *refs):
    applied, refs = refs[:n_rows], refs[n_rows:]
    pieces, refs = refs[:n_pieces], refs[n_pieces:]
    proj = pieces[0].shape[2]
    values = pieces[0]
    if n_pieces > 1:
        values, refs = refs[-1], refs[:-1]
        join_pieces(meta, pieces, values, 0)
    outs, field = refs[:-1], refs[-1]
    field[...] = jnp.zeros_like(field)
    every = slice(None)

    def product(lanes, segments, tiles):
        terms = lax.dot_general(
            jnp.concatenate(tiles, axis=0),
            rows_of(applied, lanes),
            (((1,), (1,)), ((), ())),
            preferred_element_type=jnp.float32,
        )
        return [
            (
                field,
                pl.ds(pl.multiple_of(at * TILE, TILE), TILE),
                every,
                terms[number * TILE : (number + 1) * TILE],
            )
            for number, at in enumerate(segments)
        ]

    group_loop(sizes, meta, values, proj, which, 0, len(RANGES), 0, product)
    for pair in range(sizes[1] // 2):
        points = slice(pair * PAIR, (pair + 1) * PAIR)
        values, start = field[points, :].T, 0
        for out in outs:
            out[:, points] = values[start : start + out.shape[0]].astype(out.dtype)
            start += out.shape[0]


WHOLE = pl.BlockSpec(memory_space=pltpu.VMEM)


def cost(us):
    return pl.CostEstimate(flops=1 + us * 10**9, bytes_accessed=1, transcendentals=0)


def join_small(blocks):
    return blocks if blocks[0].shape[0] % 16 == 0 else [jnp.concatenate(blocks)]


def split_small(blocks, count):
    return blocks if len(blocks) == count else jnp.split(blocks[0], count)


def joined_shape(pieces):
    if len(pieces) == 1:
        return []
    count = sum(piece.shape[0] for piece in pieces)
    return [pltpu.VMEM((count,) + pieces[0].shape[1:], jnp.bfloat16)]


def project(sizes, meta, wave, pieces, count, width, spot, total=None, last=False, us=0):
    rows = wave.shape[0]
    bands = rows // count
    split = bands % 16 == 0
    operands = [wave, *pieces] + ([] if total is None else [total])
    outs = count if split else 1
    out_shape = [jax.ShapeDtypeStruct((rows // outs, width), jnp.bfloat16)] * outs
    return pl.pallas_call(
        functools.partial(
            project_kernel, sizes, len(pieces), spot, total is None, last
        ),
        grid_spec=pltpu.PrefetchScalarGridSpec(
            num_scalar_prefetch=1,
            grid=(1,),
            in_specs=[WHOLE] * len(operands),
            out_specs=[WHOLE] * outs if last else WHOLE,
            scratch_shapes=([pltpu.VMEM((rows, width), jnp.float32)] if last else [])
            + joined_shape(pieces)
            + [pltpu.VMEM((2, sizes[1] // 2 + 1, rows, PAIR), jnp.bfloat16)],
        ),
        out_shape=out_shape if last else jax.ShapeDtypeStruct((rows, width), jnp.float32),
        compiler_params=pltpu.CompilerParams(vmem_limit_bytes=VMEM_LIMIT),
        cost_estimate=cost(us),
    )(meta, *operands)


def spread(sizes, meta, applied, pieces, points, which):
    count = len(applied)
    applied = join_small(applied)
    rows = sum(block.shape[0] for block in applied)
    result = pl.pallas_call(
        functools.partial(spread_kernel, sizes, len(applied), len(pieces), which),
        grid_spec=pltpu.PrefetchScalarGridSpec(
            num_scalar_prefetch=1,
            grid=(1,),
            in_specs=[WHOLE] * (len(applied) + len(pieces)),
            out_specs=[WHOLE] * len(applied),
            scratch_shapes=[pltpu.VMEM((points + TILE, rows), jnp.float32)] + joined_shape(pieces),
        ),
        out_shape=[
            jax.ShapeDtypeStruct((block.shape[0], points), jnp.bfloat16) for block in applied
        ],
        compiler_params=pltpu.CompilerParams(vmem_limit_bytes=VMEM_LIMIT),
        cost_estimate=cost(0),
    )(meta, *applied, *pieces)
    return split_small(result, count)


def two_parts(values):
    high = values.astype(jnp.bfloat16)
    return high, (values - high.astype(jnp.float32)).astype(jnp.bfloat16)


def couple_kernel(high_ref, low_ref, *refs):
    parts, out_ref = refs[:-1], refs[-1]
    blocks, proj, unused = high_ref.shape
    for block in range(blocks):
        lanes = slice(block * proj, (block + 1) * proj)
        total = parts[0][:, lanes].astype(jnp.float32)
        for part in parts[1:]:
            total += part[:, lanes].astype(jnp.float32)
        high, low = two_parts(total)
        result = jnp.dot(high, high_ref[block], preferred_element_type=jnp.float32)
        result += jnp.dot(high, low_ref[block], preferred_element_type=jnp.float32)
        result += jnp.dot(low, high_ref[block], preferred_element_type=jnp.float32)
        out_ref[:, lanes] = result.astype(out_ref.dtype)


def couple(parts, high, low):
    return pl.pallas_call(
        couple_kernel,
        in_specs=[WHOLE] * (2 + len(parts)),
        out_specs=WHOLE,
        out_shape=jax.ShapeDtypeStruct(parts[0].shape, jnp.bfloat16),
        compiler_params=pltpu.CompilerParams(vmem_limit_bytes=VMEM_LIMIT),
        cost_estimate=cost(0),
    )(high, low, *parts)


def coupling_matrix(coupling):
    blocks, atoms, width, unused = coupling.shape
    proj = atoms * width
    wide = jnp.tile(coupling.reshape(blocks, proj, width), (1, 1, atoms))
    same = jnp.arange(proj)[:, None] // width == jnp.arange(proj)[None, :] // width
    return jnp.where(same[None], wide, 0.0)


def body(n_grid, wavefunctions, tile_segment, tile_block, tile_count, projectors, coupling):
    half = n_grid // 2
    bands, npts = wavefunctions.shape
    points = npts // n_grid
    tiles = projectors.shape[0]
    width = coupling.shape[0] * projectors.shape[2]
    index = lax.axis_index("grid")
    side, place = index // half, index % half
    group, core = lax.axis_index("groups"), lax.axis_index("band")
    partners = [(i, (i + half) % n_grid) for i in range(n_grid)]
    pools = [list(range(half)), list(range(half, n_grid))]
    swap = [(0, 1), (1, 0)]

    def exchange(blocks):
        return [blocks[0]] + [
            lax.ppermute(
                blocks[d], "grid", [(i, i // half * half + (i % half ^ d)) for i in range(n_grid)]
            )
            for d in range(1, half)
        ]

    def to_bricks(which):
        part = lax.dynamic_slice_in_dim(wavefunctions, which * half * points, half * points, 1)
        return lax.all_to_all(
            part, "grid", split_axis=1, concat_axis=0, tiled=True, axis_index_groups=pools
        )

    segments, blocks = points // TILE, coupling.shape[0]
    sizes = (tiles, segments, blocks)
    slots = jnp.arange(tiles, dtype=jnp.int32)
    starts = [tiles * sum(PARTS[:number]) // sum(PARTS) for number in range(len(PARTS) + 1)]
    held, range_of = slots, 0
    for start, end in zip(starts, starts[1:]):
        share = (end - start) // 4
        quarter, rest = (slots - start) // share, (slots - start) % share
        at = start + rest + share * ((quarter // 2 ^ group) + 2 * (quarter % 2 ^ core))
        held = jnp.where((slots >= start) & (slots < end), at, held)
    for first, end in RANGES[1:]:
        range_of += jnp.where(slots >= starts[first], 1, 0)

    numbers = jnp.stack([tile_segment, tile_block, jnp.broadcast_to(tile_count, (tiles,))])
    others = lax.ppermute(numbers, "grid", partners)
    absent = segments << bits(tiles)
    segment, block = (jnp.stack([numbers[i], others[i]]) for i in (0, 1))
    codes = jnp.stack([slots, held])
    codes += (segment + (block << bits(segments + 1))) << bits(tiles)
    live = slots < jnp.stack([numbers[2], others[2]])
    keys = block + blocks * jnp.stack([jnp.zeros_like(slots), range_of])
    meta = jnp.concatenate(
        [
            jnp.stack([place, numbers[2, 0], others[2, 0]]),
            group_lists(codes, keys, live, blocks, absent),
        ]
    )

    own_wave = to_bricks(side)
    other_wave = to_bricks(1 - side)
    matrix = two_parts(coupling_matrix(coupling))

    arrived, pieces, across = [], [], None
    source = projectors
    for number, (start, end) in enumerate(zip(starts, starts[1:])):
        share = (end - start) // 4
        start += (2 * group + core) * share
        sent = lax.dynamic_slice_in_dim(source, start, share, 0)
        if number == 0:
            sent, source = lax.optimization_barrier((sent, source))
        if number > 1:
            sent = lax.optimization_barrier((sent, arrived[number - 2]))[0]
        arrived.append(lax.ppermute(sent, "grid", partners))
    own_wave, late = lax.optimization_barrier((own_wave, arrived[-1]))
    spot = (OWN, 0, len(RANGES), 0)
    total = project(sizes, meta, own_wave, [projectors], half, width, spot, us=10)
    for number, mine in enumerate(arrived):
        sent = mine
        if number == 1:
            sent, across, matrix, meta = lax.optimization_barrier((sent, across, matrix, meta))
        if number > 1:
            sent, across = lax.optimization_barrier((sent, across))
        across = lax.ppermute(sent, "groups", swap)
        both = jnp.concatenate([mine, across])
        pieces += [both, lax.ppermute(both, "band", swap)]

    for number, (first, end) in enumerate(RANGES):
        total = project(
            sizes,
            meta,
            other_wave,
            pieces[2 * first : 2 * end],
            half,
            width,
            (OTHER, number, number + 1, starts[first]),
            total,
            last=end == len(PARTS),
            us=8 if end < len(PARTS) else 0,
        )
    if len(total) < half:
        total = [lax.dynamic_slice_in_dim(total[0], (place ^ d) * bands, bands, 0) for d in range(half)]

    applied = couple(exchange(total), *matrix)
    applied = exchange([applied] * half)

    result = jnp.zeros((bands, npts), jnp.bfloat16)
    for which, field in (
        (1 - side, spread(sizes, meta, applied, pieces, points, OTHER)),
        (side, spread(sizes, meta, applied, [projectors], points, OWN)),
    ):
        for d, block in enumerate(exchange(field)):
            start = (which * half + (place ^ d)) * points
            result = lax.dynamic_update_slice_in_dim(result, block, start, 1)
    return result


def solution(mesh):
    in_specs = (
        P(("groups", "grid", "band"), None),
        P("grid"),
        P("grid"),
        P("grid"),
        P("grid", None, None),
        P(),
    )
    out_specs = P(("groups", "grid", "band"), None)
    return jax.shard_map(
        functools.partial(body, mesh.shape["grid"]),
        mesh=mesh,
        in_specs=in_specs,
        out_specs=out_specs,
        check_vma=False,
    )
```

```python
import functools
import math

import jax
import jax.numpy as jnp
from jax import lax
from jax.experimental import pallas as pl
from jax.experimental.pallas import tpu as pltpu
from jax.sharding import PartitionSpec as P

TILE = 64
PAIR = 2 * TILE
GROUP = 4
UNROLL = 4
VMEM_SLACK = 10 * 1024 * 1024
PARTS = (15, 17, 16)
RANGES = ((0, 2), (2, 3))
OWN, OTHER = range(2)
BOUNDS = 3
STEPS = len(RANGES) + 1
LISTS = BOUNDS + 2 * STEPS


def bits(count):
    return max(1, (count - 1).bit_length())


def list_length(tiles, blocks):
    return tiles + len(RANGES) * ((GROUP - 1) * blocks + GROUP * UNROLL)


def group_lists(codes, keys, live, blocks, absent):
    n_lists, tiles = codes.shape
    n_keys = len(RANGES) * blocks
    order = jnp.arange(tiles, dtype=jnp.int32)
    key_range = jnp.arange(n_keys, dtype=jnp.int32)
    ranges = jnp.arange(STEPS, dtype=jnp.int32)
    mine = (keys[:, None, :] == key_range[None, :, None]) & live[:, None, :]
    groups = (jnp.sum(mine, axis=2, dtype=jnp.int32) + GROUP - 1) // GROUP
    in_range = key_range[:, None] // blocks == ranges[None, :]
    totals = jnp.sum(jnp.where(in_range, groups[:, :, None], 0), axis=1, dtype=jnp.int32)
    totals = (totals + UNROLL - 1) // UNROLL * UNROLL
    bounds = jnp.sum(
        jnp.where(ranges[:, None] < ranges[None, :], totals[:, :, None], 0), axis=1, dtype=jnp.int32
    )
    lower = (key_range[:, None] < key_range[None, :]) & (
        key_range[:, None] // blocks == key_range[None, :] // blocks
    )
    starts = jnp.sum(jnp.where(lower, groups[:, :, None], 0), axis=1, dtype=jnp.int32)
    starts += jnp.sum(jnp.where(in_range, bounds[:, None, :], 0), axis=2, dtype=jnp.int32)
    before = (
        (keys[:, :, None] == keys[:, None, :]) & live[:, :, None] & (order[:, None] < order[None, :])
    )
    entry = jnp.sum(before, axis=1, dtype=jnp.int32) + GROUP * jnp.sum(
        jnp.where(mine, starts[:, :, None], 0), axis=1, dtype=jnp.int32
    )
    entry = jnp.where(live, entry, -1)
    found = entry[:, :, None] == jnp.arange(list_length(tiles, blocks), dtype=jnp.int32)
    entries = absent + jnp.sum(
        jnp.where(found, codes[:, :, None] - absent, 0), axis=1, dtype=jnp.int32
    )
    return jnp.concatenate([bounds.reshape(-1), entries.reshape(-1)])


def group_loop(sizes, meta, values, proj, which, first, last, origin, product):
    tiles, segments, blocks = sizes
    begin, end = (meta[BOUNDS + STEPS * which + number] for number in (first, last))
    base = LISTS + which * list_length(tiles, blocks)

    def group(number):
        places = []
        for entry in range(GROUP):
            code = meta[base + GROUP * number + entry]
            index = jnp.maximum((code & ((1 << bits(tiles)) - 1)) - origin, 0)
            code = code >> bits(tiles)
            places.append((code & ((1 << bits(segments + 1)) - 1), values[index]))
            if entry == 0:
                block = code >> bits(segments + 1)
        lanes = pl.ds(pl.multiple_of(block * proj, proj), proj)
        return product(lanes, [at for at, tile in places], [tile for at, tile in places])

    def step(index, carry):
        sums = [group(begin + index * UNROLL + lane) for lane in range(UNROLL)]
        for additions in sums:
            for ref, rows, lanes, term in additions:
                ref[rows, lanes] += term
        return carry

    lax.fori_loop(0, (end - begin) // UNROLL, step, 0)


def join_pieces(meta, pieces, joined, first):
    end = 0
    for number, ref in enumerate(pieces):
        start, end = end, end + ref.shape[0]

        @pl.when(meta[2] > first + start - number % 4 * ref.shape[0])
        def copy(start=start, end=end, ref=ref):
            joined[start:end] = ref[...]


def rows_of(refs, lanes):
    return jnp.concatenate([ref[:, lanes] for ref in refs], axis=0)


def turn_waves(wave, turned, segments):
    for pair in range(segments // 2):
        values = wave[:, pair * PAIR : (pair + 1) * PAIR]
        turned[0, pair] = values
        turned[1, pair] = pltpu.roll(values.astype(jnp.float32), TILE, 1).astype(values.dtype)
    for way in range(2):
        turned[way, segments // 2] = jnp.zeros(turned.shape[2:], turned.dtype)


def project_kernel(sizes, n_pieces, spot, first, last, meta, wave, *refs):
    pieces, refs = refs[:n_pieces], refs[n_pieces:]
    turned, refs = refs[-1], refs[:-1]
    if not first:
        before, refs = refs[0], refs[1:]
    values = pieces[0]
    if n_pieces > 1:
        values, refs = refs[0], refs[1:]
        join_pieces(meta, pieces, values, spot[-1])
    total = refs[-1]
    total[...] = jnp.zeros_like(total) if first else before[...]
    every = slice(None)

    def product(lanes, segments, tiles):
        low = lax.broadcasted_iota(jnp.int32, turned.shape[2:], 1) < TILE
        waves = [
            jnp.where(
                low,
                turned[segments[at] & 1, segments[at] >> 1],
                turned[1 - (segments[at + 1] & 1), segments[at + 1] >> 1],
            )
            for at in range(0, GROUP, 2)
        ]
        term = jnp.dot(
            jnp.concatenate(waves, axis=1),
            jnp.concatenate(tiles, axis=0),
            preferred_element_type=jnp.float32,
        )
        return [(total, every, lanes, term)]

    @pl.when(meta[1 + spot[0]] > spot[-1])
    def loop():
        turn_waves(wave, turned, sizes[1])
        group_loop(sizes, meta, values, values.shape[2], *spot, product)

    if last:
        outs = refs[:-1]
        rows = outs[0].shape[0]
        for d, out in enumerate(outs):
            start = 0 if len(outs) == 1 else pl.multiple_of((meta[0] ^ d) * rows, rows)
            out[...] = total[pl.ds(start, rows), :].astype(out.dtype)


def spread_kernel(sizes, n_rows, spots, meta, *refs):
    applied, refs = refs[:n_rows], refs[n_rows:]
    lists, refs = refs[: len(spots)], refs[len(spots) :]
    outs, field = refs[:-1], refs[-1]
    field[...] = jnp.zeros_like(field)
    every = slice(None)

    def product(lanes, segments, tiles):
        terms = lax.dot_general(
            jnp.concatenate(tiles, axis=0),
            rows_of(applied, lanes),
            (((1,), (1,)), ((), ())),
            preferred_element_type=jnp.float32,
        )
        return [
            (
                field,
                pl.ds(pl.multiple_of(at * TILE, TILE), TILE),
                every,
                terms[number * TILE : (number + 1) * TILE],
            )
            for number, at in enumerate(segments)
        ]

    for values, spot in zip(lists, spots):
        group_loop(sizes, meta, values, values.shape[2], *spot, product)
    for pair in range(sizes[1] // 2):
        points = slice(pair * PAIR, (pair + 1) * PAIR)
        values, start = field[points, :].T, 0
        for out in outs:
            out[:, points] = values[start : start + out.shape[0]].astype(out.dtype)
            start += out.shape[0]


WHOLE = pl.BlockSpec(memory_space=pltpu.VMEM)


def cost(us):
    return pl.CostEstimate(flops=1 + us * 10**9, bytes_accessed=1, transcendentals=0)


def join_small(blocks):
    return blocks if blocks[0].shape[0] % 16 == 0 else [jnp.concatenate(blocks)]


def split_small(blocks, count):
    return blocks if len(blocks) == count else jnp.split(blocks[0], count)


def vmem(scratch):
    size = sum(math.prod(ref.shape) * jnp.dtype(ref.dtype).itemsize for ref in scratch)
    return pltpu.CompilerParams(vmem_limit_bytes=size + VMEM_SLACK)


def project(sizes, meta, wave, pieces, count, width, spot, total=None, last=False, us=0):
    rows = wave.shape[0]
    operands = [wave, *pieces] + ([] if total is None else [total])
    shapes = []
    if len(pieces) > 1:
        held = sum(piece.shape[0] for piece in pieces)
        shapes.append(jax.ShapeDtypeStruct((held,) + pieces[0].shape[1:], jnp.bfloat16))
    scratch = [pltpu.VMEM((2, sizes[1] // 2 + 1, rows, PAIR), jnp.bfloat16)]
    if last:
        outs = count if rows // count % 16 == 0 else 1
        shapes += [jax.ShapeDtypeStruct((rows // outs, width), jnp.bfloat16)] * outs
        scratch = [pltpu.VMEM((rows, width), jnp.float32)] + scratch
    else:
        shapes.append(jax.ShapeDtypeStruct((rows, width), jnp.float32))
    result = pl.pallas_call(
        functools.partial(project_kernel, sizes, len(pieces), spot, total is None, last),
        grid_spec=pltpu.PrefetchScalarGridSpec(
            num_scalar_prefetch=1,
            grid=(1,),
            in_specs=[WHOLE] * len(operands),
            out_specs=[WHOLE] * len(shapes),
            scratch_shapes=scratch,
        ),
        out_shape=shapes,
        compiler_params=vmem(scratch),
        cost_estimate=cost(us),
    )(meta, *operands)
    joined, result = (result[0], result[1:]) if len(pieces) > 1 else (pieces[0], result)
    return (list(result) if last else result[0]), joined


def spread(sizes, meta, applied, lists, points, spots):
    count = len(applied)
    applied = join_small(applied)
    rows = sum(block.shape[0] for block in applied)
    scratch = [pltpu.VMEM((points + TILE, rows), jnp.float32)]
    result = pl.pallas_call(
        functools.partial(spread_kernel, sizes, len(applied), spots),
        grid_spec=pltpu.PrefetchScalarGridSpec(
            num_scalar_prefetch=1,
            grid=(1,),
            in_specs=[WHOLE] * (len(applied) + len(lists)),
            out_specs=[WHOLE] * len(applied),
            scratch_shapes=scratch,
        ),
        out_shape=[
            jax.ShapeDtypeStruct((block.shape[0], points), jnp.bfloat16) for block in applied
        ],
        compiler_params=vmem(scratch),
        cost_estimate=cost(0),
    )(meta, *applied, *lists)
    return split_small(result, count)


def two_parts(values):
    high = values.astype(jnp.bfloat16)
    return high, (values - high.astype(jnp.float32)).astype(jnp.bfloat16)


def couple_kernel(high_ref, low_ref, *refs):
    parts, out_ref = refs[:-1], refs[-1]
    blocks, proj, unused = high_ref.shape
    for block in range(blocks):
        lanes = slice(block * proj, (block + 1) * proj)
        total = parts[0][:, lanes].astype(jnp.float32)
        for part in parts[1:]:
            total += part[:, lanes].astype(jnp.float32)
        high, low = two_parts(total)
        result = jnp.dot(high, high_ref[block], preferred_element_type=jnp.float32)
        result += jnp.dot(high, low_ref[block], preferred_element_type=jnp.float32)
        result += jnp.dot(low, high_ref[block], preferred_element_type=jnp.float32)
        out_ref[:, lanes] = result.astype(out_ref.dtype)


def couple(parts, high, low):
    return pl.pallas_call(
        couple_kernel,
        in_specs=[WHOLE] * (2 + len(parts)),
        out_specs=WHOLE,
        out_shape=jax.ShapeDtypeStruct(parts[0].shape, jnp.bfloat16),
        compiler_params=vmem([]),
        cost_estimate=cost(0),
    )(high, low, *parts)


def coupling_matrix(coupling):
    blocks, atoms, width, unused = coupling.shape
    proj = atoms * width
    wide = jnp.tile(coupling.reshape(blocks, proj, width), (1, 1, atoms))
    same = jnp.arange(proj)[:, None] // width == jnp.arange(proj)[None, :] // width
    return jnp.where(same[None], wide, 0.0)


def body(n_grid, wavefunctions, tile_segment, tile_block, tile_count, projectors, coupling):
    half = n_grid // 2
    bands, npts = wavefunctions.shape
    points = npts // n_grid
    tiles = projectors.shape[0]
    width = coupling.shape[0] * projectors.shape[2]
    index = lax.axis_index("grid")
    side, place = index // half, index % half
    group, core = lax.axis_index("groups"), lax.axis_index("band")
    partners = [(i, (i + half) % n_grid) for i in range(n_grid)]
    pools = [list(range(half)), list(range(half, n_grid))]
    swap = [(0, 1), (1, 0)]

    def exchange(blocks):
        return [blocks[0]] + [
            lax.ppermute(
                blocks[d], "grid", [(i, i // half * half + (i % half ^ d)) for i in range(n_grid)]
            )
            for d in range(1, half)
        ]

    def to_bricks(which):
        part = lax.dynamic_slice_in_dim(wavefunctions, which * half * points, half * points, 1)
        return lax.all_to_all(
            part, "grid", split_axis=1, concat_axis=0, tiled=True, axis_index_groups=pools
        )

    segments, blocks = points // TILE, coupling.shape[0]
    sizes = (tiles, segments, blocks)
    slots = jnp.arange(tiles, dtype=jnp.int32)
    starts = [tiles * sum(PARTS[:number]) // sum(PARTS) for number in range(len(PARTS) + 1)]
    held, range_of = slots, 0
    for start, end in zip(starts, starts[1:]):
        share = (end - start) // 4
        quarter, rest = (slots - start) // share, (slots - start) % share
        at = start + rest + share * ((quarter // 2 ^ group) + 2 * (quarter % 2 ^ core))
        held = jnp.where((slots >= start) & (slots < end), at, held)
    for first, end in RANGES[1:]:
        range_of += jnp.where(slots >= starts[first], 1, 0)

    own_wave = to_bricks(side)
    other_wave = to_bricks(1 - side)
    matrix = two_parts(coupling_matrix(coupling))

    arrived, pieces, across = [], [], None
    source = projectors
    for number, (start, end) in enumerate(zip(starts, starts[1:])):
        share = (end - start) // 4
        start += (2 * group + core) * share
        sent = lax.dynamic_slice_in_dim(source, start, share, 0)
        if number == 0:
            sent, source = lax.optimization_barrier((sent, source))
        if number > 0:
            sent = lax.optimization_barrier((sent, arrived[0]))[0]
        arrived.append(lax.ppermute(sent, "grid", partners))

    numbers = jnp.stack([tile_segment, tile_block, jnp.broadcast_to(tile_count, (tiles,))])
    numbers = lax.optimization_barrier((numbers, arrived[0]))[0]
    others = lax.ppermute(numbers, "grid", partners)
    absent = segments << bits(tiles)
    segment, block = (jnp.stack([numbers[i], others[i]]) for i in (0, 1))
    codes = jnp.stack([slots, held])
    codes += (segment + (block << bits(segments + 1))) << bits(tiles)
    live = slots < jnp.stack([numbers[2], others[2]])
    keys = block + blocks * jnp.stack([jnp.zeros_like(slots), range_of])
    meta = jnp.concatenate(
        [
            jnp.stack([place, numbers[2, 0], others[2, 0]]),
            group_lists(codes, keys, live, blocks, absent),
        ]
    )

    own_wave = lax.optimization_barrier((own_wave, arrived[-1]))[0]
    own_spot = (OWN, 0, len(RANGES), 0)
    total, own_tiles = project(
        sizes, meta, own_wave, [projectors], half, width, own_spot, us=10
    )
    for number, mine in enumerate(arrived):
        sent = mine
        if number == 1:
            sent, across, matrix = lax.optimization_barrier((sent, across, matrix))
        if number == 2:
            sent, across, other_wave = lax.optimization_barrier((sent, across, other_wave))
        across = lax.ppermute(sent, "groups", swap)
        pieces += [mine, across]
        pieces += [lax.ppermute(mine, "band", swap), lax.ppermute(across, "band", swap)]

    joined, other_spots = [], []
    for number, (first, end) in enumerate(RANGES):
        other_spots.append((OTHER, number, number + 1, starts[first]))
        last = end == len(PARTS)
        total, tiles_held = project(
            sizes,
            meta,
            other_wave,
            pieces[4 * first : 4 * end],
            half,
            width,
            other_spots[-1],
            total,
            last=last,
            us=0 if last else 8,
        )
        joined.append(tiles_held)
    if len(total) < half:
        total = [lax.dynamic_slice_in_dim(total[0], (place ^ d) * bands, bands, 0) for d in range(half)]

    applied = couple(exchange(total), *matrix)
    applied = exchange([applied] * half)

    result = jnp.zeros((bands, npts), jnp.bfloat16)
    for which, field in (
        (1 - side, spread(sizes, meta, applied, joined, points, other_spots)),
        (side, spread(sizes, meta, applied, [own_tiles], points, [own_spot])),
    ):
        for d, block in enumerate(exchange(field)):
            start = (which * half + (place ^ d)) * points
            result = lax.dynamic_update_slice_in_dim(result, block, start, 1)
    return result


def solution(mesh):
    in_specs = (
        P(("groups", "grid", "band"), None),
        P("grid"),
        P("grid"),
        P("grid"),
        P("grid", None, None),
        P(),
    )
    out_specs = P(("groups", "grid", "band"), None)
    return jax.shard_map(
        functools.partial(body, mesh.shape["grid"]),
        mesh=mesh,
        in_specs=in_specs,
        out_specs=out_specs,
        check_vma=False,
    )
```

```python
import functools
import math

import jax
import jax.numpy as jnp
from jax import lax
from jax.experimental import pallas as pl
from jax.experimental.pallas import tpu as pltpu
from jax.sharding import PartitionSpec as P

TILE = 64
PAIR = 2 * TILE
GROUP = 4
UNROLL = 4
VMEM_SLACK = 10 * 1024 * 1024
PARTS = (1, 1, 2)
ORDER = (0, 2, 1)
RANGES = ((0, 2), (2, 3))
OWN, OTHER = range(2)
BOUNDS = 3
STEPS = len(RANGES) + 1
LISTS = BOUNDS + 2 * STEPS


def bits(count):
    return max(1, (count - 1).bit_length())


def list_length(tiles, blocks):
    return tiles + len(RANGES) * ((GROUP - 1) * blocks + GROUP * UNROLL)


def group_lists(codes, keys, live, blocks, absent):
    n_lists, tiles = codes.shape
    n_keys = len(RANGES) * blocks
    order = jnp.arange(tiles, dtype=jnp.int32)
    key_range = jnp.arange(n_keys, dtype=jnp.int32)
    ranges = jnp.arange(STEPS, dtype=jnp.int32)
    mine = (keys[:, None, :] == key_range[None, :, None]) & live[:, None, :]
    groups = (jnp.sum(mine, axis=2, dtype=jnp.int32) + GROUP - 1) // GROUP
    in_range = key_range[:, None] // blocks == ranges[None, :]
    totals = jnp.sum(jnp.where(in_range, groups[:, :, None], 0), axis=1, dtype=jnp.int32)
    totals = (totals + UNROLL - 1) // UNROLL * UNROLL
    bounds = jnp.sum(
        jnp.where(ranges[:, None] < ranges[None, :], totals[:, :, None], 0), axis=1, dtype=jnp.int32
    )
    lower = (key_range[:, None] < key_range[None, :]) & (
        key_range[:, None] // blocks == key_range[None, :] // blocks
    )
    starts = jnp.sum(jnp.where(lower, groups[:, :, None], 0), axis=1, dtype=jnp.int32)
    starts += jnp.sum(jnp.where(in_range, bounds[:, None, :], 0), axis=2, dtype=jnp.int32)
    before = (
        (keys[:, :, None] == keys[:, None, :]) & live[:, :, None] & (order[:, None] < order[None, :])
    )
    entry = jnp.sum(before, axis=1, dtype=jnp.int32) + GROUP * jnp.sum(
        jnp.where(mine, starts[:, :, None], 0), axis=1, dtype=jnp.int32
    )
    entry = jnp.where(live, entry, -1)
    found = entry[:, :, None] == jnp.arange(list_length(tiles, blocks), dtype=jnp.int32)
    entries = absent + jnp.sum(
        jnp.where(found, codes[:, :, None] - absent, 0), axis=1, dtype=jnp.int32
    )
    return jnp.concatenate([bounds.reshape(-1), entries.reshape(-1)])


def group_loop(sizes, meta, values, proj, which, first, last, origin, product):
    tiles, segments, blocks = sizes
    begin, end = (meta[BOUNDS + STEPS * which + number] for number in (first, last))
    base = LISTS + which * list_length(tiles, blocks)

    def group(number):
        places = []
        for entry in range(GROUP):
            code = meta[base + GROUP * number + entry]
            index = jnp.maximum((code & ((1 << bits(tiles)) - 1)) - origin, 0)
            code = code >> bits(tiles)
            places.append((code & ((1 << bits(segments + 1)) - 1), values[index]))
            if entry == 0:
                block = code >> bits(segments + 1)
        lanes = pl.ds(pl.multiple_of(block * proj, proj), proj)
        return product(lanes, [at for at, tile in places], [tile for at, tile in places])

    def step(index, carry):
        sums = [group(begin + index * UNROLL + lane) for lane in range(UNROLL)]
        for additions in sums:
            for ref, rows, lanes, term in additions:
                ref[rows, lanes] += term
        return carry

    lax.fori_loop(0, (end - begin) // UNROLL, step, 0)


def join_pieces(meta, pieces, joined, firsts):
    end = 0
    for first, ref in zip(firsts, pieces):
        start, end = end, end + ref.shape[0]

        @pl.when(meta[2] > first)
        def copy(start=start, end=end, ref=ref):
            joined[start:end] = ref[...]


def rows_of(refs, lanes):
    return jnp.concatenate([ref[:, lanes] for ref in refs], axis=0)


def turn_waves(wave, turned, segments):
    for pair in range(segments // 2):
        values = wave[:, pair * PAIR : (pair + 1) * PAIR]
        turned[0, pair] = values
        turned[1, pair] = pltpu.roll(values.astype(jnp.float32), TILE, 1).astype(values.dtype)
    for way in range(2):
        turned[way, segments // 2] = jnp.zeros(turned.shape[2:], turned.dtype)


def project_kernel(sizes, firsts, spot, first, last, meta, wave, *refs):
    n_pieces = max(1, len(firsts))
    pieces, refs = refs[:n_pieces], refs[n_pieces:]
    turned, refs = refs[-1], refs[:-1]
    if not first:
        before, refs = refs[0], refs[1:]
    values = pieces[0]
    if n_pieces > 1:
        values, refs = refs[0], refs[1:]
        join_pieces(meta, pieces, values, firsts)
    total = refs[-1]
    total[...] = jnp.zeros_like(total) if first else before[...]
    every = slice(None)

    def product(lanes, segments, tiles):
        low = lax.broadcasted_iota(jnp.int32, turned.shape[2:], 1) < TILE
        waves = [
            jnp.where(
                low,
                turned[segments[at] & 1, segments[at] >> 1],
                turned[1 - (segments[at + 1] & 1), segments[at + 1] >> 1],
            )
            for at in range(0, GROUP, 2)
        ]
        term = jnp.dot(
            jnp.concatenate(waves, axis=1),
            jnp.concatenate(tiles, axis=0),
            preferred_element_type=jnp.float32,
        )
        return [(total, every, lanes, term)]

    begin, end = (meta[BOUNDS + STEPS * spot[0] + number] for number in spot[1:3])

    @pl.when(end > begin)
    def loop():
        turn_waves(wave, turned, sizes[1])
        group_loop(sizes, meta, values, values.shape[2], *spot, product)

    if last:
        outs = refs[:-1]
        rows = outs[0].shape[0]
        for d, out in enumerate(outs):
            start = 0 if len(outs) == 1 else pl.multiple_of((meta[0] ^ d) * rows, rows)
            out[...] = total[pl.ds(start, rows), :].astype(out.dtype)


def spread_kernel(sizes, n_rows, spots, meta, *refs):
    applied, refs = refs[:n_rows], refs[n_rows:]
    lists, refs = refs[: len(spots)], refs[len(spots) :]
    outs, field = refs[:-1], refs[-1]
    field[...] = jnp.zeros_like(field)
    every = slice(None)

    def product(lanes, segments, tiles):
        terms = lax.dot_general(
            jnp.concatenate(tiles, axis=0),
            rows_of(applied, lanes),
            (((1,), (1,)), ((), ())),
            preferred_element_type=jnp.float32,
        )
        return [
            (
                field,
                pl.ds(pl.multiple_of(at * TILE, TILE), TILE),
                every,
                terms[number * TILE : (number + 1) * TILE],
            )
            for number, at in enumerate(segments)
        ]

    for values, spot in zip(lists, spots):
        group_loop(sizes, meta, values, values.shape[2], *spot, product)
    for pair in range(sizes[1] // 2):
        points = slice(pair * PAIR, (pair + 1) * PAIR)
        values, start = field[points, :].T, 0
        for out in outs:
            out[:, points] = values[start : start + out.shape[0]].astype(out.dtype)
            start += out.shape[0]


WHOLE = pl.BlockSpec(memory_space=pltpu.VMEM)


def cost(us):
    return pl.CostEstimate(flops=1 + us * 10**9, bytes_accessed=1, transcendentals=0)


def join_small(blocks):
    return blocks if blocks[0].shape[0] % 16 == 0 else [jnp.concatenate(blocks)]


def split_small(blocks, count):
    return blocks if len(blocks) == count else jnp.split(blocks[0], count)


def vmem(scratch):
    size = sum(math.prod(ref.shape) * jnp.dtype(ref.dtype).itemsize for ref in scratch)
    return pltpu.CompilerParams(vmem_limit_bytes=size + VMEM_SLACK)


def project(
    sizes, meta, wave, pieces, count, width, spot, firsts=(), total=None, last=False, us=0
):
    rows = wave.shape[0]
    operands = [wave, *pieces] + ([] if total is None else [total])
    shapes = []
    if len(pieces) > 1:
        held = sum(piece.shape[0] for piece in pieces)
        shapes.append(jax.ShapeDtypeStruct((held,) + pieces[0].shape[1:], jnp.bfloat16))
    scratch = [pltpu.VMEM((2, sizes[1] // 2 + 1, rows, PAIR), jnp.bfloat16)]
    if last:
        outs = count if rows // count % 16 == 0 else 1
        shapes += [jax.ShapeDtypeStruct((rows // outs, width), jnp.bfloat16)] * outs
        scratch = [pltpu.VMEM((rows, width), jnp.float32)] + scratch
    else:
        shapes.append(jax.ShapeDtypeStruct((rows, width), jnp.float32))
    result = pl.pallas_call(
        functools.partial(project_kernel, sizes, firsts, spot, total is None, last),
        grid_spec=pltpu.PrefetchScalarGridSpec(
            num_scalar_prefetch=1,
            grid=(1,),
            in_specs=[WHOLE] * len(operands),
            out_specs=[WHOLE] * len(shapes),
            scratch_shapes=scratch,
        ),
        out_shape=shapes,
        compiler_params=vmem(scratch),
        cost_estimate=cost(us),
    )(meta, *operands)
    joined, result = (result[0], result[1:]) if len(pieces) > 1 else (pieces[0], result)
    return (list(result) if last else result[0]), joined


def spread(sizes, meta, applied, lists, points, spots):
    count = len(applied)
    applied = join_small(applied)
    rows = sum(block.shape[0] for block in applied)
    scratch = [pltpu.VMEM((points + TILE, rows), jnp.float32)]
    result = pl.pallas_call(
        functools.partial(spread_kernel, sizes, len(applied), spots),
        grid_spec=pltpu.PrefetchScalarGridSpec(
            num_scalar_prefetch=1,
            grid=(1,),
            in_specs=[WHOLE] * (len(applied) + len(lists)),
            out_specs=[WHOLE] * len(applied),
            scratch_shapes=scratch,
        ),
        out_shape=[
            jax.ShapeDtypeStruct((block.shape[0], points), jnp.bfloat16) for block in applied
        ],
        compiler_params=vmem(scratch),
        cost_estimate=cost(0),
    )(meta, *applied, *lists)
    return split_small(result, count)


def two_parts(values):
    high = values.astype(jnp.bfloat16)
    return high, (values - high.astype(jnp.float32)).astype(jnp.bfloat16)


def couple_kernel(high_ref, low_ref, *refs):
    parts, out_ref = refs[:-1], refs[-1]
    blocks, proj, unused = high_ref.shape
    for block in range(blocks):
        lanes = slice(block * proj, (block + 1) * proj)
        total = parts[0][:, lanes].astype(jnp.float32)
        for part in parts[1:]:
            total += part[:, lanes].astype(jnp.float32)
        high, low = two_parts(total)
        result = jnp.dot(high, high_ref[block], preferred_element_type=jnp.float32)
        result += jnp.dot(high, low_ref[block], preferred_element_type=jnp.float32)
        result += jnp.dot(low, high_ref[block], preferred_element_type=jnp.float32)
        out_ref[:, lanes] = result.astype(out_ref.dtype)


def couple(parts, high, low):
    return pl.pallas_call(
        couple_kernel,
        in_specs=[WHOLE] * (2 + len(parts)),
        out_specs=WHOLE,
        out_shape=jax.ShapeDtypeStruct(parts[0].shape, jnp.bfloat16),
        compiler_params=vmem([]),
        cost_estimate=cost(0),
    )(high, low, *parts)


def coupling_matrix(coupling):
    blocks, atoms, width, unused = coupling.shape
    proj = atoms * width
    wide = jnp.tile(coupling.reshape(blocks, proj, width), (1, 1, atoms))
    same = jnp.arange(proj)[:, None] // width == jnp.arange(proj)[None, :] // width
    return jnp.where(same[None], wide, 0.0)


def body(n_grid, wavefunctions, tile_segment, tile_block, tile_count, projectors, coupling):
    half = n_grid // 2
    bands, npts = wavefunctions.shape
    points = npts // n_grid
    tiles = projectors.shape[0]
    width = coupling.shape[0] * projectors.shape[2]
    index = lax.axis_index("grid")
    side, place = index // half, index % half
    group, core = lax.axis_index("groups"), lax.axis_index("band")
    partners = [(i, (i + half) % n_grid) for i in range(n_grid)]
    pools = [list(range(half)), list(range(half, n_grid))]
    swap = [(0, 1), (1, 0)]

    def exchange(blocks):
        return [blocks[0]] + [
            lax.ppermute(
                blocks[d], "grid", [(i, i // half * half + (i % half ^ d)) for i in range(n_grid)]
            )
            for d in range(1, half)
        ]

    def to_bricks(which, after):
        part = lax.dynamic_slice_in_dim(wavefunctions, which * half * points, half * points, 1)
        part = lax.optimization_barrier((part, after))[0]
        return lax.all_to_all(
            part, "grid", split_axis=1, concat_axis=0, tiled=True, axis_index_groups=pools
        )

    segments, blocks = points // TILE, coupling.shape[0]
    sizes = (tiles, segments, blocks)
    slots = jnp.arange(tiles, dtype=jnp.int32)
    starts = [tiles * sum(PARTS[:number]) // sum(PARTS) for number in range(len(PARTS) + 1)]
    held, range_of, bases = slots, 0, [0]
    for part in ORDER:
        start, end = starts[part], starts[part + 1]
        share = (end - start) // 4
        quarter, rest = (slots - start) // share, (slots - start) % share
        at = bases[-1] + rest + share * ((quarter // 2 ^ group) + 2 * (quarter % 2 ^ core))
        inside = (slots >= start) & (slots < end)
        held = jnp.where(inside, at, held)
        later = sum(len(bases) > first for first, end in RANGES[1:])
        range_of += jnp.where(inside, later, 0)
        bases.append(bases[-1] + end - start)

    matrix = two_parts(coupling_matrix(coupling))

    neighbours = [
        (i, i // half * half + (i % half ^ max(1, half // 2))) for i in range(n_grid)
    ]

    def quarter_of(source, start, end):
        share = (end - start) // 4
        return lax.dynamic_slice_in_dim(source, start + (2 * group + core) * share, share, 0)

    first = quarter_of(projectors, starts[0], starts[1])
    first, source = lax.optimization_barrier((first, projectors))
    first = lax.ppermute(first, "grid", partners)
    upper = quarter_of(source, starts[2], starts[3])
    middle = upper.shape[0] // 2
    taken = lax.ppermute(upper[middle:], "grid", neighbours)
    upper = jnp.where(tile_count[0] > starts[2], upper[:middle], taken)
    upper = lax.ppermute(lax.optimization_barrier((upper, first))[0], "grid", partners)
    second = quarter_of(source, starts[1], starts[2])
    second = lax.ppermute(lax.optimization_barrier((second, first))[0], "grid", partners)
    rest = lax.ppermute(upper, "grid", neighbours)

    own_wave = to_bricks(side, first)
    other_wave = to_bricks(1 - side, first)
    numbers = jnp.stack([tile_segment, tile_block, jnp.broadcast_to(tile_count, (tiles,))])
    numbers = lax.optimization_barrier((numbers, first))[0]
    others = lax.ppermute(numbers, "grid", partners)
    absent = segments << bits(tiles)
    segment, block = (jnp.stack([numbers[i], others[i]]) for i in (0, 1))
    codes = jnp.stack([slots, held])
    codes += (segment + (block << bits(segments + 1))) << bits(tiles)
    live = slots < jnp.stack([numbers[2], others[2]])
    keys = block + blocks * jnp.stack([jnp.zeros_like(slots), range_of])
    meta = jnp.concatenate(
        [
            jnp.stack([place, numbers[2, 0], others[2, 0]]),
            group_lists(codes, keys, live, blocks, absent),
        ]
    )

    own_spot = (OWN, 0, len(RANGES), 0)
    total, own_tiles = project(
        sizes, meta, own_wave, [projectors], half, width, own_spot, us=10
    )

    def over_groups(block):
        return lax.ppermute(block, "groups", swap)

    def to_core(blocks):
        return blocks + [lax.ppermute(block, "band", swap) for block in blocks]

    held_first = [first, over_groups(first)]
    sent, total, matrix, held_first = lax.optimization_barrier((second, total, matrix, held_first))
    held_second = [second, over_groups(sent)]
    held_second, other_wave = lax.optimization_barrier((held_second, other_wave))
    held_upper = [upper, rest, over_groups(upper), over_groups(rest)]
    pieces = [to_core(blocks) for blocks in (held_first, held_upper, held_second)]

    joined, other_spots = [], []
    for number, (first, end) in enumerate(RANGES):
        other_spots.append((OTHER, number, number + 1, bases[first]))
        last = end == len(PARTS)
        total, tiles_held = project(
            sizes,
            meta,
            other_wave,
            sum(pieces[first:end], []),
            half,
            width,
            other_spots[-1],
            sum(([starts[ORDER[at]]] * len(pieces[at]) for at in range(first, end)), []),
            total,
            last=last,
            us=0 if last else 8,
        )
        joined.append(tiles_held)
    if len(total) < half:
        total = [lax.dynamic_slice_in_dim(total[0], (place ^ d) * bands, bands, 0) for d in range(half)]

    applied = couple(exchange(total), *matrix)
    applied = exchange([applied] * half)

    result = jnp.zeros((bands, npts), jnp.bfloat16)
    for which, field in (
        (1 - side, spread(sizes, meta, applied, joined, points, other_spots)),
        (side, spread(sizes, meta, applied, [own_tiles], points, [own_spot])),
    ):
        for d, block in enumerate(exchange(field)):
            start = (which * half + (place ^ d)) * points
            result = lax.dynamic_update_slice_in_dim(result, block, start, 1)
    return result


def solution(mesh):
    in_specs = (
        P(("groups", "grid", "band"), None),
        P("grid"),
        P("grid"),
        P("grid"),
        P("grid", None, None),
        P(),
    )
    out_specs = P(("groups", "grid", "band"), None)
    return jax.shard_map(
        functools.partial(body, mesh.shape["grid"]),
        mesh=mesh,
        in_specs=in_specs,
        out_specs=out_specs,
        check_vma=False,
    )
```

```python
import functools
import math

import jax
import jax.numpy as jnp
from jax import lax
from jax.experimental import pallas as pl
from jax.experimental.pallas import tpu as pltpu
from jax.sharding import PartitionSpec as P

TILE = 64
PAIR = 2 * TILE
GROUP = 4
UNROLL = 4
VMEM_SLACK = 10 * 1024 * 1024
PARTS = (1, 1, 2)
ORDER = (0, 2, 1)
RANGES = ((0, 2), (2, 3))
OWN, OTHER = range(2)
BOUNDS = 3
STEPS = len(RANGES) + 1
LISTS = BOUNDS + 2 * STEPS


def bits(count):
    return max(1, (count - 1).bit_length())


def list_length(tiles, blocks):
    return tiles + len(RANGES) * ((GROUP - 1) * blocks + GROUP * UNROLL)


def group_lists(codes, keys, live, blocks, absent):
    n_lists, tiles = codes.shape
    n_keys = len(RANGES) * blocks
    order = jnp.arange(tiles, dtype=jnp.int32)
    key_range = jnp.arange(n_keys, dtype=jnp.int32)
    ranges = jnp.arange(STEPS, dtype=jnp.int32)
    mine = (keys[:, None, :] == key_range[None, :, None]) & live[:, None, :]
    groups = (jnp.sum(mine, axis=2, dtype=jnp.int32) + GROUP - 1) // GROUP
    in_range = key_range[:, None] // blocks == ranges[None, :]
    totals = jnp.sum(jnp.where(in_range, groups[:, :, None], 0), axis=1, dtype=jnp.int32)
    totals = (totals + UNROLL - 1) // UNROLL * UNROLL
    bounds = jnp.sum(
        jnp.where(ranges[:, None] < ranges[None, :], totals[:, :, None], 0), axis=1, dtype=jnp.int32
    )
    lower = (key_range[:, None] < key_range[None, :]) & (
        key_range[:, None] // blocks == key_range[None, :] // blocks
    )
    starts = jnp.sum(jnp.where(lower, groups[:, :, None], 0), axis=1, dtype=jnp.int32)
    starts += jnp.sum(jnp.where(in_range, bounds[:, None, :], 0), axis=2, dtype=jnp.int32)
    before = (
        (keys[:, :, None] == keys[:, None, :]) & live[:, :, None] & (order[:, None] < order[None, :])
    )
    entry = jnp.sum(before, axis=1, dtype=jnp.int32) + GROUP * jnp.sum(
        jnp.where(mine, starts[:, :, None], 0), axis=1, dtype=jnp.int32
    )
    entry = jnp.where(live, entry, -1)
    found = entry[:, :, None] == jnp.arange(list_length(tiles, blocks), dtype=jnp.int32)
    entries = absent + jnp.sum(
        jnp.where(found, codes[:, :, None] - absent, 0), axis=1, dtype=jnp.int32
    )
    return jnp.concatenate([bounds.reshape(-1), entries.reshape(-1)])


def group_loop(sizes, meta, values, proj, which, first, last, origin, product):
    tiles, segments, blocks = sizes
    begin, end = (meta[BOUNDS + STEPS * which + number] for number in (first, last))
    base = LISTS + which * list_length(tiles, blocks)

    def group(number):
        places = []
        for entry in range(GROUP):
            code = meta[base + GROUP * number + entry]
            index = jnp.maximum((code & ((1 << bits(tiles)) - 1)) - origin, 0)
            code = code >> bits(tiles)
            places.append((code & ((1 << bits(segments + 1)) - 1), values[index]))
            if entry == 0:
                block = code >> bits(segments + 1)
        lanes = pl.ds(pl.multiple_of(block * proj, proj), proj)
        return product(lanes, [at for at, tile in places], [tile for at, tile in places])

    def step(index, carry):
        sums = [group(begin + index * UNROLL + lane) for lane in range(UNROLL)]
        for additions in sums:
            for ref, rows, lanes, term in additions:
                ref[rows, lanes] += term
        return carry

    lax.fori_loop(0, (end - begin) // UNROLL, step, 0)


def join_pieces(meta, pieces, joined, firsts):
    end = 0
    for first, ref in zip(firsts, pieces):
        start, end = end, end + ref.shape[0]

        @pl.when(meta[2] > first)
        def copy(start=start, end=end, ref=ref):
            joined[start:end] = ref[...]


def rows_of(refs, lanes):
    return jnp.concatenate([ref[:, lanes] for ref in refs], axis=0)


def turn_waves(wave, turned, segments):
    for pair in range(segments // 2):
        values = wave[:, pair * PAIR : (pair + 1) * PAIR]
        turned[0, pair] = values
        turned[1, pair] = pltpu.roll(values.astype(jnp.float32), TILE, 1).astype(values.dtype)
    for way in range(2):
        turned[way, segments // 2] = jnp.zeros(turned.shape[2:], turned.dtype)


def project_kernel(sizes, firsts, spot, first, last, meta, wave, *refs):
    n_pieces = max(1, len(firsts))
    pieces, refs = refs[:n_pieces], refs[n_pieces:]
    turned, refs = refs[-1], refs[:-1]
    if not first:
        before, refs = refs[0], refs[1:]
    values = pieces[0]
    if n_pieces > 1:
        values, refs = refs[0], refs[1:]
        join_pieces(meta, pieces, values, firsts)
    total = refs[-1]
    total[...] = jnp.zeros_like(total) if first else before[...]
    every = slice(None)

    def product(lanes, segments, tiles):
        low = lax.broadcasted_iota(jnp.int32, turned.shape[2:], 1) < TILE
        waves = [
            jnp.where(
                low,
                turned[segments[at] & 1, segments[at] >> 1],
                turned[1 - (segments[at + 1] & 1), segments[at + 1] >> 1],
            )
            for at in range(0, GROUP, 2)
        ]
        term = jnp.dot(
            jnp.concatenate(waves, axis=1),
            jnp.concatenate(tiles, axis=0),
            preferred_element_type=jnp.float32,
        )
        return [(total, every, lanes, term)]

    begin, end = (meta[BOUNDS + STEPS * spot[0] + number] for number in spot[1:3])

    @pl.when(end > begin)
    def loop():
        turn_waves(wave, turned, sizes[1])
        group_loop(sizes, meta, values, values.shape[2], *spot, product)

    if last:
        outs = refs[:-1]
        rows = outs[0].shape[0]
        for d, out in enumerate(outs):
            start = 0 if len(outs) == 1 else pl.multiple_of((meta[0] ^ d) * rows, rows)
            out[...] = total[pl.ds(start, rows), :].astype(out.dtype)


def spread_kernel(sizes, n_rows, spots, meta, *refs):
    applied, refs = refs[:n_rows], refs[n_rows:]
    lists, refs = refs[: len(spots)], refs[len(spots) :]
    outs, field = refs[:-1], refs[-1]
    field[...] = jnp.zeros_like(field)
    every = slice(None)

    def product(lanes, segments, tiles):
        terms = lax.dot_general(
            jnp.concatenate(tiles, axis=0),
            rows_of(applied, lanes),
            (((1,), (1,)), ((), ())),
            preferred_element_type=jnp.float32,
        )
        return [
            (
                field,
                pl.ds(pl.multiple_of(at * TILE, TILE), TILE),
                every,
                terms[number * TILE : (number + 1) * TILE],
            )
            for number, at in enumerate(segments)
        ]

    for values, spot in zip(lists, spots):
        group_loop(sizes, meta, values, values.shape[2], *spot, product)
    for pair in range(sizes[1] // 2):
        points = slice(pair * PAIR, (pair + 1) * PAIR)
        values, start = field[points, :].T, 0
        for out in outs:
            out[:, points] = values[start : start + out.shape[0]].astype(out.dtype)
            start += out.shape[0]


WHOLE = pl.BlockSpec(memory_space=pltpu.VMEM)


def cost(us):
    return pl.CostEstimate(flops=1 + us * 10**9, bytes_accessed=1, transcendentals=0)


def join_small(blocks):
    return blocks if blocks[0].shape[0] % 16 == 0 else [jnp.concatenate(blocks)]


def split_small(blocks, count):
    return blocks if len(blocks) == count else jnp.split(blocks[0], count)


def vmem(scratch):
    size = sum(math.prod(ref.shape) * jnp.dtype(ref.dtype).itemsize for ref in scratch)
    return pltpu.CompilerParams(vmem_limit_bytes=size + VMEM_SLACK)


def project(
    sizes, meta, wave, pieces, count, width, spot, firsts=(), total=None, last=False, us=0
):
    rows = wave.shape[0]
    operands = [wave, *pieces] + ([] if total is None else [total])
    shapes = []
    if len(pieces) > 1:
        held = sum(piece.shape[0] for piece in pieces)
        shapes.append(jax.ShapeDtypeStruct((held,) + pieces[0].shape[1:], jnp.bfloat16))
    scratch = [pltpu.VMEM((2, sizes[1] // 2 + 1, rows, PAIR), jnp.bfloat16)]
    if last:
        outs = count if rows // count % 16 == 0 else 1
        shapes += [jax.ShapeDtypeStruct((rows // outs, width), jnp.bfloat16)] * outs
        scratch = [pltpu.VMEM((rows, width), jnp.float32)] + scratch
    else:
        shapes.append(jax.ShapeDtypeStruct((rows, width), jnp.float32))
    result = pl.pallas_call(
        functools.partial(project_kernel, sizes, firsts, spot, total is None, last),
        grid_spec=pltpu.PrefetchScalarGridSpec(
            num_scalar_prefetch=1,
            grid=(1,),
            in_specs=[WHOLE] * len(operands),
            out_specs=[WHOLE] * len(shapes),
            scratch_shapes=scratch,
        ),
        out_shape=shapes,
        compiler_params=vmem(scratch),
        cost_estimate=cost(us),
    )(meta, *operands)
    joined, result = (result[0], result[1:]) if len(pieces) > 1 else (pieces[0], result)
    return (list(result) if last else result[0]), joined


def spread(sizes, meta, applied, lists, points, spots):
    count = len(applied)
    applied = join_small(applied)
    rows = sum(block.shape[0] for block in applied)
    scratch = [pltpu.VMEM((points + TILE, rows), jnp.float32)]
    result = pl.pallas_call(
        functools.partial(spread_kernel, sizes, len(applied), spots),
        grid_spec=pltpu.PrefetchScalarGridSpec(
            num_scalar_prefetch=1,
            grid=(1,),
            in_specs=[WHOLE] * (len(applied) + len(lists)),
            out_specs=[WHOLE] * len(applied),
            scratch_shapes=scratch,
        ),
        out_shape=[
            jax.ShapeDtypeStruct((block.shape[0], points), jnp.bfloat16) for block in applied
        ],
        compiler_params=vmem(scratch),
        cost_estimate=cost(0),
    )(meta, *applied, *lists)
    return split_small(result, count)


def two_parts(values):
    high = values.astype(jnp.bfloat16)
    return high, (values - high.astype(jnp.float32)).astype(jnp.bfloat16)


def couple_kernel(high_ref, low_ref, *refs):
    parts, out_ref = refs[:-1], refs[-1]
    blocks, proj, unused = high_ref.shape
    for block in range(blocks):
        lanes = slice(block * proj, (block + 1) * proj)
        total = parts[0][:, lanes].astype(jnp.float32)
        for part in parts[1:]:
            total += part[:, lanes].astype(jnp.float32)
        high, low = two_parts(total)
        result = jnp.dot(high, high_ref[block], preferred_element_type=jnp.float32)
        result += jnp.dot(high, low_ref[block], preferred_element_type=jnp.float32)
        result += jnp.dot(low, high_ref[block], preferred_element_type=jnp.float32)
        out_ref[:, lanes] = result.astype(out_ref.dtype)


def couple(parts, high, low):
    return pl.pallas_call(
        couple_kernel,
        in_specs=[WHOLE] * (2 + len(parts)),
        out_specs=WHOLE,
        out_shape=jax.ShapeDtypeStruct(parts[0].shape, jnp.bfloat16),
        compiler_params=vmem([]),
        cost_estimate=cost(0),
    )(high, low, *parts)


def coupling_matrix(coupling):
    blocks, atoms, width, unused = coupling.shape
    proj = atoms * width
    wide = jnp.tile(coupling.reshape(blocks, proj, width), (1, 1, atoms))
    same = jnp.arange(proj)[:, None] // width == jnp.arange(proj)[None, :] // width
    return jnp.where(same[None], wide, 0.0)


def body(n_grid, wavefunctions, tile_segment, tile_block, tile_count, projectors, coupling):
    half = n_grid // 2
    bands, npts = wavefunctions.shape
    points = npts // n_grid
    tiles = projectors.shape[0]
    width = coupling.shape[0] * projectors.shape[2]
    index = lax.axis_index("grid")
    side, place = index // half, index % half
    group, core = lax.axis_index("groups"), lax.axis_index("band")
    partners = [(i, (i + half) % n_grid) for i in range(n_grid)]
    pools = [list(range(half)), list(range(half, n_grid))]
    swap = [(0, 1), (1, 0)]

    def exchange(blocks):
        return [blocks[0]] + [
            lax.ppermute(
                blocks[d], "grid", [(i, i // half * half + (i % half ^ d)) for i in range(n_grid)]
            )
            for d in range(1, half)
        ]

    def to_bricks(which, after):
        part = lax.dynamic_slice_in_dim(wavefunctions, which * half * points, half * points, 1)
        part = lax.optimization_barrier((part, after))[0]
        return lax.all_to_all(
            part, "grid", split_axis=1, concat_axis=0, tiled=True, axis_index_groups=pools
        )

    segments, blocks = points // TILE, coupling.shape[0]
    sizes = (tiles, segments, blocks)
    slots = jnp.arange(tiles, dtype=jnp.int32)
    starts = [tiles * sum(PARTS[:number]) // sum(PARTS) for number in range(len(PARTS) + 1)]
    held, range_of, bases = slots, 0, [0]
    for part in ORDER:
        start, end = starts[part], starts[part + 1]
        share = (end - start) // 4
        quarter, rest = (slots - start) // share, (slots - start) % share
        at = bases[-1] + rest + share * ((quarter // 2 ^ group) + 2 * (quarter % 2 ^ core))
        inside = (slots >= start) & (slots < end)
        held = jnp.where(inside, at, held)
        later = sum(len(bases) > first for first, end in RANGES[1:])
        range_of += jnp.where(inside, later, 0)
        bases.append(bases[-1] + end - start)

    matrix = two_parts(coupling_matrix(coupling))

    neighbours = [
        (i, i // half * half + (i % half ^ max(1, half // 2))) for i in range(n_grid)
    ]

    def quarter_of(source, start, end):
        share = (end - start) // 4
        return lax.dynamic_slice_in_dim(source, start + (2 * group + core) * share, share, 0)

    first = quarter_of(projectors, starts[0], starts[1])
    first, source = lax.optimization_barrier((first, projectors))
    first = lax.ppermute(first, "grid", partners)
    upper = quarter_of(source, starts[2], starts[3])
    middle = upper.shape[0] // 2
    taken = lax.ppermute(upper[middle:], "grid", neighbours)
    upper = jnp.where(tile_count[0] > starts[2], upper[:middle], taken)
    upper = lax.ppermute(lax.optimization_barrier((upper, first))[0], "grid", partners)
    rest = lax.ppermute(upper, "grid", neighbours)
    second = quarter_of(source, starts[1], starts[2])

    own_wave = to_bricks(side, first)
    other_wave = to_bricks(1 - side, first)
    numbers = jnp.stack([tile_segment, tile_block, jnp.broadcast_to(tile_count, (tiles,))])
    numbers = lax.optimization_barrier((numbers, first))[0]
    others = lax.ppermute(numbers, "grid", partners)
    second = lax.ppermute(lax.optimization_barrier((second, others))[0], "grid", partners)
    absent = segments << bits(tiles)
    segment, block = (jnp.stack([numbers[i], others[i]]) for i in (0, 1))
    codes = jnp.stack([slots, held])
    codes += (segment + (block << bits(segments + 1))) << bits(tiles)
    live = slots < jnp.stack([numbers[2], others[2]])
    keys = block + blocks * jnp.stack([jnp.zeros_like(slots), range_of])
    meta = jnp.concatenate(
        [
            jnp.stack([place, numbers[2, 0], others[2, 0]]),
            group_lists(codes, keys, live, blocks, absent),
        ]
    )

    own_wave = lax.optimization_barrier((own_wave, upper))[0]
    own_spot = (OWN, 0, len(RANGES), 0)
    total, own_tiles = project(
        sizes, meta, own_wave, [projectors], half, width, own_spot, us=5
    )

    def over_groups(block):
        return lax.ppermute(block, "groups", swap)

    def to_core(blocks):
        return blocks + [lax.ppermute(block, "band", swap) for block in blocks]

    held_first = [first, over_groups(first)]
    sent, matrix = lax.optimization_barrier((second, matrix))
    held_second = [second, over_groups(sent)]
    held_second, other_wave = lax.optimization_barrier((held_second, other_wave))
    held_upper = [upper, rest, over_groups(upper), over_groups(rest)]
    pieces = [to_core(blocks) for blocks in (held_first, held_upper, held_second)]

    joined, other_spots = [], []
    for number, (first, end) in enumerate(RANGES):
        other_spots.append((OTHER, number, number + 1, bases[first]))
        last = end == len(PARTS)
        total, tiles_held = project(
            sizes,
            meta,
            other_wave,
            sum(pieces[first:end], []),
            half,
            width,
            other_spots[-1],
            sum(([starts[ORDER[at]]] * len(pieces[at]) for at in range(first, end)), []),
            total,
            last=last,
            us=0 if last else 8,
        )
        joined.append(tiles_held)
    if len(total) < half:
        total = [lax.dynamic_slice_in_dim(total[0], (place ^ d) * bands, bands, 0) for d in range(half)]

    applied = couple(exchange(total), *matrix)
    applied = exchange([applied] * half)

    result = jnp.zeros((bands, npts), jnp.bfloat16)
    for which, field in (
        (1 - side, spread(sizes, meta, applied, joined, points, other_spots)),
        (side, spread(sizes, meta, applied, [own_tiles], points, [own_spot])),
    ):
        for d, block in enumerate(exchange(field)):
            start = (which * half + (place ^ d)) * points
            result = lax.dynamic_update_slice_in_dim(result, block, start, 1)
    return result


def solution(mesh):
    in_specs = (
        P(("groups", "grid", "band"), None),
        P("grid"),
        P("grid"),
        P("grid"),
        P("grid", None, None),
        P(),
    )
    out_specs = P(("groups", "grid", "band"), None)
    return jax.shard_map(
        functools.partial(body, mesh.shape["grid"]),
        mesh=mesh,
        in_specs=in_specs,
        out_specs=out_specs,
        check_vma=False,
    )
```

```python
import functools
import math

import jax
import jax.numpy as jnp
from jax import lax
from jax.experimental import pallas as pl
from jax.experimental.pallas import tpu as pltpu
from jax.sharding import PartitionSpec as P

TILE = 64
PAIR = 2 * TILE
GROUP = 4
UNROLL = 4
VMEM_SLACK = 10 * 1024 * 1024
PARTS = (1, 1, 2)
ORDER = (0, 2, 1)
RANGES = ((0, 2), (2, 3))
OWN, OTHER = range(2)
BOUNDS = 3
STEPS = len(RANGES) + 1
LISTS = BOUNDS + 2 * STEPS


def bits(count):
    return max(1, (count - 1).bit_length())


def list_length(tiles, blocks):
    return tiles + len(RANGES) * ((GROUP - 1) * blocks + GROUP * UNROLL)


def group_lists(codes, keys, live, blocks, absent):
    n_lists, tiles = codes.shape
    n_keys = len(RANGES) * blocks
    order = jnp.arange(tiles, dtype=jnp.int32)
    key_range = jnp.arange(n_keys, dtype=jnp.int32)
    ranges = jnp.arange(STEPS, dtype=jnp.int32)
    mine = (keys[:, None, :] == key_range[None, :, None]) & live[:, None, :]
    groups = (jnp.sum(mine, axis=2, dtype=jnp.int32) + GROUP - 1) // GROUP
    in_range = key_range[:, None] // blocks == ranges[None, :]
    totals = jnp.sum(jnp.where(in_range, groups[:, :, None], 0), axis=1, dtype=jnp.int32)
    totals = (totals + UNROLL - 1) // UNROLL * UNROLL
    bounds = jnp.sum(
        jnp.where(ranges[:, None] < ranges[None, :], totals[:, :, None], 0), axis=1, dtype=jnp.int32
    )
    lower = (key_range[:, None] < key_range[None, :]) & (
        key_range[:, None] // blocks == key_range[None, :] // blocks
    )
    starts = jnp.sum(jnp.where(lower, groups[:, :, None], 0), axis=1, dtype=jnp.int32)
    starts += jnp.sum(jnp.where(in_range, bounds[:, None, :], 0), axis=2, dtype=jnp.int32)
    before = (
        (keys[:, :, None] == keys[:, None, :]) & live[:, :, None] & (order[:, None] < order[None, :])
    )
    entry = jnp.sum(before, axis=1, dtype=jnp.int32) + GROUP * jnp.sum(
        jnp.where(mine, starts[:, :, None], 0), axis=1, dtype=jnp.int32
    )
    entry = jnp.where(live, entry, -1)
    found = entry[:, :, None] == jnp.arange(list_length(tiles, blocks), dtype=jnp.int32)
    entries = absent + jnp.sum(
        jnp.where(found, codes[:, :, None] - absent, 0), axis=1, dtype=jnp.int32
    )
    return jnp.concatenate([bounds.reshape(-1), entries.reshape(-1)])


def group_loop(sizes, meta, values, proj, which, first, last, origin, product):
    tiles, segments, blocks = sizes
    begin, end = (meta[BOUNDS + STEPS * which + number] for number in (first, last))
    base = LISTS + which * list_length(tiles, blocks)

    def group(number):
        places = []
        for entry in range(GROUP):
            code = meta[base + GROUP * number + entry]
            index = jnp.maximum((code & ((1 << bits(tiles)) - 1)) - origin, 0)
            code = code >> bits(tiles)
            places.append((code & ((1 << bits(segments + 1)) - 1), values[index]))
            if entry == 0:
                block = code >> bits(segments + 1)
        lanes = pl.ds(pl.multiple_of(block * proj, proj), proj)
        return product(lanes, [at for at, tile in places], [tile for at, tile in places])

    def step(index, carry):
        sums = [group(begin + index * UNROLL + lane) for lane in range(UNROLL)]
        for additions in sums:
            for ref, rows, lanes, term in additions:
                ref[rows, lanes] += term
        return carry

    lax.fori_loop(0, (end - begin) // UNROLL, step, 0)


def join_pieces(meta, pieces, joined, firsts):
    end = 0
    for first, ref in zip(firsts, pieces):
        start, end = end, end + ref.shape[0]

        @pl.when(meta[2] > first)
        def copy(start=start, end=end, ref=ref):
            joined[start:end] = ref[...]


def rows_of(refs, lanes):
    return jnp.concatenate([ref[:, lanes] for ref in refs], axis=0)


def turn_waves(wave, turned, segments):
    for pair in range(segments // 2):
        values = wave[:, pair * PAIR : (pair + 1) * PAIR]
        turned[0, pair] = values
        turned[1, pair] = pltpu.roll(values.astype(jnp.float32), TILE, 1).astype(values.dtype)
    for way in range(2):
        turned[way, segments // 2] = jnp.zeros(turned.shape[2:], turned.dtype)


def project_kernel(sizes, firsts, spot, first, last, meta, wave, *refs):
    n_pieces = max(1, len(firsts))
    pieces, refs = refs[:n_pieces], refs[n_pieces:]
    turned, refs = refs[-1], refs[:-1]
    if not first:
        before, refs = refs[0], refs[1:]
    values = pieces[0]
    if n_pieces > 1:
        values, refs = refs[0], refs[1:]
        join_pieces(meta, pieces, values, firsts)
    total = refs[-1]
    total[...] = jnp.zeros_like(total) if first else before[...]
    every = slice(None)

    def product(lanes, segments, tiles):
        low = lax.broadcasted_iota(jnp.int32, turned.shape[2:], 1) < TILE
        waves = [
            jnp.where(
                low,
                turned[segments[at] & 1, segments[at] >> 1],
                turned[1 - (segments[at + 1] & 1), segments[at + 1] >> 1],
            )
            for at in range(0, GROUP, 2)
        ]
        term = jnp.dot(
            jnp.concatenate(waves, axis=1),
            jnp.concatenate(tiles, axis=0),
            preferred_element_type=jnp.float32,
        )
        return [(total, every, lanes, term)]

    begin, end = (meta[BOUNDS + STEPS * spot[0] + number] for number in spot[1:3])

    @pl.when(end > begin)
    def loop():
        turn_waves(wave, turned, sizes[1])
        group_loop(sizes, meta, values, values.shape[2], *spot, product)

    if last:
        outs = refs[:-1]
        rows = outs[0].shape[0]
        for d, out in enumerate(outs):
            start = 0 if len(outs) == 1 else pl.multiple_of((meta[0] ^ d) * rows, rows)
            out[...] = total[pl.ds(start, rows), :].astype(out.dtype)


def spread_kernel(sizes, n_rows, spots, meta, *refs):
    applied, refs = refs[:n_rows], refs[n_rows:]
    lists, refs = refs[: len(spots)], refs[len(spots) :]
    outs, field = refs[:-1], refs[-1]
    field[...] = jnp.zeros_like(field)
    every = slice(None)

    def product(lanes, segments, tiles):
        terms = lax.dot_general(
            jnp.concatenate(tiles, axis=0),
            rows_of(applied, lanes),
            (((1,), (1,)), ((), ())),
            preferred_element_type=jnp.float32,
        )
        return [
            (
                field,
                pl.ds(pl.multiple_of(at * TILE, TILE), TILE),
                every,
                terms[number * TILE : (number + 1) * TILE],
            )
            for number, at in enumerate(segments)
        ]

    for values, spot in zip(lists, spots):
        group_loop(sizes, meta, values, values.shape[2], *spot, product)
    for pair in range(sizes[1] // 2):
        points = slice(pair * PAIR, (pair + 1) * PAIR)
        values, start = field[points, :].T, 0
        for out in outs:
            out[:, points] = values[start : start + out.shape[0]].astype(out.dtype)
            start += out.shape[0]


WHOLE = pl.BlockSpec(memory_space=pltpu.VMEM)


def cost(us):
    return pl.CostEstimate(flops=1 + us * 10**9, bytes_accessed=1, transcendentals=0)


def join_small(blocks):
    return blocks if blocks[0].shape[0] % 16 == 0 else [jnp.concatenate(blocks)]


def split_small(blocks, count):
    return blocks if len(blocks) == count else jnp.split(blocks[0], count)


def vmem(scratch):
    size = sum(math.prod(ref.shape) * jnp.dtype(ref.dtype).itemsize for ref in scratch)
    return pltpu.CompilerParams(vmem_limit_bytes=size + VMEM_SLACK)


def project(
    sizes, meta, wave, pieces, count, width, spot, firsts=(), total=None, last=False, us=0
):
    rows = wave.shape[0]
    operands = [wave, *pieces] + ([] if total is None else [total])
    shapes = []
    if len(pieces) > 1:
        held = sum(piece.shape[0] for piece in pieces)
        shapes.append(jax.ShapeDtypeStruct((held,) + pieces[0].shape[1:], jnp.bfloat16))
    scratch = [pltpu.VMEM((2, sizes[1] // 2 + 1, rows, PAIR), jnp.bfloat16)]
    if last:
        outs = count if rows // count % 16 == 0 else 1
        shapes += [jax.ShapeDtypeStruct((rows // outs, width), jnp.bfloat16)] * outs
        scratch = [pltpu.VMEM((rows, width), jnp.float32)] + scratch
    else:
        shapes.append(jax.ShapeDtypeStruct((rows, width), jnp.float32))
    result = pl.pallas_call(
        functools.partial(project_kernel, sizes, firsts, spot, total is None, last),
        grid_spec=pltpu.PrefetchScalarGridSpec(
            num_scalar_prefetch=1,
            grid=(1,),
            in_specs=[WHOLE] * len(operands),
            out_specs=[WHOLE] * len(shapes),
            scratch_shapes=scratch,
        ),
        out_shape=shapes,
        compiler_params=vmem(scratch),
        cost_estimate=cost(us),
    )(meta, *operands)
    joined, result = (result[0], result[1:]) if len(pieces) > 1 else (pieces[0], result)
    return (list(result) if last else result[0]), joined


def spread(sizes, meta, applied, lists, points, spots):
    count = len(applied)
    applied = join_small(applied)
    rows = sum(block.shape[0] for block in applied)
    scratch = [pltpu.VMEM((points + TILE, rows), jnp.float32)]
    result = pl.pallas_call(
        functools.partial(spread_kernel, sizes, len(applied), spots),
        grid_spec=pltpu.PrefetchScalarGridSpec(
            num_scalar_prefetch=1,
            grid=(1,),
            in_specs=[WHOLE] * (len(applied) + len(lists)),
            out_specs=[WHOLE] * len(applied),
            scratch_shapes=scratch,
        ),
        out_shape=[
            jax.ShapeDtypeStruct((block.shape[0], points), jnp.bfloat16) for block in applied
        ],
        compiler_params=vmem(scratch),
        cost_estimate=cost(8),
    )(meta, *applied, *lists)
    return split_small(result, count)


def two_parts(values):
    high = values.astype(jnp.bfloat16)
    return high, (values - high.astype(jnp.float32)).astype(jnp.bfloat16)


def couple_kernel(high_ref, low_ref, *refs):
    parts, out_ref = refs[:-1], refs[-1]
    blocks, proj, unused = high_ref.shape
    for block in range(blocks):
        lanes = slice(block * proj, (block + 1) * proj)
        total = parts[0][:, lanes].astype(jnp.float32)
        for part in parts[1:]:
            total += part[:, lanes].astype(jnp.float32)
        high, low = two_parts(total)
        result = jnp.dot(high, high_ref[block], preferred_element_type=jnp.float32)
        result += jnp.dot(high, low_ref[block], preferred_element_type=jnp.float32)
        result += jnp.dot(low, high_ref[block], preferred_element_type=jnp.float32)
        out_ref[:, lanes] = result.astype(out_ref.dtype)


def couple(parts, high, low):
    return pl.pallas_call(
        couple_kernel,
        in_specs=[WHOLE] * (2 + len(parts)),
        out_specs=WHOLE,
        out_shape=jax.ShapeDtypeStruct(parts[0].shape, jnp.bfloat16),
        compiler_params=vmem([]),
        cost_estimate=cost(6),
    )(high, low, *parts)


def coupling_matrix(coupling):
    blocks, atoms, width, unused = coupling.shape
    proj = atoms * width
    wide = jnp.tile(coupling.reshape(blocks, proj, width), (1, 1, atoms))
    same = jnp.arange(proj)[:, None] // width == jnp.arange(proj)[None, :] // width
    return jnp.where(same[None], wide, 0.0)


def body(n_grid, wavefunctions, tile_segment, tile_block, tile_count, projectors, coupling):
    half = n_grid // 2
    bands, npts = wavefunctions.shape
    points = npts // n_grid
    tiles = projectors.shape[0]
    width = coupling.shape[0] * projectors.shape[2]
    index = lax.axis_index("grid")
    side, place = index // half, index % half
    group, core = lax.axis_index("groups"), lax.axis_index("band")
    partners = [(i, (i + half) % n_grid) for i in range(n_grid)]
    pools = [list(range(half)), list(range(half, n_grid))]
    swap = [(0, 1), (1, 0)]

    def exchange(blocks):
        return [blocks[0]] + [
            lax.ppermute(
                blocks[d], "grid", [(i, i // half * half + (i % half ^ d)) for i in range(n_grid)]
            )
            for d in range(1, half)
        ]

    def to_bricks(which, after=None):
        part = lax.dynamic_slice_in_dim(wavefunctions, which * half * points, half * points, 1)
        part = lax.optimization_barrier((part, after))[0]
        return lax.all_to_all(
            part, "grid", split_axis=1, concat_axis=0, tiled=True, axis_index_groups=pools
        )

    segments, blocks = points // TILE, coupling.shape[0]
    sizes = (tiles, segments, blocks)
    slots = jnp.arange(tiles, dtype=jnp.int32)
    starts = [tiles * sum(PARTS[:number]) // sum(PARTS) for number in range(len(PARTS) + 1)]
    held, range_of, bases = slots, 0, [0]
    for part in ORDER:
        start, end = starts[part], starts[part + 1]
        share = (end - start) // 4
        quarter, rest = (slots - start) // share, (slots - start) % share
        at = bases[-1] + rest + share * ((quarter // 2 ^ group) + 2 * (quarter % 2 ^ core))
        inside = (slots >= start) & (slots < end)
        held = jnp.where(inside, at, held)
        later = sum(len(bases) > first for first, end in RANGES[1:])
        range_of += jnp.where(inside, later, 0)
        bases.append(bases[-1] + end - start)

    matrix = two_parts(coupling_matrix(coupling))

    neighbours = [
        (i, i // half * half + (i % half ^ max(1, half // 2))) for i in range(n_grid)
    ]

    def quarter_of(source, start, end):
        share = (end - start) // 4
        return lax.dynamic_slice_in_dim(source, start + (2 * group + core) * share, share, 0)

    upper = quarter_of(projectors, starts[2], starts[3])
    middle = upper.shape[0] // 2
    taken = lax.ppermute(upper[middle:], "grid", neighbours)
    upper = jnp.where(tile_count[0] > starts[2], upper[:middle], taken)
    upper = lax.ppermute(upper, "grid", partners)
    source = lax.optimization_barrier((projectors, taken))[0]
    first, second = (quarter_of(source, starts[at], starts[at + 1]) for at in (0, 1))
    first, second, late = lax.optimization_barrier((first, second, upper))
    first = lax.ppermute(first, "grid", partners)
    second = lax.ppermute(second, "grid", partners)
    rest = lax.ppermute(upper, "grid", neighbours)

    own_wave = to_bricks(side)
    other_wave = to_bricks(1 - side, upper)
    numbers = jnp.stack([tile_segment, tile_block, jnp.broadcast_to(tile_count, (tiles,))])
    numbers = lax.optimization_barrier((numbers, taken))[0]
    others = lax.ppermute(numbers, "grid", partners)
    absent = segments << bits(tiles)
    segment, block = (jnp.stack([numbers[i], others[i]]) for i in (0, 1))
    codes = jnp.stack([slots, held])
    codes += (segment + (block << bits(segments + 1))) << bits(tiles)
    live = slots < jnp.stack([numbers[2], others[2]])
    keys = block + blocks * jnp.stack([jnp.zeros_like(slots), range_of])
    meta = jnp.concatenate(
        [
            jnp.stack([place, numbers[2, 0], others[2, 0]]),
            group_lists(codes, keys, live, blocks, absent),
        ]
    )

    own_wave = lax.optimization_barrier((own_wave, upper))[0]
    own_spot = (OWN, 0, len(RANGES), 0)
    total, own_tiles = project(
        sizes, meta, own_wave, [projectors], half, width, own_spot, us=5
    )

    def over_groups(block):
        return lax.ppermute(block, "groups", swap)

    def to_core(blocks):
        return blocks + [lax.ppermute(block, "band", swap) for block in blocks]

    held_upper = [upper, rest, over_groups(upper)]
    held_first = [first, over_groups(first)]
    rest, late = lax.optimization_barrier((rest, held_upper[-1]))
    held_upper.append(over_groups(rest))
    sent, late, matrix = lax.optimization_barrier((second, (held_upper, held_first), matrix))
    held_second = [second, over_groups(sent)]
    held_second, other_wave = lax.optimization_barrier((held_second, other_wave))
    pieces = [to_core(blocks) for blocks in (held_first, held_upper, held_second)]

    joined, other_spots = [], []
    for number, (first, end) in enumerate(RANGES):
        other_spots.append((OTHER, number, number + 1, bases[first]))
        last = end == len(PARTS)
        total, tiles_held = project(
            sizes,
            meta,
            other_wave,
            sum(pieces[first:end], []),
            half,
            width,
            other_spots[-1],
            sum(([starts[ORDER[at]]] * len(pieces[at]) for at in range(first, end)), []),
            total,
            last=last,
            us=0 if last else 8,
        )
        joined.append(tiles_held)
    if len(total) < half:
        total = [lax.dynamic_slice_in_dim(total[0], (place ^ d) * bands, bands, 0) for d in range(half)]

    applied = couple(exchange(total), *matrix)
    applied = exchange([applied] * half)

    result = jnp.zeros((bands, npts), jnp.bfloat16)
    for which, field in (
        (1 - side, spread(sizes, meta, applied, joined, points, other_spots)),
        (side, spread(sizes, meta, applied, [own_tiles], points, [own_spot])),
    ):
        for d, block in enumerate(exchange(field)):
            start = (which * half + (place ^ d)) * points
            result = lax.dynamic_update_slice_in_dim(result, block, start, 1)
    return result


def solution(mesh):
    in_specs = (
        P(("groups", "grid", "band"), None),
        P("grid"),
        P("grid"),
        P("grid"),
        P("grid", None, None),
        P(),
    )
    out_specs = P(("groups", "grid", "band"), None)
    return jax.shard_map(
        functools.partial(body, mesh.shape["grid"]),
        mesh=mesh,
        in_specs=in_specs,
        out_specs=out_specs,
        check_vma=False,
    )
```

```python
import functools
import math

import jax
import jax.numpy as jnp
from jax import lax
from jax.experimental import pallas as pl
from jax.experimental.pallas import tpu as pltpu
from jax.sharding import PartitionSpec as P

TILE = 64
PAIR = 2 * TILE
GROUP = 4
UNROLL = 4
VMEM_SLACK = 10 * 1024 * 1024
PARTS = (1, 1, 2)
ORDER = (0, 2, 1)
RANGES = ((0, 2), (2, 3))
OWN, OTHER = range(2)
BOUNDS = 3
STEPS = len(RANGES) + 1
LISTS = BOUNDS + 2 * STEPS


def bits(count):
    return max(1, (count - 1).bit_length())


def list_length(tiles, blocks):
    return tiles + len(RANGES) * ((GROUP - 1) * blocks + GROUP * UNROLL)


def group_lists(codes, keys, live, blocks, absent):
    n_lists, tiles = codes.shape
    n_keys = len(RANGES) * blocks
    order = jnp.arange(tiles, dtype=jnp.int32)
    key_range = jnp.arange(n_keys, dtype=jnp.int32)
    ranges = jnp.arange(STEPS, dtype=jnp.int32)
    mine = (keys[:, None, :] == key_range[None, :, None]) & live[:, None, :]
    groups = (jnp.sum(mine, axis=2, dtype=jnp.int32) + GROUP - 1) // GROUP
    in_range = key_range[:, None] // blocks == ranges[None, :]
    totals = jnp.sum(jnp.where(in_range, groups[:, :, None], 0), axis=1, dtype=jnp.int32)
    totals = (totals + UNROLL - 1) // UNROLL * UNROLL
    bounds = jnp.sum(
        jnp.where(ranges[:, None] < ranges[None, :], totals[:, :, None], 0), axis=1, dtype=jnp.int32
    )
    lower = (key_range[:, None] < key_range[None, :]) & (
        key_range[:, None] // blocks == key_range[None, :] // blocks
    )
    starts = jnp.sum(jnp.where(lower, groups[:, :, None], 0), axis=1, dtype=jnp.int32)
    starts += jnp.sum(jnp.where(in_range, bounds[:, None, :], 0), axis=2, dtype=jnp.int32)
    before = (
        (keys[:, :, None] == keys[:, None, :]) & live[:, :, None] & (order[:, None] < order[None, :])
    )
    entry = jnp.sum(before, axis=1, dtype=jnp.int32) + GROUP * jnp.sum(
        jnp.where(mine, starts[:, :, None], 0), axis=1, dtype=jnp.int32
    )
    entry = jnp.where(live, entry, -1)
    found = entry[:, :, None] == jnp.arange(list_length(tiles, blocks), dtype=jnp.int32)
    entries = absent + jnp.sum(
        jnp.where(found, codes[:, :, None] - absent, 0), axis=1, dtype=jnp.int32
    )
    return jnp.concatenate([bounds.reshape(-1), entries.reshape(-1)])


def group_loop(sizes, meta, values, proj, which, first, last, origin, product):
    tiles, segments, blocks = sizes
    begin, end = (meta[BOUNDS + STEPS * which + number] for number in (first, last))
    base = LISTS + which * list_length(tiles, blocks)

    def group(number):
        places = []
        for entry in range(GROUP):
            code = meta[base + GROUP * number + entry]
            index = jnp.maximum((code & ((1 << bits(tiles)) - 1)) - origin, 0)
            code = code >> bits(tiles)
            places.append((code & ((1 << bits(segments + 1)) - 1), values[index]))
            if entry == 0:
                block = code >> bits(segments + 1)
        lanes = pl.ds(pl.multiple_of(block * proj, proj), proj)
        return product(lanes, [at for at, tile in places], [tile for at, tile in places])

    def step(index, carry):
        sums = [group(begin + index * UNROLL + lane) for lane in range(UNROLL)]
        for additions in sums:
            for ref, rows, lanes, term in additions:
                ref[rows, lanes] += term
        return carry

    lax.fori_loop(0, (end - begin) // UNROLL, step, 0)


def join_pieces(meta, pieces, joined, firsts):
    end = 0
    for first, ref in zip(firsts, pieces):
        start, end = end, end + ref.shape[0]

        @pl.when(meta[2] > first)
        def copy(start=start, end=end, ref=ref):
            joined[start:end] = ref[...]


def rows_of(refs, lanes):
    return jnp.concatenate([ref[:, lanes] for ref in refs], axis=0)


def turn_waves(wave, turned, segments):
    for pair in range(segments // 2):
        values = wave[:, pair * PAIR : (pair + 1) * PAIR]
        turned[0, pair] = values
        turned[1, pair] = pltpu.roll(values.astype(jnp.float32), TILE, 1).astype(values.dtype)
    for way in range(2):
        turned[way, segments // 2] = jnp.zeros(turned.shape[2:], turned.dtype)


def project_kernel(sizes, firsts, spot, first, last, meta, wave, *refs):
    n_pieces = max(1, len(firsts))
    pieces, refs = refs[:n_pieces], refs[n_pieces:]
    turned, refs = refs[-1], refs[:-1]
    if not first:
        before, refs = refs[0], refs[1:]
    values = pieces[0]
    if n_pieces > 1:
        values, refs = refs[0], refs[1:]
        join_pieces(meta, pieces, values, firsts)
    total = refs[-1]
    total[...] = jnp.zeros_like(total) if first else before[...]
    every = slice(None)

    def product(lanes, segments, tiles):
        low = lax.broadcasted_iota(jnp.int32, turned.shape[2:], 1) < TILE
        waves = [
            jnp.where(
                low,
                turned[segments[at] & 1, segments[at] >> 1],
                turned[1 - (segments[at + 1] & 1), segments[at + 1] >> 1],
            )
            for at in range(0, GROUP, 2)
        ]
        term = jnp.dot(
            jnp.concatenate(waves, axis=1),
            jnp.concatenate(tiles, axis=0),
            preferred_element_type=jnp.float32,
        )
        return [(total, every, lanes, term)]

    begin, end = (meta[BOUNDS + STEPS * spot[0] + number] for number in spot[1:3])

    @pl.when(end > begin)
    def loop():
        turn_waves(wave, turned, sizes[1])
        group_loop(sizes, meta, values, values.shape[2], *spot, product)

    if last:
        outs = refs[:-1]
        rows = outs[0].shape[0]
        for d, out in enumerate(outs):
            start = 0 if len(outs) == 1 else pl.multiple_of((meta[0] ^ d) * rows, rows)
            out[...] = total[pl.ds(start, rows), :].astype(out.dtype)


def spread_kernel(sizes, n_rows, spots, meta, *refs):
    applied, refs = refs[:n_rows], refs[n_rows:]
    lists, refs = refs[: len(spots)], refs[len(spots) :]
    outs, field = refs[:-1], refs[-1]
    field[...] = jnp.zeros_like(field)
    every = slice(None)

    def product(lanes, segments, tiles):
        terms = lax.dot_general(
            jnp.concatenate(tiles, axis=0),
            rows_of(applied, lanes),
            (((1,), (1,)), ((), ())),
            preferred_element_type=jnp.float32,
        )
        return [
            (
                field,
                pl.ds(pl.multiple_of(at * TILE, TILE), TILE),
                every,
                terms[number * TILE : (number + 1) * TILE],
            )
            for number, at in enumerate(segments)
        ]

    for values, spot in zip(lists, spots):
        group_loop(sizes, meta, values, values.shape[2], *spot, product)
    for pair in range(sizes[1] // 2):
        points = slice(pair * PAIR, (pair + 1) * PAIR)
        values, start = field[points, :].T, 0
        for out in outs:
            out[:, points] = values[start : start + out.shape[0]].astype(out.dtype)
            start += out.shape[0]


WHOLE = pl.BlockSpec(memory_space=pltpu.VMEM)


def cost(us):
    return pl.CostEstimate(flops=1 + us * 10**9, bytes_accessed=1, transcendentals=0)


def join_small(blocks):
    return blocks if blocks[0].shape[0] % 16 == 0 else [jnp.concatenate(blocks)]


def split_small(blocks, count):
    return blocks if len(blocks) == count else jnp.split(blocks[0], count)


def vmem(scratch):
    size = sum(math.prod(ref.shape) * jnp.dtype(ref.dtype).itemsize for ref in scratch)
    return pltpu.CompilerParams(vmem_limit_bytes=size + VMEM_SLACK)


def project(
    sizes, meta, wave, pieces, count, width, spot, firsts=(), total=None, last=False, us=0
):
    rows = wave.shape[0]
    operands = [wave, *pieces] + ([] if total is None else [total])
    shapes = []
    if len(pieces) > 1:
        held = sum(piece.shape[0] for piece in pieces)
        shapes.append(jax.ShapeDtypeStruct((held,) + pieces[0].shape[1:], jnp.bfloat16))
    scratch = [pltpu.VMEM((2, sizes[1] // 2 + 1, rows, PAIR), jnp.bfloat16)]
    if last:
        outs = count if rows // count % 16 == 0 else 1
        shapes += [jax.ShapeDtypeStruct((rows // outs, width), jnp.bfloat16)] * outs
        scratch = [pltpu.VMEM((rows, width), jnp.float32)] + scratch
    else:
        shapes.append(jax.ShapeDtypeStruct((rows, width), jnp.float32))
    result = pl.pallas_call(
        functools.partial(project_kernel, sizes, firsts, spot, total is None, last),
        grid_spec=pltpu.PrefetchScalarGridSpec(
            num_scalar_prefetch=1,
            grid=(1,),
            in_specs=[WHOLE] * len(operands),
            out_specs=[WHOLE] * len(shapes),
            scratch_shapes=scratch,
        ),
        out_shape=shapes,
        compiler_params=vmem(scratch),
        cost_estimate=cost(us),
    )(meta, *operands)
    joined, result = (result[0], result[1:]) if len(pieces) > 1 else (pieces[0], result)
    return (list(result) if last else result[0]), joined


def spread(sizes, meta, applied, lists, points, spots):
    count = len(applied)
    applied = join_small(applied)
    rows = sum(block.shape[0] for block in applied)
    scratch = [pltpu.VMEM((points + TILE, rows), jnp.float32)]
    result = pl.pallas_call(
        functools.partial(spread_kernel, sizes, len(applied), spots),
        grid_spec=pltpu.PrefetchScalarGridSpec(
            num_scalar_prefetch=1,
            grid=(1,),
            in_specs=[WHOLE] * (len(applied) + len(lists)),
            out_specs=[WHOLE] * len(applied),
            scratch_shapes=scratch,
        ),
        out_shape=[
            jax.ShapeDtypeStruct((block.shape[0], points), jnp.bfloat16) for block in applied
        ],
        compiler_params=vmem(scratch),
        cost_estimate=cost(8),
    )(meta, *applied, *lists)
    return split_small(result, count)


def two_parts(values):
    high = values.astype(jnp.bfloat16)
    return high, (values - high.astype(jnp.float32)).astype(jnp.bfloat16)


def couple_kernel(high_ref, low_ref, *refs):
    parts, out_ref = refs[:-1], refs[-1]
    blocks, proj, unused = high_ref.shape
    for block in range(blocks):
        lanes = slice(block * proj, (block + 1) * proj)
        total = parts[0][:, lanes].astype(jnp.float32)
        for part in parts[1:]:
            total += part[:, lanes].astype(jnp.float32)
        high, low = two_parts(total)
        result = jnp.dot(high, high_ref[block], preferred_element_type=jnp.float32)
        result += jnp.dot(high, low_ref[block], preferred_element_type=jnp.float32)
        result += jnp.dot(low, high_ref[block], preferred_element_type=jnp.float32)
        out_ref[:, lanes] = result.astype(out_ref.dtype)


def couple(parts, high, low):
    return pl.pallas_call(
        couple_kernel,
        in_specs=[WHOLE] * (2 + len(parts)),
        out_specs=WHOLE,
        out_shape=jax.ShapeDtypeStruct(parts[0].shape, jnp.bfloat16),
        compiler_params=vmem([]),
        cost_estimate=cost(6),
    )(high, low, *parts)


def coupling_matrix(coupling):
    blocks, atoms, width, unused = coupling.shape
    proj = atoms * width
    wide = jnp.tile(coupling.reshape(blocks, proj, width), (1, 1, atoms))
    same = jnp.arange(proj)[:, None] // width == jnp.arange(proj)[None, :] // width
    return jnp.where(same[None], wide, 0.0)


def body(n_grid, wavefunctions, tile_segment, tile_block, tile_count, projectors, coupling):
    half = n_grid // 2
    bands, npts = wavefunctions.shape
    points = npts // n_grid
    tiles = projectors.shape[0]
    width = coupling.shape[0] * projectors.shape[2]
    index = lax.axis_index("grid")
    side, place = index // half, index % half
    group, core = lax.axis_index("groups"), lax.axis_index("band")
    partners = [(i, (i + half) % n_grid) for i in range(n_grid)]
    pools = [list(range(half)), list(range(half, n_grid))]
    swap = [(0, 1), (1, 0)]

    def exchange(blocks):
        return [blocks[0]] + [
            lax.ppermute(
                blocks[d], "grid", [(i, i // half * half + (i % half ^ d)) for i in range(n_grid)]
            )
            for d in range(1, half)
        ]

    def to_bricks(which, after=None):
        part = lax.dynamic_slice_in_dim(wavefunctions, which * half * points, half * points, 1)
        part = lax.optimization_barrier((part, after))[0]
        return lax.all_to_all(
            part, "grid", split_axis=1, concat_axis=0, tiled=True, axis_index_groups=pools
        )

    segments, blocks = points // TILE, coupling.shape[0]
    sizes = (tiles, segments, blocks)
    slots = jnp.arange(tiles, dtype=jnp.int32)
    starts = [tiles * sum(PARTS[:number]) // sum(PARTS) for number in range(len(PARTS) + 1)]
    held, range_of, bases = slots, 0, [0]
    for part in ORDER:
        start, end = starts[part], starts[part + 1]
        share = (end - start) // 4
        quarter, rest = (slots - start) // share, (slots - start) % share
        at = bases[-1] + rest + share * ((quarter // 2 ^ group) + 2 * (quarter % 2 ^ core))
        inside = (slots >= start) & (slots < end)
        held = jnp.where(inside, at, held)
        later = sum(len(bases) > first for first, end in RANGES[1:])
        range_of += jnp.where(inside, later, 0)
        bases.append(bases[-1] + end - start)

    matrix = two_parts(coupling_matrix(coupling))

    neighbours = [
        (i, i // half * half + (i % half ^ max(1, half // 2))) for i in range(n_grid)
    ]

    def quarter_of(source, start, end):
        share = (end - start) // 4
        return lax.dynamic_slice_in_dim(source, start + (2 * group + core) * share, share, 0)

    upper = quarter_of(projectors, starts[2], starts[3])
    middle = upper.shape[0] // 2
    taken = lax.ppermute(upper[middle:], "grid", neighbours)
    upper = jnp.where(tile_count[0] > starts[2], upper[:middle], taken)
    upper = lax.ppermute(upper, "grid", partners)
    source = lax.optimization_barrier((projectors, taken))[0]
    first, second = (quarter_of(source, starts[at], starts[at + 1]) for at in (0, 1))
    first, second, late = lax.optimization_barrier((first, second, upper))
    first = lax.ppermute(first, "grid", partners)
    second = lax.ppermute(second, "grid", partners)
    rest = lax.ppermute(upper, "grid", neighbours)

    own_wave = to_bricks(side)
    other_wave = to_bricks(1 - side, upper)
    numbers = jnp.stack([tile_segment, tile_block, jnp.broadcast_to(tile_count, (tiles,))])
    numbers = lax.optimization_barrier((numbers, taken))[0]
    others = lax.ppermute(numbers, "grid", partners)
    absent = segments << bits(tiles)
    segment, block = (jnp.stack([numbers[i], others[i]]) for i in (0, 1))
    codes = jnp.stack([slots, held])
    codes += (segment + (block << bits(segments + 1))) << bits(tiles)
    live = slots < jnp.stack([numbers[2], others[2]])
    keys = block + blocks * jnp.stack([jnp.zeros_like(slots), range_of])
    meta = jnp.concatenate(
        [
            jnp.stack([place, numbers[2, 0], others[2, 0]]),
            group_lists(codes, keys, live, blocks, absent),
        ]
    )

    own_wave = lax.optimization_barrier((own_wave, upper))[0]
    own_spot = (OWN, 0, len(RANGES), 0)
    total, own_tiles = project(
        sizes, meta, own_wave, [projectors], half, width, own_spot, us=5
    )

    def over_groups(block):
        return lax.ppermute(block, "groups", swap)

    def to_core(blocks):
        return blocks + [lax.ppermute(block, "band", swap) for block in blocks]

    held_upper = [upper, rest, over_groups(upper)]
    held_first = [first, over_groups(first)]
    rest, late = lax.optimization_barrier((rest, held_upper[-1]))
    held_upper.append(over_groups(rest))
    sent, late, matrix, total = lax.optimization_barrier(
        (second, (held_upper, held_first), matrix, total)
    )
    held_second = [second, over_groups(sent)]
    pieces = [to_core(blocks) for blocks in (held_first, held_upper)]

    joined, other_spots = [], []
    for number, (first, end) in enumerate(RANGES):
        other_spots.append((OTHER, number, number + 1, bases[first]))
        last = end == len(PARTS)
        if last:
            held_second, total = lax.optimization_barrier((held_second, total))
            pieces.append(to_core(held_second))
        total, tiles_held = project(
            sizes,
            meta,
            other_wave,
            sum(pieces[first:end], []),
            half,
            width,
            other_spots[-1],
            sum(([starts[ORDER[at]]] * len(pieces[at]) for at in range(first, end)), []),
            total,
            last=last,
            us=0 if last else 8,
        )
        joined.append(tiles_held)
    if len(total) < half:
        total = [lax.dynamic_slice_in_dim(total[0], (place ^ d) * bands, bands, 0) for d in range(half)]

    applied = couple(exchange(total), *matrix)
    applied = exchange([applied] * half)

    result = jnp.zeros((bands, npts), jnp.bfloat16)
    for which, field in (
        (1 - side, spread(sizes, meta, applied, joined, points, other_spots)),
        (side, spread(sizes, meta, applied, [own_tiles], points, [own_spot])),
    ):
        for d, block in enumerate(exchange(field)):
            start = (which * half + (place ^ d)) * points
            result = lax.dynamic_update_slice_in_dim(result, block, start, 1)
    return result


def solution(mesh):
    in_specs = (
        P(("groups", "grid", "band"), None),
        P("grid"),
        P("grid"),
        P("grid"),
        P("grid", None, None),
        P(),
    )
    out_specs = P(("groups", "grid", "band"), None)
    return jax.shard_map(
        functools.partial(body, mesh.shape["grid"]),
        mesh=mesh,
        in_specs=in_specs,
        out_specs=out_specs,
        check_vma=False,
    )
```

```python
import functools
import math

import jax
import jax.numpy as jnp
from jax import lax
from jax.experimental import pallas as pl
from jax.experimental.pallas import tpu as pltpu
from jax.sharding import PartitionSpec as P

TILE = 64
PAIR = 2 * TILE
GROUP = 4
UNROLL = 8
VMEM_SLACK = 10 * 1024 * 1024
PARTS = (15, 17, 16)
RANGES = ((0, 2), (2, 3))
OWN, OTHER = range(2)
BOUNDS = 3
STEPS = len(RANGES) + 1
LISTS = BOUNDS + 2 * STEPS


def bits(count):
    return max(1, (count - 1).bit_length())


def list_length(tiles, blocks):
    return tiles + len(RANGES) * ((GROUP - 1) * blocks + GROUP * UNROLL)


def group_lists(codes, keys, live, blocks, absent):
    n_lists, tiles = codes.shape
    n_keys = len(RANGES) * blocks
    order = jnp.arange(tiles, dtype=jnp.int32)
    key_range = jnp.arange(n_keys, dtype=jnp.int32)
    ranges = jnp.arange(STEPS, dtype=jnp.int32)
    mine = (keys[:, None, :] == key_range[None, :, None]) & live[:, None, :]
    groups = (jnp.sum(mine, axis=2, dtype=jnp.int32) + GROUP - 1) // GROUP
    in_range = key_range[:, None] // blocks == ranges[None, :]
    totals = jnp.sum(jnp.where(in_range, groups[:, :, None], 0), axis=1, dtype=jnp.int32)
    totals = (totals + UNROLL - 1) // UNROLL * UNROLL
    bounds = jnp.sum(
        jnp.where(ranges[:, None] < ranges[None, :], totals[:, :, None], 0), axis=1, dtype=jnp.int32
    )
    lower = (key_range[:, None] < key_range[None, :]) & (
        key_range[:, None] // blocks == key_range[None, :] // blocks
    )
    starts = jnp.sum(jnp.where(lower, groups[:, :, None], 0), axis=1, dtype=jnp.int32)
    starts += jnp.sum(jnp.where(in_range, bounds[:, None, :], 0), axis=2, dtype=jnp.int32)
    before = (
        (keys[:, :, None] == keys[:, None, :]) & live[:, :, None] & (order[:, None] < order[None, :])
    )
    entry = jnp.sum(before, axis=1, dtype=jnp.int32) + GROUP * jnp.sum(
        jnp.where(mine, starts[:, :, None], 0), axis=1, dtype=jnp.int32
    )
    entry = jnp.where(live, entry, -1)
    found = entry[:, :, None] == jnp.arange(list_length(tiles, blocks), dtype=jnp.int32)
    entries = absent + jnp.sum(
        jnp.where(found, codes[:, :, None] - absent, 0), axis=1, dtype=jnp.int32
    )
    return jnp.concatenate([bounds.reshape(-1), entries.reshape(-1)])


def group_loop(sizes, meta, values, proj, which, first, last, origin, product):
    tiles, segments, blocks = sizes
    begin, end = (meta[BOUNDS + STEPS * which + number] for number in (first, last))
    base = LISTS + which * list_length(tiles, blocks)

    def group(number):
        places = []
        for entry in range(GROUP):
            code = meta[base + GROUP * number + entry]
            index = jnp.maximum((code & ((1 << bits(tiles)) - 1)) - origin, 0)
            code = code >> bits(tiles)
            places.append((code & ((1 << bits(segments + 1)) - 1), values[index]))
            if entry == 0:
                block = code >> bits(segments + 1)
        lanes = pl.ds(pl.multiple_of(block * proj, proj), proj)
        return product(lanes, [at for at, tile in places], [tile for at, tile in places])

    def step(index, carry):
        sums = [group(begin + index * UNROLL + lane) for lane in range(UNROLL)]
        for additions in sums:
            for ref, rows, lanes, term in additions:
                ref[rows, lanes] += term
        return carry

    lax.fori_loop(0, (end - begin) // UNROLL, step, 0)


def join_pieces(meta, pieces, joined, first):
    end = 0
    for number, ref in enumerate(pieces):
        start, end = end, end + ref.shape[0]

        @pl.when(meta[2] > first + start - number % 4 * ref.shape[0])
        def copy(start=start, end=end, ref=ref):
            joined[start:end] = ref[...]


def rows_of(refs, lanes):
    return jnp.concatenate([ref[:, lanes] for ref in refs], axis=0)


def turn_waves(wave, turned, segments):
    for pair in range(segments // 2):
        values = wave[:, pair * PAIR : (pair + 1) * PAIR]
        turned[0, pair] = values
        turned[1, pair] = pltpu.roll(values.astype(jnp.float32), TILE, 1).astype(values.dtype)
    for way in range(2):
        turned[way, segments // 2] = jnp.zeros(turned.shape[2:], turned.dtype)


def project_kernel(sizes, n_pieces, spot, first, last, meta, wave, *refs):
    pieces, refs = refs[:n_pieces], refs[n_pieces:]
    turned, refs = refs[-1], refs[:-1]
    if not first:
        before, refs = refs[0], refs[1:]
    values = pieces[0]
    if n_pieces > 1:
        values, refs = refs[-1], refs[:-1]
        join_pieces(meta, pieces, values, spot[-1])
    total = refs[-1]
    total[...] = jnp.zeros_like(total) if first else before[...]
    every = slice(None)

    def product(lanes, segments, tiles):
        low = lax.broadcasted_iota(jnp.int32, turned.shape[2:], 1) < TILE
        waves = [
            jnp.where(
                low,
                turned[segments[at] & 1, segments[at] >> 1],
                turned[1 - (segments[at + 1] & 1), segments[at + 1] >> 1],
            )
            for at in range(0, GROUP, 2)
        ]
        term = jnp.dot(
            jnp.concatenate(waves, axis=1),
            jnp.concatenate(tiles, axis=0),
            preferred_element_type=jnp.float32,
        )
        return [(total, every, lanes, term)]

    @pl.when(meta[1 + spot[0]] > spot[-1])
    def loop():
        turn_waves(wave, turned, sizes[1])
        group_loop(sizes, meta, values, values.shape[2], *spot, product)

    if last:
        outs = refs[:-1]
        rows = outs[0].shape[0]
        for d, out in enumerate(outs):
            start = 0 if len(outs) == 1 else pl.multiple_of((meta[0] ^ d) * rows, rows)
            out[...] = total[pl.ds(start, rows), :].astype(out.dtype)


def spread_kernel(sizes, n_rows, n_pieces, which, meta, *refs):
    applied, refs = refs[:n_rows], refs[n_rows:]
    pieces, refs = refs[:n_pieces], refs[n_pieces:]
    values = pieces[0]
    if n_pieces > 1:
        values, refs = refs[-1], refs[:-1]
        join_pieces(meta, pieces, values, 0)
    outs, field = refs[:-1], refs[-1]
    field[...] = jnp.zeros_like(field)
    every = slice(None)

    def product(lanes, segments, tiles):
        terms = lax.dot_general(
            jnp.concatenate(tiles, axis=0),
            rows_of(applied, lanes),
            (((1,), (1,)), ((), ())),
            preferred_element_type=jnp.float32,
        )
        return [
            (
                field,
                pl.ds(pl.multiple_of(at * TILE, TILE), TILE),
                every,
                terms[number * TILE : (number + 1) * TILE],
            )
            for number, at in enumerate(segments)
        ]

    group_loop(sizes, meta, values, values.shape[2], which, 0, len(RANGES), 0, product)
    for pair in range(sizes[1] // 2):
        points = slice(pair * PAIR, (pair + 1) * PAIR)
        values, start = field[points, :].T, 0
        for out in outs:
            out[:, points] = values[start : start + out.shape[0]].astype(out.dtype)
            start += out.shape[0]


WHOLE = pl.BlockSpec(memory_space=pltpu.VMEM)


def cost(us):
    return pl.CostEstimate(flops=1 + us * 10**9, bytes_accessed=1, transcendentals=0)


def join_small(blocks):
    return blocks if blocks[0].shape[0] % 16 == 0 else [jnp.concatenate(blocks)]


def split_small(blocks, count):
    return blocks if len(blocks) == count else jnp.split(blocks[0], count)


def vmem(scratch):
    size = sum(math.prod(ref.shape) * jnp.dtype(ref.dtype).itemsize for ref in scratch)
    return pltpu.CompilerParams(vmem_limit_bytes=size + VMEM_SLACK)


def joined_shape(pieces):
    if len(pieces) == 1:
        return []
    count = sum(piece.shape[0] for piece in pieces)
    return [pltpu.VMEM((count,) + pieces[0].shape[1:], jnp.bfloat16)]


def project(sizes, meta, wave, pieces, count, width, spot, total=None, last=False, us=0):
    rows = wave.shape[0]
    operands = [wave, *pieces] + ([] if total is None else [total])
    scratch = joined_shape(pieces)
    scratch.append(pltpu.VMEM((2, sizes[1] // 2 + 1, rows, PAIR), jnp.bfloat16))
    if last:
        outs = count if rows // count % 16 == 0 else 1
        shapes = [jax.ShapeDtypeStruct((rows // outs, width), jnp.bfloat16)] * outs
        scratch = [pltpu.VMEM((rows, width), jnp.float32)] + scratch
    else:
        shapes = [jax.ShapeDtypeStruct((rows, width), jnp.float32)]
    result = pl.pallas_call(
        functools.partial(project_kernel, sizes, len(pieces), spot, total is None, last),
        grid_spec=pltpu.PrefetchScalarGridSpec(
            num_scalar_prefetch=1,
            grid=(1,),
            in_specs=[WHOLE] * len(operands),
            out_specs=[WHOLE] * len(shapes),
            scratch_shapes=scratch,
        ),
        out_shape=shapes,
        compiler_params=vmem(scratch),
        cost_estimate=cost(us),
    )(meta, *operands)
    return list(result) if last else result[0]


def spread(sizes, meta, applied, pieces, points, which):
    count = len(applied)
    applied = join_small(applied)
    rows = sum(block.shape[0] for block in applied)
    scratch = [pltpu.VMEM((points + TILE, rows), jnp.float32)] + joined_shape(pieces)
    result = pl.pallas_call(
        functools.partial(spread_kernel, sizes, len(applied), len(pieces), which),
        grid_spec=pltpu.PrefetchScalarGridSpec(
            num_scalar_prefetch=1,
            grid=(1,),
            in_specs=[WHOLE] * (len(applied) + len(pieces)),
            out_specs=[WHOLE] * len(applied),
            scratch_shapes=scratch,
        ),
        out_shape=[
            jax.ShapeDtypeStruct((block.shape[0], points), jnp.bfloat16) for block in applied
        ],
        compiler_params=vmem(scratch),
        cost_estimate=cost(0),
    )(meta, *applied, *pieces)
    return split_small(result, count)


def two_parts(values):
    high = values.astype(jnp.bfloat16)
    return high, (values - high.astype(jnp.float32)).astype(jnp.bfloat16)


def couple_kernel(high_ref, low_ref, *refs):
    parts, out_ref = refs[:-1], refs[-1]
    blocks, proj, unused = high_ref.shape
    for block in range(blocks):
        lanes = slice(block * proj, (block + 1) * proj)
        total = parts[0][:, lanes].astype(jnp.float32)
        for part in parts[1:]:
            total += part[:, lanes].astype(jnp.float32)
        high, low = two_parts(total)
        result = jnp.dot(high, high_ref[block], preferred_element_type=jnp.float32)
        result += jnp.dot(high, low_ref[block], preferred_element_type=jnp.float32)
        result += jnp.dot(low, high_ref[block], preferred_element_type=jnp.float32)
        out_ref[:, lanes] = result.astype(out_ref.dtype)


def couple(parts, high, low):
    return pl.pallas_call(
        couple_kernel,
        in_specs=[WHOLE] * (2 + len(parts)),
        out_specs=WHOLE,
        out_shape=jax.ShapeDtypeStruct(parts[0].shape, jnp.bfloat16),
        compiler_params=vmem([]),
        cost_estimate=cost(0),
    )(high, low, *parts)


def coupling_matrix(coupling):
    blocks, atoms, width, unused = coupling.shape
    proj = atoms * width
    wide = jnp.tile(coupling.reshape(blocks, proj, width), (1, 1, atoms))
    same = jnp.arange(proj)[:, None] // width == jnp.arange(proj)[None, :] // width
    return jnp.where(same[None], wide, 0.0)


def body(n_grid, wavefunctions, tile_segment, tile_block, tile_count, projectors, coupling):
    half = n_grid // 2
    bands, npts = wavefunctions.shape
    points = npts // n_grid
    tiles = projectors.shape[0]
    width = coupling.shape[0] * projectors.shape[2]
    index = lax.axis_index("grid")
    side, place = index // half, index % half
    group, core = lax.axis_index("groups"), lax.axis_index("band")
    partners = [(i, (i + half) % n_grid) for i in range(n_grid)]
    pools = [list(range(half)), list(range(half, n_grid))]
    swap = [(0, 1), (1, 0)]

    def exchange(blocks):
        return [blocks[0]] + [
            lax.ppermute(
                blocks[d], "grid", [(i, i // half * half + (i % half ^ d)) for i in range(n_grid)]
            )
            for d in range(1, half)
        ]

    def to_bricks(which):
        part = lax.dynamic_slice_in_dim(wavefunctions, which * half * points, half * points, 1)
        return lax.all_to_all(
            part, "grid", split_axis=1, concat_axis=0, tiled=True, axis_index_groups=pools
        )

    segments, blocks = points // TILE, coupling.shape[0]
    sizes = (tiles, segments, blocks)
    slots = jnp.arange(tiles, dtype=jnp.int32)
    starts = [tiles * sum(PARTS[:number]) // sum(PARTS) for number in range(len(PARTS) + 1)]
    held, range_of = slots, 0
    for start, end in zip(starts, starts[1:]):
        share = (end - start) // 4
        quarter, rest = (slots - start) // share, (slots - start) % share
        at = start + rest + share * ((quarter // 2 ^ group) + 2 * (quarter % 2 ^ core))
        held = jnp.where((slots >= start) & (slots < end), at, held)
    for first, end in RANGES[1:]:
        range_of += jnp.where(slots >= starts[first], 1, 0)

    own_wave = to_bricks(side)
    other_wave = to_bricks(1 - side)
    matrix = two_parts(coupling_matrix(coupling))

    arrived, pieces, across = [], [], None
    source = projectors
    for number, (start, end) in enumerate(zip(starts, starts[1:])):
        share = (end - start) // 4
        start += (2 * group + core) * share
        sent = lax.dynamic_slice_in_dim(source, start, share, 0)
        if number == 0:
            sent, source = lax.optimization_barrier((sent, source))
        if number > 0:
            sent = lax.optimization_barrier((sent, arrived[0]))[0]
        arrived.append(lax.ppermute(sent, "grid", partners))

    numbers = jnp.stack([tile_segment, tile_block, jnp.broadcast_to(tile_count, (tiles,))])
    numbers = lax.optimization_barrier((numbers, arrived[0]))[0]
    others = lax.ppermute(numbers, "grid", partners)
    absent = segments << bits(tiles)
    segment, block = (jnp.stack([numbers[i], others[i]]) for i in (0, 1))
    codes = jnp.stack([slots, held])
    codes += (segment + (block << bits(segments + 1))) << bits(tiles)
    live = slots < jnp.stack([numbers[2], others[2]])
    keys = block + blocks * jnp.stack([jnp.zeros_like(slots), range_of])
    meta = jnp.concatenate(
        [
            jnp.stack([place, numbers[2, 0], others[2, 0]]),
            group_lists(codes, keys, live, blocks, absent),
        ]
    )

    own_wave = lax.optimization_barrier((own_wave, arrived[-1]))[0]
    own_spot = (OWN, 0, len(RANGES), 0)
    total = project(sizes, meta, own_wave, [projectors], half, width, own_spot, us=10)
    for number, mine in enumerate(arrived):
        sent = mine
        if number == 1:
            sent, across, matrix = lax.optimization_barrier((sent, across, matrix))
        if number == 2:
            sent, across, other_wave = lax.optimization_barrier((sent, across, other_wave))
        across = lax.ppermute(sent, "groups", swap)
        pieces += [mine, across]
        pieces += [lax.ppermute(mine, "band", swap), lax.ppermute(across, "band", swap)]

    for number, (first, end) in enumerate(RANGES):
        last = end == len(PARTS)
        total = project(
            sizes,
            meta,
            other_wave,
            pieces[4 * first : 4 * end],
            half,
            width,
            (OTHER, number, number + 1, starts[first]),
            total,
            last=last,
            us=0 if last else 8,
        )
    if len(total) < half:
        total = [lax.dynamic_slice_in_dim(total[0], (place ^ d) * bands, bands, 0) for d in range(half)]

    applied = couple(exchange(total), *matrix)
    applied = exchange([applied] * half)

    result = jnp.zeros((bands, npts), jnp.bfloat16)
    for which, field in (
        (1 - side, spread(sizes, meta, applied, pieces, points, OTHER)),
        (side, spread(sizes, meta, applied, [projectors], points, OWN)),
    ):
        for d, block in enumerate(exchange(field)):
            start = (which * half + (place ^ d)) * points
            result = lax.dynamic_update_slice_in_dim(result, block, start, 1)
    return result


def solution(mesh):
    in_specs = (
        P(("groups", "grid", "band"), None),
        P("grid"),
        P("grid"),
        P("grid"),
        P("grid", None, None),
        P(),
    )
    out_specs = P(("groups", "grid", "band"), None)
    return jax.shard_map(
        functools.partial(body, mesh.shape["grid"]),
        mesh=mesh,
        in_specs=in_specs,
        out_specs=out_specs,
        check_vma=False,
    )
```

```python
import functools
import math

import jax
import jax.numpy as jnp
from jax import lax
from jax.experimental import pallas as pl
from jax.experimental.pallas import tpu as pltpu
from jax.sharding import PartitionSpec as P

TILE = 64
PAIR = 2 * TILE
GROUP = 4
UNROLL = 8
VMEM_SLACK = 10 * 1024 * 1024
PARTS = (19, 17, 12)
RANGES = ((0, 2), (2, 3))
OWN, OTHER = range(2)
BOUNDS = 3
STEPS = len(RANGES) + 1
LISTS = BOUNDS + 2 * STEPS


def bits(count):
    return max(1, (count - 1).bit_length())


def list_length(tiles, blocks):
    return tiles + len(RANGES) * ((GROUP - 1) * blocks + GROUP * UNROLL)


def group_lists(codes, keys, live, blocks, absent):
    n_lists, tiles = codes.shape
    n_keys = len(RANGES) * blocks
    order = jnp.arange(tiles, dtype=jnp.int32)
    key_range = jnp.arange(n_keys, dtype=jnp.int32)
    ranges = jnp.arange(STEPS, dtype=jnp.int32)
    mine = (keys[:, None, :] == key_range[None, :, None]) & live[:, None, :]
    groups = (jnp.sum(mine, axis=2, dtype=jnp.int32) + GROUP - 1) // GROUP
    in_range = key_range[:, None] // blocks == ranges[None, :]
    totals = jnp.sum(jnp.where(in_range, groups[:, :, None], 0), axis=1, dtype=jnp.int32)
    totals = (totals + UNROLL - 1) // UNROLL * UNROLL
    bounds = jnp.sum(
        jnp.where(ranges[:, None] < ranges[None, :], totals[:, :, None], 0), axis=1, dtype=jnp.int32
    )
    lower = (key_range[:, None] < key_range[None, :]) & (
        key_range[:, None] // blocks == key_range[None, :] // blocks
    )
    starts = jnp.sum(jnp.where(lower, groups[:, :, None], 0), axis=1, dtype=jnp.int32)
    starts += jnp.sum(jnp.where(in_range, bounds[:, None, :], 0), axis=2, dtype=jnp.int32)
    before = (
        (keys[:, :, None] == keys[:, None, :]) & live[:, :, None] & (order[:, None] < order[None, :])
    )
    entry = jnp.sum(before, axis=1, dtype=jnp.int32) + GROUP * jnp.sum(
        jnp.where(mine, starts[:, :, None], 0), axis=1, dtype=jnp.int32
    )
    entry = jnp.where(live, entry, -1)
    found = entry[:, :, None] == jnp.arange(list_length(tiles, blocks), dtype=jnp.int32)
    entries = absent + jnp.sum(
        jnp.where(found, codes[:, :, None] - absent, 0), axis=1, dtype=jnp.int32
    )
    return jnp.concatenate([bounds.reshape(-1), entries.reshape(-1)])


def group_loop(sizes, meta, values, proj, which, first, last, origin, product):
    tiles, segments, blocks = sizes
    begin, end = (meta[BOUNDS + STEPS * which + number] for number in (first, last))
    base = LISTS + which * list_length(tiles, blocks)

    def group(number):
        places = []
        for entry in range(GROUP):
            code = meta[base + GROUP * number + entry]
            index = jnp.maximum((code & ((1 << bits(tiles)) - 1)) - origin, 0)
            code = code >> bits(tiles)
            places.append((code & ((1 << bits(segments + 1)) - 1), values[index]))
            if entry == 0:
                block = code >> bits(segments + 1)
        lanes = pl.ds(pl.multiple_of(block * proj, proj), proj)
        return product(lanes, [at for at, tile in places], [tile for at, tile in places])

    def step(index, carry):
        sums = [group(begin + index * UNROLL + lane) for lane in range(UNROLL)]
        for additions in sums:
            for ref, rows, lanes, term in additions:
                ref[rows, lanes] += term
        return carry

    lax.fori_loop(0, (end - begin) // UNROLL, step, 0)


def join_pieces(meta, pieces, joined, first):
    end = 0
    for number, ref in enumerate(pieces):
        start, end = end, end + ref.shape[0]

        @pl.when(meta[2] > first + start - number % 4 * ref.shape[0])
        def copy(start=start, end=end, ref=ref):
            joined[start:end] = ref[...]


def rows_of(refs, lanes):
    return jnp.concatenate([ref[:, lanes] for ref in refs], axis=0)


def turn_waves(wave, turned, segments):
    for pair in range(segments // 2):
        values = wave[:, pair * PAIR : (pair + 1) * PAIR]
        turned[0, pair] = values
        turned[1, pair] = pltpu.roll(values.astype(jnp.float32), TILE, 1).astype(values.dtype)
    for way in range(2):
        turned[way, segments // 2] = jnp.zeros(turned.shape[2:], turned.dtype)


def project_kernel(sizes, n_pieces, spot, first, last, meta, wave, *refs):
    pieces, refs = refs[:n_pieces], refs[n_pieces:]
    turned, refs = refs[-1], refs[:-1]
    if not first:
        before, refs = refs[0], refs[1:]
    values = pieces[0]
    if n_pieces > 1:
        values, refs = refs[-1], refs[:-1]
        join_pieces(meta, pieces, values, spot[-1])
    total = refs[-1]
    total[...] = jnp.zeros_like(total) if first else before[...]
    every = slice(None)

    def product(lanes, segments, tiles):
        low = lax.broadcasted_iota(jnp.int32, turned.shape[2:], 1) < TILE
        waves = [
            jnp.where(
                low,
                turned[segments[at] & 1, segments[at] >> 1],
                turned[1 - (segments[at + 1] & 1), segments[at + 1] >> 1],
            )
            for at in range(0, GROUP, 2)
        ]
        term = jnp.dot(
            jnp.concatenate(waves, axis=1),
            jnp.concatenate(tiles, axis=0),
            preferred_element_type=jnp.float32,
        )
        return [(total, every, lanes, term)]

    @pl.when(meta[1 + spot[0]] > spot[-1])
    def loop():
        turn_waves(wave, turned, sizes[1])
        group_loop(sizes, meta, values, values.shape[2], *spot, product)

    if last:
        outs = refs[:-1]
        rows = outs[0].shape[0]
        for d, out in enumerate(outs):
            start = 0 if len(outs) == 1 else pl.multiple_of((meta[0] ^ d) * rows, rows)
            out[...] = total[pl.ds(start, rows), :].astype(out.dtype)


def spread_kernel(sizes, n_rows, n_pieces, which, meta, *refs):
    applied, refs = refs[:n_rows], refs[n_rows:]
    pieces, refs = refs[:n_pieces], refs[n_pieces:]
    values = pieces[0]
    if n_pieces > 1:
        values, refs = refs[-1], refs[:-1]
        join_pieces(meta, pieces, values, 0)
    outs, field = refs[:-1], refs[-1]
    field[...] = jnp.zeros_like(field)
    every = slice(None)

    def product(lanes, segments, tiles):
        terms = lax.dot_general(
            jnp.concatenate(tiles, axis=0),
            rows_of(applied, lanes),
            (((1,), (1,)), ((), ())),
            preferred_element_type=jnp.float32,
        )
        return [
            (
                field,
                pl.ds(pl.multiple_of(at * TILE, TILE), TILE),
                every,
                terms[number * TILE : (number + 1) * TILE],
            )
            for number, at in enumerate(segments)
        ]

    group_loop(sizes, meta, values, values.shape[2], which, 0, len(RANGES), 0, product)
    for pair in range(sizes[1] // 2):
        points = slice(pair * PAIR, (pair + 1) * PAIR)
        values, start = field[points, :].T, 0
        for out in outs:
            out[:, points] = values[start : start + out.shape[0]].astype(out.dtype)
            start += out.shape[0]


WHOLE = pl.BlockSpec(memory_space=pltpu.VMEM)


def cost(us):
    return pl.CostEstimate(flops=1 + us * 10**9, bytes_accessed=1, transcendentals=0)


def join_small(blocks):
    return blocks if blocks[0].shape[0] % 16 == 0 else [jnp.concatenate(blocks)]


def split_small(blocks, count):
    return blocks if len(blocks) == count else jnp.split(blocks[0], count)


def vmem(scratch):
    size = sum(math.prod(ref.shape) * jnp.dtype(ref.dtype).itemsize for ref in scratch)
    return pltpu.CompilerParams(vmem_limit_bytes=size + VMEM_SLACK)


def joined_shape(pieces):
    if len(pieces) == 1:
        return []
    count = sum(piece.shape[0] for piece in pieces)
    return [pltpu.VMEM((count,) + pieces[0].shape[1:], jnp.bfloat16)]


def project(sizes, meta, wave, pieces, count, width, spot, total=None, last=False, us=0):
    rows = wave.shape[0]
    operands = [wave, *pieces] + ([] if total is None else [total])
    scratch = joined_shape(pieces)
    scratch.append(pltpu.VMEM((2, sizes[1] // 2 + 1, rows, PAIR), jnp.bfloat16))
    if last:
        outs = count if rows // count % 16 == 0 else 1
        shapes = [jax.ShapeDtypeStruct((rows // outs, width), jnp.bfloat16)] * outs
        scratch = [pltpu.VMEM((rows, width), jnp.float32)] + scratch
    else:
        shapes = [jax.ShapeDtypeStruct((rows, width), jnp.float32)]
    result = pl.pallas_call(
        functools.partial(project_kernel, sizes, len(pieces), spot, total is None, last),
        grid_spec=pltpu.PrefetchScalarGridSpec(
            num_scalar_prefetch=1,
            grid=(1,),
            in_specs=[WHOLE] * len(operands),
            out_specs=[WHOLE] * len(shapes),
            scratch_shapes=scratch,
        ),
        out_shape=shapes,
        compiler_params=vmem(scratch),
        cost_estimate=cost(us),
    )(meta, *operands)
    return list(result) if last else result[0]


def spread(sizes, meta, applied, pieces, points, which):
    count = len(applied)
    applied = join_small(applied)
    rows = sum(block.shape[0] for block in applied)
    scratch = [pltpu.VMEM((points + TILE, rows), jnp.float32)] + joined_shape(pieces)
    result = pl.pallas_call(
        functools.partial(spread_kernel, sizes, len(applied), len(pieces), which),
        grid_spec=pltpu.PrefetchScalarGridSpec(
            num_scalar_prefetch=1,
            grid=(1,),
            in_specs=[WHOLE] * (len(applied) + len(pieces)),
            out_specs=[WHOLE] * len(applied),
            scratch_shapes=scratch,
        ),
        out_shape=[
            jax.ShapeDtypeStruct((block.shape[0], points), jnp.bfloat16) for block in applied
        ],
        compiler_params=vmem(scratch),
        cost_estimate=cost(0),
    )(meta, *applied, *pieces)
    return split_small(result, count)


def two_parts(values):
    high = values.astype(jnp.bfloat16)
    return high, (values - high.astype(jnp.float32)).astype(jnp.bfloat16)


def couple_kernel(high_ref, low_ref, *refs):
    parts, out_ref = refs[:-1], refs[-1]
    blocks, proj, unused = high_ref.shape
    for block in range(blocks):
        lanes = slice(block * proj, (block + 1) * proj)
        total = parts[0][:, lanes].astype(jnp.float32)
        for part in parts[1:]:
            total += part[:, lanes].astype(jnp.float32)
        high, low = two_parts(total)
        result = jnp.dot(high, high_ref[block], preferred_element_type=jnp.float32)
        result += jnp.dot(high, low_ref[block], preferred_element_type=jnp.float32)
        result += jnp.dot(low, high_ref[block], preferred_element_type=jnp.float32)
        out_ref[:, lanes] = result.astype(out_ref.dtype)


def couple(parts, high, low):
    return pl.pallas_call(
        couple_kernel,
        in_specs=[WHOLE] * (2 + len(parts)),
        out_specs=WHOLE,
        out_shape=jax.ShapeDtypeStruct(parts[0].shape, jnp.bfloat16),
        compiler_params=vmem([]),
        cost_estimate=cost(0),
    )(high, low, *parts)


def coupling_matrix(coupling):
    blocks, atoms, width, unused = coupling.shape
    proj = atoms * width
    wide = jnp.tile(coupling.reshape(blocks, proj, width), (1, 1, atoms))
    same = jnp.arange(proj)[:, None] // width == jnp.arange(proj)[None, :] // width
    return jnp.where(same[None], wide, 0.0)


def body(n_grid, wavefunctions, tile_segment, tile_block, tile_count, projectors, coupling):
    half = n_grid // 2
    bands, npts = wavefunctions.shape
    points = npts // n_grid
    tiles = projectors.shape[0]
    width = coupling.shape[0] * projectors.shape[2]
    index = lax.axis_index("grid")
    side, place = index // half, index % half
    group, core = lax.axis_index("groups"), lax.axis_index("band")
    partners = [(i, (i + half) % n_grid) for i in range(n_grid)]
    pools = [list(range(half)), list(range(half, n_grid))]
    swap = [(0, 1), (1, 0)]

    def exchange(blocks):
        return [blocks[0]] + [
            lax.ppermute(
                blocks[d], "grid", [(i, i // half * half + (i % half ^ d)) for i in range(n_grid)]
            )
            for d in range(1, half)
        ]

    def to_bricks(which):
        part = lax.dynamic_slice_in_dim(wavefunctions, which * half * points, half * points, 1)
        return lax.all_to_all(
            part, "grid", split_axis=1, concat_axis=0, tiled=True, axis_index_groups=pools
        )

    segments, blocks = points // TILE, coupling.shape[0]
    sizes = (tiles, segments, blocks)
    slots = jnp.arange(tiles, dtype=jnp.int32)
    starts = [tiles * sum(PARTS[:number]) // sum(PARTS) for number in range(len(PARTS) + 1)]
    held, range_of = slots, 0
    for start, end in zip(starts, starts[1:]):
        share = (end - start) // 4
        quarter, rest = (slots - start) // share, (slots - start) % share
        at = start + rest + share * ((quarter // 2 ^ group) + 2 * (quarter % 2 ^ core))
        held = jnp.where((slots >= start) & (slots < end), at, held)
    for first, end in RANGES[1:]:
        range_of += jnp.where(slots >= starts[first], 1, 0)

    own_wave = to_bricks(side)
    other_wave = to_bricks(1 - side)
    matrix = two_parts(coupling_matrix(coupling))

    arrived, pieces, across = [], [], None
    source = projectors
    for number, (start, end) in enumerate(zip(starts, starts[1:])):
        share = (end - start) // 4
        start += (2 * group + core) * share
        sent = lax.dynamic_slice_in_dim(source, start, share, 0)
        if number == 0:
            sent, source = lax.optimization_barrier((sent, source))
        if number > 0:
            sent = lax.optimization_barrier((sent, arrived[-1]))[0]
        arrived.append(lax.ppermute(sent, "grid", partners))

    numbers = jnp.stack([tile_segment, tile_block, jnp.broadcast_to(tile_count, (tiles,))])
    numbers = lax.optimization_barrier((numbers, arrived[0]))[0]
    others = lax.ppermute(numbers, "grid", partners)
    absent = segments << bits(tiles)
    segment, block = (jnp.stack([numbers[i], others[i]]) for i in (0, 1))
    codes = jnp.stack([slots, held])
    codes += (segment + (block << bits(segments + 1))) << bits(tiles)
    live = slots < jnp.stack([numbers[2], others[2]])
    keys = block + blocks * jnp.stack([jnp.zeros_like(slots), range_of])
    meta = jnp.concatenate(
        [
            jnp.stack([place, numbers[2, 0], others[2, 0]]),
            group_lists(codes, keys, live, blocks, absent),
        ]
    )

    own_wave = lax.optimization_barrier((own_wave, arrived[1]))[0]
    own_spot = (OWN, 0, len(RANGES), 0)
    total = project(sizes, meta, own_wave, [projectors], half, width, own_spot, us=2)
    for number, mine in enumerate(arrived):
        sent = mine
        if number == 1:
            sent, across, matrix = lax.optimization_barrier((sent, across, matrix))
        if number == 2:
            sent, across, other_wave, total = lax.optimization_barrier(
                (sent, across, other_wave, total)
            )
        across = lax.ppermute(sent, "groups", swap)
        pieces += [mine, across]
        pieces += [lax.ppermute(mine, "band", swap), lax.ppermute(across, "band", swap)]

    for number, (first, end) in enumerate(RANGES):
        last = end == len(PARTS)
        total = project(
            sizes,
            meta,
            other_wave,
            pieces[4 * first : 4 * end],
            half,
            width,
            (OTHER, number, number + 1, starts[first]),
            total,
            last=last,
            us=0 if last else 8,
        )
    if len(total) < half:
        total = [lax.dynamic_slice_in_dim(total[0], (place ^ d) * bands, bands, 0) for d in range(half)]

    applied = couple(exchange(total), *matrix)
    applied = exchange([applied] * half)

    result = jnp.zeros((bands, npts), jnp.bfloat16)
    for which, field in (
        (1 - side, spread(sizes, meta, applied, pieces, points, OTHER)),
        (side, spread(sizes, meta, applied, [projectors], points, OWN)),
    ):
        for d, block in enumerate(exchange(field)):
            start = (which * half + (place ^ d)) * points
            result = lax.dynamic_update_slice_in_dim(result, block, start, 1)
    return result


def solution(mesh):
    in_specs = (
        P(("groups", "grid", "band"), None),
        P("grid"),
        P("grid"),
        P("grid"),
        P("grid", None, None),
        P(),
    )
    out_specs = P(("groups", "grid", "band"), None)
    return jax.shard_map(
        functools.partial(body, mesh.shape["grid"]),
        mesh=mesh,
        in_specs=in_specs,
        out_specs=out_specs,
        check_vma=False,
    )
```

```python
import functools
import math

import jax
import jax.numpy as jnp
from jax import lax
from jax.experimental import pallas as pl
from jax.experimental.pallas import tpu as pltpu
from jax.sharding import PartitionSpec as P

TILE = 64
PAIR = 2 * TILE
GROUP = 4
UNROLL = 8
VMEM_SLACK = 10 * 1024 * 1024
PARTS = (15, 17, 16)
RANGES = ((0, 2), (2, 3))
OWN, OTHER = range(2)
BOUNDS = 3
STEPS = len(RANGES) + 1
LISTS = BOUNDS + 2 * STEPS


def bits(count):
    return max(1, (count - 1).bit_length())


def list_length(tiles, blocks):
    return tiles + len(RANGES) * ((GROUP - 1) * blocks + GROUP * UNROLL)


def group_lists(codes, keys, live, blocks, absent):
    n_lists, tiles = codes.shape
    n_keys = len(RANGES) * blocks
    order = jnp.arange(tiles, dtype=jnp.int32)
    key_range = jnp.arange(n_keys, dtype=jnp.int32)
    ranges = jnp.arange(STEPS, dtype=jnp.int32)
    mine = (keys[:, None, :] == key_range[None, :, None]) & live[:, None, :]
    groups = (jnp.sum(mine, axis=2, dtype=jnp.int32) + GROUP - 1) // GROUP
    in_range = key_range[:, None] // blocks == ranges[None, :]
    totals = jnp.sum(jnp.where(in_range, groups[:, :, None], 0), axis=1, dtype=jnp.int32)
    totals = (totals + UNROLL - 1) // UNROLL * UNROLL
    bounds = jnp.sum(
        jnp.where(ranges[:, None] < ranges[None, :], totals[:, :, None], 0), axis=1, dtype=jnp.int32
    )
    lower = (key_range[:, None] < key_range[None, :]) & (
        key_range[:, None] // blocks == key_range[None, :] // blocks
    )
    starts = jnp.sum(jnp.where(lower, groups[:, :, None], 0), axis=1, dtype=jnp.int32)
    starts += jnp.sum(jnp.where(in_range, bounds[:, None, :], 0), axis=2, dtype=jnp.int32)
    before = (
        (keys[:, :, None] == keys[:, None, :]) & live[:, :, None] & (order[:, None] < order[None, :])
    )
    entry = jnp.sum(before, axis=1, dtype=jnp.int32) + GROUP * jnp.sum(
        jnp.where(mine, starts[:, :, None], 0), axis=1, dtype=jnp.int32
    )
    entry = jnp.where(live, entry, -1)
    found = entry[:, :, None] == jnp.arange(list_length(tiles, blocks), dtype=jnp.int32)
    entries = absent + jnp.sum(
        jnp.where(found, codes[:, :, None] - absent, 0), axis=1, dtype=jnp.int32
    )
    return jnp.concatenate([bounds.reshape(-1), entries.reshape(-1)])


def group_loop(sizes, meta, values, proj, which, first, last, origin, product):
    tiles, segments, blocks = sizes
    begin, end = (meta[BOUNDS + STEPS * which + number] for number in (first, last))
    base = LISTS + which * list_length(tiles, blocks)

    def group(number):
        places = []
        for entry in range(GROUP):
            code = meta[base + GROUP * number + entry]
            index = jnp.maximum((code & ((1 << bits(tiles)) - 1)) - origin, 0)
            code = code >> bits(tiles)
            places.append((code & ((1 << bits(segments + 1)) - 1), values[index]))
            if entry == 0:
                block = code >> bits(segments + 1)
        lanes = pl.ds(pl.multiple_of(block * proj, proj), proj)
        return product(lanes, [at for at, tile in places], [tile for at, tile in places])

    def step(index, carry):
        sums = [group(begin + index * UNROLL + lane) for lane in range(UNROLL)]
        for additions in sums:
            for ref, rows, lanes, term in additions:
                ref[rows, lanes] += term
        return carry

    lax.fori_loop(0, (end - begin) // UNROLL, step, 0)


def join_pieces(meta, pieces, joined, first):
    end = 0
    for number, ref in enumerate(pieces):
        start, end = end, end + ref.shape[0]

        @pl.when(meta[2] > first + start - number % 4 * ref.shape[0])
        def copy(start=start, end=end, ref=ref):
            joined[start:end] = ref[...]


def rows_of(refs, lanes):
    return jnp.concatenate([ref[:, lanes] for ref in refs], axis=0)


def turn_waves(wave, turned, segments):
    for pair in range(segments // 2):
        values = wave[:, pair * PAIR : (pair + 1) * PAIR]
        turned[0, pair] = values
        turned[1, pair] = pltpu.roll(values.astype(jnp.float32), TILE, 1).astype(values.dtype)
    for way in range(2):
        turned[way, segments // 2] = jnp.zeros(turned.shape[2:], turned.dtype)


def project_kernel(sizes, n_pieces, spot, first, last, meta, wave, *refs):
    pieces, refs = refs[:n_pieces], refs[n_pieces:]
    turned, refs = refs[-1], refs[:-1]
    if not first:
        before, refs = refs[0], refs[1:]
    values = pieces[0]
    if n_pieces > 1:
        values, refs = refs[-1], refs[:-1]
        join_pieces(meta, pieces, values, spot[-1])
    total = refs[-1]
    total[...] = jnp.zeros_like(total) if first else before[...]
    every = slice(None)

    def product(lanes, segments, tiles):
        low = lax.broadcasted_iota(jnp.int32, turned.shape[2:], 1) < TILE
        waves = [
            jnp.where(
                low,
                turned[segments[at] & 1, segments[at] >> 1],
                turned[1 - (segments[at + 1] & 1), segments[at + 1] >> 1],
            )
            for at in range(0, GROUP, 2)
        ]
        term = jnp.dot(
            jnp.concatenate(waves, axis=1),
            jnp.concatenate(tiles, axis=0),
            preferred_element_type=jnp.float32,
        )
        return [(total, every, lanes, term)]

    @pl.when(meta[1 + spot[0]] > spot[-1])
    def loop():
        turn_waves(wave, turned, sizes[1])
        group_loop(sizes, meta, values, values.shape[2], *spot, product)

    if last:
        outs = refs[:-1]
        rows = outs[0].shape[0]
        for d, out in enumerate(outs):
            start = 0 if len(outs) == 1 else pl.multiple_of((meta[0] ^ d) * rows, rows)
            out[...] = total[pl.ds(start, rows), :].astype(out.dtype)


def spread_kernel(sizes, n_rows, n_pieces, which, meta, *refs):
    applied, refs = refs[:n_rows], refs[n_rows:]
    pieces, refs = refs[:n_pieces], refs[n_pieces:]
    values = pieces[0]
    if n_pieces > 1:
        values, refs = refs[-1], refs[:-1]
        join_pieces(meta, pieces, values, 0)
    outs, field = refs[:-1], refs[-1]
    field[...] = jnp.zeros_like(field)
    every = slice(None)

    def product(lanes, segments, tiles):
        terms = lax.dot_general(
            jnp.concatenate(tiles, axis=0),
            rows_of(applied, lanes),
            (((1,), (1,)), ((), ())),
            preferred_element_type=jnp.float32,
        )
        return [
            (
                field,
                pl.ds(pl.multiple_of(at * TILE, TILE), TILE),
                every,
                terms[number * TILE : (number + 1) * TILE],
            )
            for number, at in enumerate(segments)
        ]

    group_loop(sizes, meta, values, values.shape[2], which, 0, len(RANGES), 0, product)
    for pair in range(sizes[1] // 2):
        points = slice(pair * PAIR, (pair + 1) * PAIR)
        values, start = field[points, :].T, 0
        for out in outs:
            out[:, points] = values[start : start + out.shape[0]].astype(out.dtype)
            start += out.shape[0]


WHOLE = pl.BlockSpec(memory_space=pltpu.VMEM)


def cost(us):
    return pl.CostEstimate(flops=1 + us * 10**9, bytes_accessed=1, transcendentals=0)


def join_small(blocks):
    return blocks if blocks[0].shape[0] % 16 == 0 else [jnp.concatenate(blocks)]


def split_small(blocks, count):
    return blocks if len(blocks) == count else jnp.split(blocks[0], count)


def vmem(scratch):
    size = sum(math.prod(ref.shape) * jnp.dtype(ref.dtype).itemsize for ref in scratch)
    return pltpu.CompilerParams(vmem_limit_bytes=size + VMEM_SLACK)


def joined_shape(pieces):
    if len(pieces) == 1:
        return []
    count = sum(piece.shape[0] for piece in pieces)
    return [pltpu.VMEM((count,) + pieces[0].shape[1:], jnp.bfloat16)]


def project(sizes, meta, wave, pieces, count, width, spot, total=None, last=False, us=0):
    rows = wave.shape[0]
    operands = [wave, *pieces] + ([] if total is None else [total])
    scratch = joined_shape(pieces)
    scratch.append(pltpu.VMEM((2, sizes[1] // 2 + 1, rows, PAIR), jnp.bfloat16))
    if last:
        outs = count if rows // count % 16 == 0 else 1
        shapes = [jax.ShapeDtypeStruct((rows // outs, width), jnp.bfloat16)] * outs
        scratch = [pltpu.VMEM((rows, width), jnp.float32)] + scratch
    else:
        shapes = [jax.ShapeDtypeStruct((rows, width), jnp.float32)]
    result = pl.pallas_call(
        functools.partial(project_kernel, sizes, len(pieces), spot, total is None, last),
        grid_spec=pltpu.PrefetchScalarGridSpec(
            num_scalar_prefetch=1,
            grid=(1,),
            in_specs=[WHOLE] * len(operands),
            out_specs=[WHOLE] * len(shapes),
            scratch_shapes=scratch,
        ),
        out_shape=shapes,
        compiler_params=vmem(scratch),
        cost_estimate=cost(us),
    )(meta, *operands)
    return list(result) if last else result[0]


def spread(sizes, meta, applied, pieces, points, which):
    count = len(applied)
    applied = join_small(applied)
    rows = sum(block.shape[0] for block in applied)
    scratch = [pltpu.VMEM((points + TILE, rows), jnp.float32)] + joined_shape(pieces)
    result = pl.pallas_call(
        functools.partial(spread_kernel, sizes, len(applied), len(pieces), which),
        grid_spec=pltpu.PrefetchScalarGridSpec(
            num_scalar_prefetch=1,
            grid=(1,),
            in_specs=[WHOLE] * (len(applied) + len(pieces)),
            out_specs=[WHOLE] * len(applied),
            scratch_shapes=scratch,
        ),
        out_shape=[
            jax.ShapeDtypeStruct((block.shape[0], points), jnp.bfloat16) for block in applied
        ],
        compiler_params=vmem(scratch),
        cost_estimate=cost(0),
    )(meta, *applied, *pieces)
    return split_small(result, count)


def two_parts(values):
    high = values.astype(jnp.bfloat16)
    return high, (values - high.astype(jnp.float32)).astype(jnp.bfloat16)


def couple_kernel(high_ref, low_ref, *refs):
    parts, out_ref = refs[:-1], refs[-1]
    blocks, proj, unused = high_ref.shape
    for block in range(blocks):
        lanes = slice(block * proj, (block + 1) * proj)
        total = parts[0][:, lanes].astype(jnp.float32)
        for part in parts[1:]:
            total += part[:, lanes].astype(jnp.float32)
        high, low = two_parts(total)
        result = jnp.dot(high, high_ref[block], preferred_element_type=jnp.float32)
        result += jnp.dot(high, low_ref[block], preferred_element_type=jnp.float32)
        result += jnp.dot(low, high_ref[block], preferred_element_type=jnp.float32)
        out_ref[:, lanes] = result.astype(out_ref.dtype)


def couple(parts, high, low):
    return pl.pallas_call(
        couple_kernel,
        in_specs=[WHOLE] * (2 + len(parts)),
        out_specs=WHOLE,
        out_shape=jax.ShapeDtypeStruct(parts[0].shape, jnp.bfloat16),
        compiler_params=vmem([]),
        cost_estimate=cost(0),
    )(high, low, *parts)


def coupling_matrix(coupling):
    blocks, atoms, width, unused = coupling.shape
    proj = atoms * width
    wide = jnp.tile(coupling.reshape(blocks, proj, width), (1, 1, atoms))
    same = jnp.arange(proj)[:, None] // width == jnp.arange(proj)[None, :] // width
    return jnp.where(same[None], wide, 0.0)


def body(n_grid, wavefunctions, tile_segment, tile_block, tile_count, projectors, coupling):
    half = n_grid // 2
    bands, npts = wavefunctions.shape
    points = npts // n_grid
    tiles = projectors.shape[0]
    width = coupling.shape[0] * projectors.shape[2]
    index = lax.axis_index("grid")
    side, place = index // half, index % half
    group, core = lax.axis_index("groups"), lax.axis_index("band")
    partners = [(i, (i + half) % n_grid) for i in range(n_grid)]
    pools = [list(range(half)), list(range(half, n_grid))]
    swap = [(0, 1), (1, 0)]

    def exchange(blocks):
        return [blocks[0]] + [
            lax.ppermute(
                blocks[d], "grid", [(i, i // half * half + (i % half ^ d)) for i in range(n_grid)]
            )
            for d in range(1, half)
        ]

    def to_bricks(which, after):
        part = lax.dynamic_slice_in_dim(wavefunctions, which * half * points, half * points, 1)
        part = lax.optimization_barrier((part, after))[0]
        return lax.all_to_all(
            part, "grid", split_axis=1, concat_axis=0, tiled=True, axis_index_groups=pools
        )

    segments, blocks = points // TILE, coupling.shape[0]
    sizes = (tiles, segments, blocks)
    slots = jnp.arange(tiles, dtype=jnp.int32)
    starts = [tiles * sum(PARTS[:number]) // sum(PARTS) for number in range(len(PARTS) + 1)]
    held, range_of = slots, 0
    for start, end in zip(starts, starts[1:]):
        share = (end - start) // 4
        quarter, rest = (slots - start) // share, (slots - start) % share
        at = start + rest + share * ((quarter // 2 ^ group) + 2 * (quarter % 2 ^ core))
        held = jnp.where((slots >= start) & (slots < end), at, held)
    for first, end in RANGES[1:]:
        range_of += jnp.where(slots >= starts[first], 1, 0)

    matrix = two_parts(coupling_matrix(coupling))

    arrived, pieces, across = [], [], None
    source = projectors
    for number, (start, end) in enumerate(zip(starts, starts[1:])):
        share = (end - start) // 4
        start += (2 * group + core) * share
        sent = lax.dynamic_slice_in_dim(source, start, share, 0)
        if number == 0:
            sent, source = lax.optimization_barrier((sent, source))
        if number > 0:
            sent = lax.optimization_barrier((sent, arrived[0]))[0]
        arrived.append(lax.ppermute(sent, "grid", partners))

    numbers = jnp.stack([tile_segment, tile_block, jnp.broadcast_to(tile_count, (tiles,))])
    numbers = lax.optimization_barrier((numbers, arrived[0]))[0]
    others = lax.ppermute(numbers, "grid", partners)
    absent = segments << bits(tiles)
    segment, block = (jnp.stack([numbers[i], others[i]]) for i in (0, 1))
    codes = jnp.stack([slots, held])
    codes += (segment + (block << bits(segments + 1))) << bits(tiles)
    live = slots < jnp.stack([numbers[2], others[2]])
    keys = block + blocks * jnp.stack([jnp.zeros_like(slots), range_of])
    meta = jnp.concatenate(
        [
            jnp.stack([place, numbers[2, 0], others[2, 0]]),
            group_lists(codes, keys, live, blocks, absent),
        ]
    )

    own_wave = to_bricks(side, arrived[0])
    other_wave = to_bricks(1 - side, own_wave)
    own_spot = (OWN, 0, len(RANGES), 0)
    total = project(sizes, meta, own_wave, [projectors], half, width, own_spot, us=2)
    for number, mine in enumerate(arrived):
        sent = mine
        if number == 1:
            sent, across, matrix = lax.optimization_barrier((sent, across, matrix))
        if number == 2:
            sent, across, other_wave, total = lax.optimization_barrier(
                (sent, across, other_wave, total)
            )
        across = lax.ppermute(sent, "groups", swap)
        pieces += [mine, across]
        pieces += [lax.ppermute(mine, "band", swap), lax.ppermute(across, "band", swap)]

    for number, (first, end) in enumerate(RANGES):
        last = end == len(PARTS)
        total = project(
            sizes,
            meta,
            other_wave,
            pieces[4 * first : 4 * end],
            half,
            width,
            (OTHER, number, number + 1, starts[first]),
            total,
            last=last,
            us=0 if last else 8,
        )
    if len(total) < half:
        total = [lax.dynamic_slice_in_dim(total[0], (place ^ d) * bands, bands, 0) for d in range(half)]

    applied = couple(exchange(total), *matrix)
    applied = exchange([applied] * half)

    result = jnp.zeros((bands, npts), jnp.bfloat16)
    for which, field in (
        (1 - side, spread(sizes, meta, applied, pieces, points, OTHER)),
        (side, spread(sizes, meta, applied, [projectors], points, OWN)),
    ):
        for d, block in enumerate(exchange(field)):
            start = (which * half + (place ^ d)) * points
            result = lax.dynamic_update_slice_in_dim(result, block, start, 1)
    return result


def solution(mesh):
    in_specs = (
        P(("groups", "grid", "band"), None),
        P("grid"),
        P("grid"),
        P("grid"),
        P("grid", None, None),
        P(),
    )
    out_specs = P(("groups", "grid", "band"), None)
    return jax.shard_map(
        functools.partial(body, mesh.shape["grid"]),
        mesh=mesh,
        in_specs=in_specs,
        out_specs=out_specs,
        check_vma=False,
    )
```

```python
import functools
import math

import jax
import jax.numpy as jnp
from jax import lax
from jax.experimental import pallas as pl
from jax.experimental.pallas import tpu as pltpu
from jax.sharding import PartitionSpec as P

TILE = 64
PAIR = 2 * TILE
GROUP = 4
UNROLL = 8
VMEM_SLACK = 10 * 1024 * 1024
PARTS = (17, 17, 14)
RANGES = ((0, 2), (2, 3))
OWN, OTHER = range(2)
BOUNDS = 3
STEPS = len(RANGES) + 1
LISTS = BOUNDS + 2 * STEPS


def bits(count):
    return max(1, (count - 1).bit_length())


def list_length(tiles, blocks):
    return tiles + len(RANGES) * ((GROUP - 1) * blocks + GROUP * UNROLL)


def group_lists(codes, keys, live, blocks, absent):
    n_lists, tiles = codes.shape
    n_keys = len(RANGES) * blocks
    order = jnp.arange(tiles, dtype=jnp.int32)
    key_range = jnp.arange(n_keys, dtype=jnp.int32)
    ranges = jnp.arange(STEPS, dtype=jnp.int32)
    mine = (keys[:, None, :] == key_range[None, :, None]) & live[:, None, :]
    groups = (jnp.sum(mine, axis=2, dtype=jnp.int32) + GROUP - 1) // GROUP
    in_range = key_range[:, None] // blocks == ranges[None, :]
    totals = jnp.sum(jnp.where(in_range, groups[:, :, None], 0), axis=1, dtype=jnp.int32)
    totals = (totals + UNROLL - 1) // UNROLL * UNROLL
    bounds = jnp.sum(
        jnp.where(ranges[:, None] < ranges[None, :], totals[:, :, None], 0), axis=1, dtype=jnp.int32
    )
    lower = (key_range[:, None] < key_range[None, :]) & (
        key_range[:, None] // blocks == key_range[None, :] // blocks
    )
    starts = jnp.sum(jnp.where(lower, groups[:, :, None], 0), axis=1, dtype=jnp.int32)
    starts += jnp.sum(jnp.where(in_range, bounds[:, None, :], 0), axis=2, dtype=jnp.int32)
    before = (
        (keys[:, :, None] == keys[:, None, :]) & live[:, :, None] & (order[:, None] < order[None, :])
    )
    entry = jnp.sum(before, axis=1, dtype=jnp.int32) + GROUP * jnp.sum(
        jnp.where(mine, starts[:, :, None], 0), axis=1, dtype=jnp.int32
    )
    entry = jnp.where(live, entry, -1)
    found = entry[:, :, None] == jnp.arange(list_length(tiles, blocks), dtype=jnp.int32)
    entries = absent + jnp.sum(
        jnp.where(found, codes[:, :, None] - absent, 0), axis=1, dtype=jnp.int32
    )
    return jnp.concatenate([bounds.reshape(-1), entries.reshape(-1)])


def group_loop(sizes, meta, values, proj, which, first, last, origin, product):
    tiles, segments, blocks = sizes
    begin, end = (meta[BOUNDS + STEPS * which + number] for number in (first, last))
    base = LISTS + which * list_length(tiles, blocks)

    def group(number):
        places = []
        for entry in range(GROUP):
            code = meta[base + GROUP * number + entry]
            index = jnp.maximum((code & ((1 << bits(tiles)) - 1)) - origin, 0)
            code = code >> bits(tiles)
            places.append((code & ((1 << bits(segments + 1)) - 1), values[index]))
            if entry == 0:
                block = code >> bits(segments + 1)
        lanes = pl.ds(pl.multiple_of(block * proj, proj), proj)
        return product(lanes, [at for at, tile in places], [tile for at, tile in places])

    def step(index, carry):
        sums = [group(begin + index * UNROLL + lane) for lane in range(UNROLL)]
        for additions in sums:
            for ref, rows, lanes, term in additions:
                ref[rows, lanes] += term
        return carry

    lax.fori_loop(0, (end - begin) // UNROLL, step, 0)


def join_pieces(meta, pieces, joined, first):
    end = 0
    for number, ref in enumerate(pieces):
        start, end = end, end + ref.shape[0]

        @pl.when(meta[2] > first + start - number % 4 * ref.shape[0])
        def copy(start=start, end=end, ref=ref):
            joined[start:end] = ref[...]


def rows_of(refs, lanes):
    return jnp.concatenate([ref[:, lanes] for ref in refs], axis=0)


def turn_waves(wave, turned, segments):
    for pair in range(segments // 2):
        values = wave[:, pair * PAIR : (pair + 1) * PAIR]
        turned[0, pair] = values
        turned[1, pair] = pltpu.roll(values.astype(jnp.float32), TILE, 1).astype(values.dtype)
    for way in range(2):
        turned[way, segments // 2] = jnp.zeros(turned.shape[2:], turned.dtype)


def project_kernel(sizes, n_pieces, spot, first, last, meta, wave, *refs):
    pieces, refs = refs[:n_pieces], refs[n_pieces:]
    turned, refs = refs[-1], refs[:-1]
    if not first:
        before, refs = refs[0], refs[1:]
    values = pieces[0]
    if n_pieces > 1:
        values, refs = refs[-1], refs[:-1]
        join_pieces(meta, pieces, values, spot[-1])
    total = refs[-1]
    total[...] = jnp.zeros_like(total) if first else before[...]
    every = slice(None)

    def product(lanes, segments, tiles):
        low = lax.broadcasted_iota(jnp.int32, turned.shape[2:], 1) < TILE
        waves = [
            jnp.where(
                low,
                turned[segments[at] & 1, segments[at] >> 1],
                turned[1 - (segments[at + 1] & 1), segments[at + 1] >> 1],
            )
            for at in range(0, GROUP, 2)
        ]
        term = jnp.dot(
            jnp.concatenate(waves, axis=1),
            jnp.concatenate(tiles, axis=0),
            preferred_element_type=jnp.float32,
        )
        return [(total, every, lanes, term)]

    @pl.when(meta[1 + spot[0]] > spot[-1])
    def loop():
        turn_waves(wave, turned, sizes[1])
        group_loop(sizes, meta, values, values.shape[2], *spot, product)

    if last:
        outs = refs[:-1]
        rows = outs[0].shape[0]
        for d, out in enumerate(outs):
            start = 0 if len(outs) == 1 else pl.multiple_of((meta[0] ^ d) * rows, rows)
            out[...] = total[pl.ds(start, rows), :].astype(out.dtype)


def spread_kernel(sizes, n_rows, n_pieces, which, meta, *refs):
    applied, refs = refs[:n_rows], refs[n_rows:]
    pieces, refs = refs[:n_pieces], refs[n_pieces:]
    values = pieces[0]
    if n_pieces > 1:
        values, refs = refs[-1], refs[:-1]
        join_pieces(meta, pieces, values, 0)
    outs, field = refs[:-1], refs[-1]
    field[...] = jnp.zeros_like(field)
    every = slice(None)

    def product(lanes, segments, tiles):
        terms = lax.dot_general(
            jnp.concatenate(tiles, axis=0),
            rows_of(applied, lanes),
            (((1,), (1,)), ((), ())),
            preferred_element_type=jnp.float32,
        )
        return [
            (
                field,
                pl.ds(pl.multiple_of(at * TILE, TILE), TILE),
                every,
                terms[number * TILE : (number + 1) * TILE],
            )
            for number, at in enumerate(segments)
        ]

    group_loop(sizes, meta, values, values.shape[2], which, 0, len(RANGES), 0, product)
    for pair in range(sizes[1] // 2):
        points = slice(pair * PAIR, (pair + 1) * PAIR)
        values, start = field[points, :].T, 0
        for out in outs:
            out[:, points] = values[start : start + out.shape[0]].astype(out.dtype)
            start += out.shape[0]


WHOLE = pl.BlockSpec(memory_space=pltpu.VMEM)


def cost(us):
    return pl.CostEstimate(flops=1 + us * 10**9, bytes_accessed=1, transcendentals=0)


def join_small(blocks):
    return blocks if blocks[0].shape[0] % 16 == 0 else [jnp.concatenate(blocks)]


def split_small(blocks, count):
    return blocks if len(blocks) == count else jnp.split(blocks[0], count)


def vmem(scratch):
    size = sum(math.prod(ref.shape) * jnp.dtype(ref.dtype).itemsize for ref in scratch)
    return pltpu.CompilerParams(vmem_limit_bytes=size + VMEM_SLACK)


def joined_shape(pieces):
    if len(pieces) == 1:
        return []
    count = sum(piece.shape[0] for piece in pieces)
    return [pltpu.VMEM((count,) + pieces[0].shape[1:], jnp.bfloat16)]


def project(sizes, meta, wave, pieces, count, width, spot, total=None, last=False, us=0):
    rows = wave.shape[0]
    operands = [wave, *pieces] + ([] if total is None else [total])
    scratch = joined_shape(pieces)
    scratch.append(pltpu.VMEM((2, sizes[1] // 2 + 1, rows, PAIR), jnp.bfloat16))
    if last:
        outs = count if rows // count % 16 == 0 else 1
        shapes = [jax.ShapeDtypeStruct((rows // outs, width), jnp.bfloat16)] * outs
        scratch = [pltpu.VMEM((rows, width), jnp.float32)] + scratch
    else:
        shapes = [jax.ShapeDtypeStruct((rows, width), jnp.float32)]
    result = pl.pallas_call(
        functools.partial(project_kernel, sizes, len(pieces), spot, total is None, last),
        grid_spec=pltpu.PrefetchScalarGridSpec(
            num_scalar_prefetch=1,
            grid=(1,),
            in_specs=[WHOLE] * len(operands),
            out_specs=[WHOLE] * len(shapes),
            scratch_shapes=scratch,
        ),
        out_shape=shapes,
        compiler_params=vmem(scratch),
        cost_estimate=cost(us),
    )(meta, *operands)
    return list(result) if last else result[0]


def spread(sizes, meta, applied, pieces, points, which):
    count = len(applied)
    applied = join_small(applied)
    rows = sum(block.shape[0] for block in applied)
    scratch = [pltpu.VMEM((points + TILE, rows), jnp.float32)] + joined_shape(pieces)
    result = pl.pallas_call(
        functools.partial(spread_kernel, sizes, len(applied), len(pieces), which),
        grid_spec=pltpu.PrefetchScalarGridSpec(
            num_scalar_prefetch=1,
            grid=(1,),
            in_specs=[WHOLE] * (len(applied) + len(pieces)),
            out_specs=[WHOLE] * len(applied),
            scratch_shapes=scratch,
        ),
        out_shape=[
            jax.ShapeDtypeStruct((block.shape[0], points), jnp.bfloat16) for block in applied
        ],
        compiler_params=vmem(scratch),
        cost_estimate=cost(0),
    )(meta, *applied, *pieces)
    return split_small(result, count)


def two_parts(values):
    high = values.astype(jnp.bfloat16)
    return high, (values - high.astype(jnp.float32)).astype(jnp.bfloat16)


def couple_kernel(high_ref, low_ref, *refs):
    parts, out_ref = refs[:-1], refs[-1]
    blocks, proj, unused = high_ref.shape
    for block in range(blocks):
        lanes = slice(block * proj, (block + 1) * proj)
        total = parts[0][:, lanes].astype(jnp.float32)
        for part in parts[1:]:
            total += part[:, lanes].astype(jnp.float32)
        high, low = two_parts(total)
        result = jnp.dot(high, high_ref[block], preferred_element_type=jnp.float32)
        result += jnp.dot(high, low_ref[block], preferred_element_type=jnp.float32)
        result += jnp.dot(low, high_ref[block], preferred_element_type=jnp.float32)
        out_ref[:, lanes] = result.astype(out_ref.dtype)


def couple(parts, high, low):
    return pl.pallas_call(
        couple_kernel,
        in_specs=[WHOLE] * (2 + len(parts)),
        out_specs=WHOLE,
        out_shape=jax.ShapeDtypeStruct(parts[0].shape, jnp.bfloat16),
        compiler_params=vmem([]),
        cost_estimate=cost(0),
    )(high, low, *parts)


def coupling_matrix(coupling):
    blocks, atoms, width, unused = coupling.shape
    proj = atoms * width
    wide = jnp.tile(coupling.reshape(blocks, proj, width), (1, 1, atoms))
    same = jnp.arange(proj)[:, None] // width == jnp.arange(proj)[None, :] // width
    return jnp.where(same[None], wide, 0.0)


def body(n_grid, wavefunctions, tile_segment, tile_block, tile_count, projectors, coupling):
    half = n_grid // 2
    bands, npts = wavefunctions.shape
    points = npts // n_grid
    tiles = projectors.shape[0]
    width = coupling.shape[0] * projectors.shape[2]
    index = lax.axis_index("grid")
    side, place = index // half, index % half
    group, core = lax.axis_index("groups"), lax.axis_index("band")
    partners = [(i, (i + half) % n_grid) for i in range(n_grid)]
    pools = [list(range(half)), list(range(half, n_grid))]
    swap = [(0, 1), (1, 0)]

    def exchange(blocks):
        return [blocks[0]] + [
            lax.ppermute(
                blocks[d], "grid", [(i, i // half * half + (i % half ^ d)) for i in range(n_grid)]
            )
            for d in range(1, half)
        ]

    def to_bricks(which):
        part = lax.dynamic_slice_in_dim(wavefunctions, which * half * points, half * points, 1)
        return lax.all_to_all(
            part, "grid", split_axis=1, concat_axis=0, tiled=True, axis_index_groups=pools
        )

    segments, blocks = points // TILE, coupling.shape[0]
    sizes = (tiles, segments, blocks)
    slots = jnp.arange(tiles, dtype=jnp.int32)
    starts = [tiles * sum(PARTS[:number]) // sum(PARTS) for number in range(len(PARTS) + 1)]
    held, range_of = slots, 0
    for start, end in zip(starts, starts[1:]):
        share = (end - start) // 4
        quarter, rest = (slots - start) // share, (slots - start) % share
        at = start + rest + share * ((quarter // 2 ^ group) + 2 * (quarter % 2 ^ core))
        held = jnp.where((slots >= start) & (slots < end), at, held)
    for first, end in RANGES[1:]:
        range_of += jnp.where(slots >= starts[first], 1, 0)

    own_wave = to_bricks(side)
    other_wave = to_bricks(1 - side)
    matrix = two_parts(coupling_matrix(coupling))

    arrived, pieces, across = [], [], None
    source = projectors
    for number, (start, end) in enumerate(zip(starts, starts[1:])):
        share = (end - start) // 4
        start += (2 * group + core) * share
        sent = lax.dynamic_slice_in_dim(source, start, share, 0)
        if number == 0:
            sent, source = lax.optimization_barrier((sent, source))
        if number > 0:
            sent = lax.optimization_barrier((sent, arrived[0] if number == 1 else others))[0]
        arrived.append(lax.ppermute(sent, "grid", partners))
        if number == 0:
            numbers = jnp.stack([tile_segment, tile_block, jnp.broadcast_to(tile_count, (tiles,))])
            numbers = lax.optimization_barrier((numbers, arrived[0]))[0]
            others = lax.ppermute(numbers, "grid", partners)

    absent = segments << bits(tiles)
    segment, block = (jnp.stack([numbers[i], others[i]]) for i in (0, 1))
    codes = jnp.stack([slots, held])
    codes += (segment + (block << bits(segments + 1))) << bits(tiles)
    live = slots < jnp.stack([numbers[2], others[2]])
    keys = block + blocks * jnp.stack([jnp.zeros_like(slots), range_of])
    meta = jnp.concatenate(
        [
            jnp.stack([place, numbers[2, 0], others[2, 0]]),
            group_lists(codes, keys, live, blocks, absent),
        ]
    )

    own_wave = lax.optimization_barrier((own_wave, arrived[-1]))[0]
    own_spot = (OWN, 0, len(RANGES), 0)
    total = project(sizes, meta, own_wave, [projectors], half, width, own_spot, us=10)
    for number, mine in enumerate(arrived):
        sent = mine
        if number == 1:
            sent, across, matrix = lax.optimization_barrier((sent, across, matrix))
        if number == 2:
            sent, across, other_wave = lax.optimization_barrier((sent, across, other_wave))
        across = lax.ppermute(sent, "groups", swap)
        pieces += [mine, across]
        pieces += [lax.ppermute(mine, "band", swap), lax.ppermute(across, "band", swap)]

    for number, (first, end) in enumerate(RANGES):
        last = end == len(PARTS)
        total = project(
            sizes,
            meta,
            other_wave,
            pieces[4 * first : 4 * end],
            half,
            width,
            (OTHER, number, number + 1, starts[first]),
            total,
            last=last,
            us=0 if last else 8,
        )
    if len(total) < half:
        total = [lax.dynamic_slice_in_dim(total[0], (place ^ d) * bands, bands, 0) for d in range(half)]

    applied = couple(exchange(total), *matrix)
    applied = exchange([applied] * half)

    result = jnp.zeros((bands, npts), jnp.bfloat16)
    for which, field in (
        (1 - side, spread(sizes, meta, applied, pieces, points, OTHER)),
        (side, spread(sizes, meta, applied, [projectors], points, OWN)),
    ):
        for d, block in enumerate(exchange(field)):
            start = (which * half + (place ^ d)) * points
            result = lax.dynamic_update_slice_in_dim(result, block, start, 1)
    return result


def solution(mesh):
    in_specs = (
        P(("groups", "grid", "band"), None),
        P("grid"),
        P("grid"),
        P("grid"),
        P("grid", None, None),
        P(),
    )
    out_specs = P(("groups", "grid", "band"), None)
    return jax.shard_map(
        functools.partial(body, mesh.shape["grid"]),
        mesh=mesh,
        in_specs=in_specs,
        out_specs=out_specs,
        check_vma=False,
    )
```

```python
import functools
import math

import jax
import jax.numpy as jnp
from jax import lax
from jax.experimental import pallas as pl
from jax.experimental.pallas import tpu as pltpu
from jax.sharding import PartitionSpec as P

TILE = 64
PAIR = 2 * TILE
GROUP = 4
UNROLL = 8
VMEM_SLACK = 10 * 1024 * 1024
PARTS = (17, 17, 14)
RANGES = ((0, 2), (2, 3))
OWN, OTHER = range(2)
BOUNDS = 3
STEPS = len(RANGES) + 1
LISTS = BOUNDS + 2 * STEPS


def bits(count):
    return max(1, (count - 1).bit_length())


def list_length(tiles, blocks):
    return tiles + len(RANGES) * ((GROUP - 1) * blocks + GROUP * UNROLL)


def group_lists(codes, keys, live, blocks, absent):
    n_lists, tiles = codes.shape
    n_keys = len(RANGES) * blocks
    order = jnp.arange(tiles, dtype=jnp.int32)
    key_range = jnp.arange(n_keys, dtype=jnp.int32)
    ranges = jnp.arange(STEPS, dtype=jnp.int32)
    mine = (keys[:, None, :] == key_range[None, :, None]) & live[:, None, :]
    groups = (jnp.sum(mine, axis=2, dtype=jnp.int32) + GROUP - 1) // GROUP
    in_range = key_range[:, None] // blocks == ranges[None, :]
    totals = jnp.sum(jnp.where(in_range, groups[:, :, None], 0), axis=1, dtype=jnp.int32)
    totals = (totals + UNROLL - 1) // UNROLL * UNROLL
    bounds = jnp.sum(
        jnp.where(ranges[:, None] < ranges[None, :], totals[:, :, None], 0), axis=1, dtype=jnp.int32
    )
    lower = (key_range[:, None] < key_range[None, :]) & (
        key_range[:, None] // blocks == key_range[None, :] // blocks
    )
    starts = jnp.sum(jnp.where(lower, groups[:, :, None], 0), axis=1, dtype=jnp.int32)
    starts += jnp.sum(jnp.where(in_range, bounds[:, None, :], 0), axis=2, dtype=jnp.int32)
    before = (
        (keys[:, :, None] == keys[:, None, :]) & live[:, :, None] & (order[:, None] < order[None, :])
    )
    entry = jnp.sum(before, axis=1, dtype=jnp.int32) + GROUP * jnp.sum(
        jnp.where(mine, starts[:, :, None], 0), axis=1, dtype=jnp.int32
    )
    entry = jnp.where(live, entry, -1)
    found = entry[:, :, None] == jnp.arange(list_length(tiles, blocks), dtype=jnp.int32)
    entries = absent + jnp.sum(
        jnp.where(found, codes[:, :, None] - absent, 0), axis=1, dtype=jnp.int32
    )
    return jnp.concatenate([bounds.reshape(-1), entries.reshape(-1)])


def group_loop(sizes, meta, values, proj, which, first, last, origin, product):
    tiles, segments, blocks = sizes
    begin, end = (meta[BOUNDS + STEPS * which + number] for number in (first, last))
    base = LISTS + which * list_length(tiles, blocks)

    def group(number):
        places = []
        for entry in range(GROUP):
            code = meta[base + GROUP * number + entry]
            index = jnp.maximum((code & ((1 << bits(tiles)) - 1)) - origin, 0)
            code = code >> bits(tiles)
            places.append((code & ((1 << bits(segments + 1)) - 1), values[index]))
            if entry == 0:
                block = code >> bits(segments + 1)
        lanes = pl.ds(pl.multiple_of(block * proj, proj), proj)
        return product(lanes, [at for at, tile in places], [tile for at, tile in places])

    def step(index, carry):
        sums = [group(begin + index * UNROLL + lane) for lane in range(UNROLL)]
        for additions in sums:
            for ref, rows, lanes, term in additions:
                ref[rows, lanes] += term
        return carry

    lax.fori_loop(0, (end - begin) // UNROLL, step, 0)


def join_pieces(meta, pieces, joined, first):
    end = 0
    for number, ref in enumerate(pieces):
        start, end = end, end + ref.shape[0]

        @pl.when(meta[2] > first + start - number % 4 * ref.shape[0])
        def copy(start=start, end=end, ref=ref):
            joined[start:end] = ref[...]


def rows_of(refs, lanes):
    return jnp.concatenate([ref[:, lanes] for ref in refs], axis=0)


def turn_waves(wave, turned, segments):
    for pair in range(segments // 2):
        values = wave[:, pair * PAIR : (pair + 1) * PAIR]
        turned[0, pair] = values
        turned[1, pair] = pltpu.roll(values.astype(jnp.float32), TILE, 1).astype(values.dtype)
    for way in range(2):
        turned[way, segments // 2] = jnp.zeros(turned.shape[2:], turned.dtype)


def project_kernel(sizes, n_pieces, spot, first, last, meta, wave, *refs):
    pieces, refs = refs[:n_pieces], refs[n_pieces:]
    turned, refs = refs[-1], refs[:-1]
    if not first:
        before, refs = refs[0], refs[1:]
    values = pieces[0]
    if n_pieces > 1:
        values, refs = refs[-1], refs[:-1]
        join_pieces(meta, pieces, values, spot[-1])
    total = refs[-1]
    total[...] = jnp.zeros_like(total) if first else before[...]
    every = slice(None)

    def product(lanes, segments, tiles):
        low = lax.broadcasted_iota(jnp.int32, turned.shape[2:], 1) < TILE
        waves = [
            jnp.where(
                low,
                turned[segments[at] & 1, segments[at] >> 1],
                turned[1 - (segments[at + 1] & 1), segments[at + 1] >> 1],
            )
            for at in range(0, GROUP, 2)
        ]
        term = jnp.dot(
            jnp.concatenate(waves, axis=1),
            jnp.concatenate(tiles, axis=0),
            preferred_element_type=jnp.float32,
        )
        return [(total, every, lanes, term)]

    @pl.when(meta[1 + spot[0]] > spot[-1])
    def loop():
        turn_waves(wave, turned, sizes[1])
        group_loop(sizes, meta, values, values.shape[2], *spot, product)

    if last:
        outs = refs[:-1]
        rows = outs[0].shape[0]
        for d, out in enumerate(outs):
            start = 0 if len(outs) == 1 else pl.multiple_of((meta[0] ^ d) * rows, rows)
            out[...] = total[pl.ds(start, rows), :].astype(out.dtype)


def spread_kernel(sizes, n_rows, n_pieces, which, meta, *refs):
    applied, refs = refs[:n_rows], refs[n_rows:]
    pieces, refs = refs[:n_pieces], refs[n_pieces:]
    values = pieces[0]
    if n_pieces > 1:
        values, refs = refs[-1], refs[:-1]
        join_pieces(meta, pieces, values, 0)
    outs, field = refs[:-1], refs[-1]
    field[...] = jnp.zeros_like(field)
    every = slice(None)

    def product(lanes, segments, tiles):
        terms = lax.dot_general(
            jnp.concatenate(tiles, axis=0),
            rows_of(applied, lanes),
            (((1,), (1,)), ((), ())),
            preferred_element_type=jnp.float32,
        )
        return [
            (
                field,
                pl.ds(pl.multiple_of(at * TILE, TILE), TILE),
                every,
                terms[number * TILE : (number + 1) * TILE],
            )
            for number, at in enumerate(segments)
        ]

    group_loop(sizes, meta, values, values.shape[2], which, 0, len(RANGES), 0, product)
    for pair in range(sizes[1] // 2):
        points = slice(pair * PAIR, (pair + 1) * PAIR)
        values, start = field[points, :].T, 0
        for out in outs:
            out[:, points] = values[start : start + out.shape[0]].astype(out.dtype)
            start += out.shape[0]


WHOLE = pl.BlockSpec(memory_space=pltpu.VMEM)


def cost(us):
    return pl.CostEstimate(flops=1 + us * 10**9, bytes_accessed=1, transcendentals=0)


def join_small(blocks):
    return blocks if blocks[0].shape[0] % 16 == 0 else [jnp.concatenate(blocks)]


def split_small(blocks, count):
    return blocks if len(blocks) == count else jnp.split(blocks[0], count)


def vmem(scratch):
    size = sum(math.prod(ref.shape) * jnp.dtype(ref.dtype).itemsize for ref in scratch)
    return pltpu.CompilerParams(vmem_limit_bytes=size + VMEM_SLACK)


def joined_shape(pieces):
    if len(pieces) == 1:
        return []
    count = sum(piece.shape[0] for piece in pieces)
    return [pltpu.VMEM((count,) + pieces[0].shape[1:], jnp.bfloat16)]


def project(sizes, meta, wave, pieces, count, width, spot, total=None, last=False, us=0):
    rows = wave.shape[0]
    operands = [wave, *pieces] + ([] if total is None else [total])
    scratch = joined_shape(pieces)
    scratch.append(pltpu.VMEM((2, sizes[1] // 2 + 1, rows, PAIR), jnp.bfloat16))
    if last:
        outs = count if rows // count % 16 == 0 else 1
        shapes = [jax.ShapeDtypeStruct((rows // outs, width), jnp.bfloat16)] * outs
        scratch = [pltpu.VMEM((rows, width), jnp.float32)] + scratch
    else:
        shapes = [jax.ShapeDtypeStruct((rows, width), jnp.float32)]
    result = pl.pallas_call(
        functools.partial(project_kernel, sizes, len(pieces), spot, total is None, last),
        grid_spec=pltpu.PrefetchScalarGridSpec(
            num_scalar_prefetch=1,
            grid=(1,),
            in_specs=[WHOLE] * len(operands),
            out_specs=[WHOLE] * len(shapes),
            scratch_shapes=scratch,
        ),
        out_shape=shapes,
        compiler_params=vmem(scratch),
        cost_estimate=cost(us),
    )(meta, *operands)
    return list(result) if last else result[0]


def spread(sizes, meta, applied, pieces, points, which):
    count = len(applied)
    applied = join_small(applied)
    rows = sum(block.shape[0] for block in applied)
    scratch = [pltpu.VMEM((points + TILE, rows), jnp.float32)] + joined_shape(pieces)
    result = pl.pallas_call(
        functools.partial(spread_kernel, sizes, len(applied), len(pieces), which),
        grid_spec=pltpu.PrefetchScalarGridSpec(
            num_scalar_prefetch=1,
            grid=(1,),
            in_specs=[WHOLE] * (len(applied) + len(pieces)),
            out_specs=[WHOLE] * len(applied),
            scratch_shapes=scratch,
        ),
        out_shape=[
            jax.ShapeDtypeStruct((block.shape[0], points), jnp.bfloat16) for block in applied
        ],
        compiler_params=vmem(scratch),
        cost_estimate=cost(0),
    )(meta, *applied, *pieces)
    return split_small(result, count)


def two_parts(values):
    high = values.astype(jnp.bfloat16)
    return high, (values - high.astype(jnp.float32)).astype(jnp.bfloat16)


def couple_kernel(high_ref, low_ref, *refs):
    parts, out_ref = refs[:-1], refs[-1]
    blocks, proj, unused = high_ref.shape
    for block in range(blocks):
        lanes = slice(block * proj, (block + 1) * proj)
        total = parts[0][:, lanes].astype(jnp.float32)
        for part in parts[1:]:
            total += part[:, lanes].astype(jnp.float32)
        high, low = two_parts(total)
        result = jnp.dot(high, high_ref[block], preferred_element_type=jnp.float32)
        result += jnp.dot(high, low_ref[block], preferred_element_type=jnp.float32)
        result += jnp.dot(low, high_ref[block], preferred_element_type=jnp.float32)
        out_ref[:, lanes] = result.astype(out_ref.dtype)


def couple(parts, high, low):
    return pl.pallas_call(
        couple_kernel,
        in_specs=[WHOLE] * (2 + len(parts)),
        out_specs=WHOLE,
        out_shape=jax.ShapeDtypeStruct(parts[0].shape, jnp.bfloat16),
        compiler_params=vmem([]),
        cost_estimate=cost(0),
    )(high, low, *parts)


def coupling_matrix(coupling):
    blocks, atoms, width, unused = coupling.shape
    proj = atoms * width
    wide = jnp.tile(coupling.reshape(blocks, proj, width), (1, 1, atoms))
    same = jnp.arange(proj)[:, None] // width == jnp.arange(proj)[None, :] // width
    return jnp.where(same[None], wide, 0.0)


def body(n_grid, wavefunctions, tile_segment, tile_block, tile_count, projectors, coupling):
    half = n_grid // 2
    bands, npts = wavefunctions.shape
    points = npts // n_grid
    tiles = projectors.shape[0]
    width = coupling.shape[0] * projectors.shape[2]
    index = lax.axis_index("grid")
    side, place = index // half, index % half
    group, core = lax.axis_index("groups"), lax.axis_index("band")
    partners = [(i, (i + half) % n_grid) for i in range(n_grid)]
    pools = [list(range(half)), list(range(half, n_grid))]
    swap = [(0, 1), (1, 0)]

    def exchange(blocks):
        return [blocks[0]] + [
            lax.ppermute(
                blocks[d], "grid", [(i, i // half * half + (i % half ^ d)) for i in range(n_grid)]
            )
            for d in range(1, half)
        ]

    def to_bricks(which):
        part = lax.dynamic_slice_in_dim(wavefunctions, which * half * points, half * points, 1)
        return lax.all_to_all(
            part, "grid", split_axis=1, concat_axis=0, tiled=True, axis_index_groups=pools
        )

    segments, blocks = points // TILE, coupling.shape[0]
    sizes = (tiles, segments, blocks)
    slots = jnp.arange(tiles, dtype=jnp.int32)
    starts = [tiles * sum(PARTS[:number]) // sum(PARTS) for number in range(len(PARTS) + 1)]
    held, range_of = slots, 0
    for start, end in zip(starts, starts[1:]):
        share = (end - start) // 4
        quarter, rest = (slots - start) // share, (slots - start) % share
        at = start + rest + share * ((quarter // 2 ^ group) + 2 * (quarter % 2 ^ core))
        held = jnp.where((slots >= start) & (slots < end), at, held)
    for first, end in RANGES[1:]:
        range_of += jnp.where(slots >= starts[first], 1, 0)

    own_wave = to_bricks(side)
    other_wave = to_bricks(1 - side)
    matrix = two_parts(coupling_matrix(coupling))

    arrived, pieces, across = [], [], None
    source = projectors
    for number, (start, end) in enumerate(zip(starts, starts[1:])):
        share = (end - start) // 4
        start += (2 * group + core) * share
        sent = lax.dynamic_slice_in_dim(source, start, share, 0)
        if number == 0:
            sent, source = lax.optimization_barrier((sent, source))
        if number > 0:
            sent = lax.optimization_barrier((sent, arrived[0] if number == 1 else shared))[0]
        arrived.append(lax.ppermute(sent, "grid", partners))
        if number == 0:
            numbers = jnp.stack([tile_segment, tile_block, jnp.broadcast_to(tile_count, (tiles,))])
            numbers = lax.optimization_barrier((numbers, arrived[0]))[0]
            others = lax.ppermute(numbers, "grid", partners)
            shared = (others, lax.ppermute(arrived[0], "groups", swap))

    absent = segments << bits(tiles)
    segment, block = (jnp.stack([numbers[i], others[i]]) for i in (0, 1))
    codes = jnp.stack([slots, held])
    codes += (segment + (block << bits(segments + 1))) << bits(tiles)
    live = slots < jnp.stack([numbers[2], others[2]])
    keys = block + blocks * jnp.stack([jnp.zeros_like(slots), range_of])
    meta = jnp.concatenate(
        [
            jnp.stack([place, numbers[2, 0], others[2, 0]]),
            group_lists(codes, keys, live, blocks, absent),
        ]
    )

    own_wave = lax.optimization_barrier((own_wave, arrived[-1]))[0]
    own_spot = (OWN, 0, len(RANGES), 0)
    total = project(sizes, meta, own_wave, [projectors], half, width, own_spot, us=10)
    for number, mine in enumerate(arrived):
        sent = mine
        if number == 1:
            sent, across, matrix = lax.optimization_barrier((sent, across, matrix))
        if number == 2:
            sent, across, other_wave = lax.optimization_barrier((sent, across, other_wave))
        across = lax.ppermute(sent, "groups", swap) if number > 0 else shared[1]
        pieces += [mine, across]
        pieces += [lax.ppermute(mine, "band", swap), lax.ppermute(across, "band", swap)]

    for number, (first, end) in enumerate(RANGES):
        last = end == len(PARTS)
        total = project(
            sizes,
            meta,
            other_wave,
            pieces[4 * first : 4 * end],
            half,
            width,
            (OTHER, number, number + 1, starts[first]),
            total,
            last=last,
            us=0 if last else 8,
        )
    if len(total) < half:
        total = [lax.dynamic_slice_in_dim(total[0], (place ^ d) * bands, bands, 0) for d in range(half)]

    applied = couple(exchange(total), *matrix)
    applied = exchange([applied] * half)

    result = jnp.zeros((bands, npts), jnp.bfloat16)
    for which, field in (
        (1 - side, spread(sizes, meta, applied, pieces, points, OTHER)),
        (side, spread(sizes, meta, applied, [projectors], points, OWN)),
    ):
        for d, block in enumerate(exchange(field)):
            start = (which * half + (place ^ d)) * points
            result = lax.dynamic_update_slice_in_dim(result, block, start, 1)
    return result


def solution(mesh):
    in_specs = (
        P(("groups", "grid", "band"), None),
        P("grid"),
        P("grid"),
        P("grid"),
        P("grid", None, None),
        P(),
    )
    out_specs = P(("groups", "grid", "band"), None)
    return jax.shard_map(
        functools.partial(body, mesh.shape["grid"]),
        mesh=mesh,
        in_specs=in_specs,
        out_specs=out_specs,
        check_vma=False,
    )
```

```python
import functools
import math

import jax
import jax.numpy as jnp
from jax import lax
from jax.experimental import pallas as pl
from jax.experimental.pallas import tpu as pltpu
from jax.sharding import PartitionSpec as P

TILE = 64
PAIR = 2 * TILE
GROUP = 4
UNROLL = 8
VMEM_SLACK = 10 * 1024 * 1024
PARTS = (17, 17, 14)
RANGES = ((0, 2), (2, 3))
OWN, OTHER = range(2)
BOUNDS = 3
STEPS = len(RANGES) + 1
LISTS = BOUNDS + 2 * STEPS


def bits(count):
    return max(1, (count - 1).bit_length())


def list_length(tiles, blocks):
    return tiles + len(RANGES) * ((GROUP - 1) * blocks + GROUP * UNROLL)


def group_lists(codes, keys, live, blocks, absent):
    n_lists, tiles = codes.shape
    n_keys = len(RANGES) * blocks
    order = jnp.arange(tiles, dtype=jnp.int32)
    key_range = jnp.arange(n_keys, dtype=jnp.int32)
    ranges = jnp.arange(STEPS, dtype=jnp.int32)
    mine = (keys[:, None, :] == key_range[None, :, None]) & live[:, None, :]
    groups = (jnp.sum(mine, axis=2, dtype=jnp.int32) + GROUP - 1) // GROUP
    in_range = key_range[:, None] // blocks == ranges[None, :]
    totals = jnp.sum(jnp.where(in_range, groups[:, :, None], 0), axis=1, dtype=jnp.int32)
    totals = (totals + UNROLL - 1) // UNROLL * UNROLL
    bounds = jnp.sum(
        jnp.where(ranges[:, None] < ranges[None, :], totals[:, :, None], 0), axis=1, dtype=jnp.int32
    )
    lower = (key_range[:, None] < key_range[None, :]) & (
        key_range[:, None] // blocks == key_range[None, :] // blocks
    )
    starts = jnp.sum(jnp.where(lower, groups[:, :, None], 0), axis=1, dtype=jnp.int32)
    starts += jnp.sum(jnp.where(in_range, bounds[:, None, :], 0), axis=2, dtype=jnp.int32)
    before = (
        (keys[:, :, None] == keys[:, None, :]) & live[:, :, None] & (order[:, None] < order[None, :])
    )
    entry = jnp.sum(before, axis=1, dtype=jnp.int32) + GROUP * jnp.sum(
        jnp.where(mine, starts[:, :, None], 0), axis=1, dtype=jnp.int32
    )
    entry = jnp.where(live, entry, -1)
    found = entry[:, :, None] == jnp.arange(list_length(tiles, blocks), dtype=jnp.int32)
    entries = absent + jnp.sum(
        jnp.where(found, codes[:, :, None] - absent, 0), axis=1, dtype=jnp.int32
    )
    return jnp.concatenate([bounds.reshape(-1), entries.reshape(-1)])


def group_loop(sizes, meta, values, proj, which, first, last, origin, product):
    tiles, segments, blocks = sizes
    begin, end = (meta[BOUNDS + STEPS * which + number] for number in (first, last))
    base = LISTS + which * list_length(tiles, blocks)

    def group(number):
        places = []
        for entry in range(GROUP):
            code = meta[base + GROUP * number + entry]
            index = jnp.maximum((code & ((1 << bits(tiles)) - 1)) - origin, 0)
            code = code >> bits(tiles)
            places.append((code & ((1 << bits(segments + 1)) - 1), values[index]))
            if entry == 0:
                block = code >> bits(segments + 1)
        lanes = pl.ds(pl.multiple_of(block * proj, proj), proj)
        return product(lanes, [at for at, tile in places], [tile for at, tile in places])

    def step(index, carry):
        sums = [group(begin + index * UNROLL + lane) for lane in range(UNROLL)]
        for additions in sums:
            for ref, rows, lanes, term in additions:
                ref[rows, lanes] += term
        return carry

    lax.fori_loop(0, (end - begin) // UNROLL, step, 0)


def join_pieces(meta, pieces, joined, first):
    end = 0
    for number, ref in enumerate(pieces):
        start, end = end, end + ref.shape[0]

        @pl.when(meta[2] > first + start - number % 4 * ref.shape[0])
        def copy(start=start, end=end, ref=ref):
            joined[start:end] = ref[...]


def rows_of(refs, lanes):
    return jnp.concatenate([ref[:, lanes] for ref in refs], axis=0)


def turn_waves(wave, turned, segments):
    for pair in range(segments // 2):
        values = wave[:, pair * PAIR : (pair + 1) * PAIR]
        turned[0, pair] = values
        turned[1, pair] = pltpu.roll(values.astype(jnp.float32), TILE, 1).astype(values.dtype)
    for way in range(2):
        turned[way, segments // 2] = jnp.zeros(turned.shape[2:], turned.dtype)


def project_kernel(sizes, n_pieces, spot, first, last, meta, wave, *refs):
    pieces, refs = refs[:n_pieces], refs[n_pieces:]
    turned, refs = refs[-1], refs[:-1]
    if not first:
        before, refs = refs[0], refs[1:]
    values = pieces[0]
    if n_pieces > 1:
        values, refs = refs[-1], refs[:-1]
        join_pieces(meta, pieces, values, spot[-1])
    total = refs[-1]
    total[...] = jnp.zeros_like(total) if first else before[...]
    every = slice(None)

    def product(lanes, segments, tiles):
        low = lax.broadcasted_iota(jnp.int32, turned.shape[2:], 1) < TILE
        waves = [
            jnp.where(
                low,
                turned[segments[at] & 1, segments[at] >> 1],
                turned[1 - (segments[at + 1] & 1), segments[at + 1] >> 1],
            )
            for at in range(0, GROUP, 2)
        ]
        term = jnp.dot(
            jnp.concatenate(waves, axis=1),
            jnp.concatenate(tiles, axis=0),
            preferred_element_type=jnp.float32,
        )
        return [(total, every, lanes, term)]

    @pl.when(meta[1 + spot[0]] > spot[-1])
    def loop():
        turn_waves(wave, turned, sizes[1])
        group_loop(sizes, meta, values, values.shape[2], *spot, product)

    if last:
        outs = refs[:-1]
        rows = outs[0].shape[0]
        for d, out in enumerate(outs):
            start = 0 if len(outs) == 1 else pl.multiple_of((meta[0] ^ d) * rows, rows)
            out[...] = total[pl.ds(start, rows), :].astype(out.dtype)


def spread_kernel(sizes, n_rows, n_pieces, which, meta, *refs):
    applied, refs = refs[:n_rows], refs[n_rows:]
    pieces, refs = refs[:n_pieces], refs[n_pieces:]
    values = pieces[0]
    if n_pieces > 1:
        values, refs = refs[-1], refs[:-1]
        join_pieces(meta, pieces, values, 0)
    outs, field = refs[:-1], refs[-1]
    field[...] = jnp.zeros_like(field)
    every = slice(None)

    def product(lanes, segments, tiles):
        terms = lax.dot_general(
            jnp.concatenate(tiles, axis=0),
            rows_of(applied, lanes),
            (((1,), (1,)), ((), ())),
            preferred_element_type=jnp.float32,
        )
        return [
            (
                field,
                pl.ds(pl.multiple_of(at * TILE, TILE), TILE),
                every,
                terms[number * TILE : (number + 1) * TILE],
            )
            for number, at in enumerate(segments)
        ]

    group_loop(sizes, meta, values, values.shape[2], which, 0, len(RANGES), 0, product)
    for pair in range(sizes[1] // 2):
        points = slice(pair * PAIR, (pair + 1) * PAIR)
        values, start = field[points, :].T, 0
        for out in outs:
            out[:, points] = values[start : start + out.shape[0]].astype(out.dtype)
            start += out.shape[0]


WHOLE = pl.BlockSpec(memory_space=pltpu.VMEM)


def cost(us):
    return pl.CostEstimate(flops=1 + us * 10**9, bytes_accessed=1, transcendentals=0)


def join_small(blocks):
    return blocks if blocks[0].shape[0] % 16 == 0 else [jnp.concatenate(blocks)]


def split_small(blocks, count):
    return blocks if len(blocks) == count else jnp.split(blocks[0], count)


def vmem(scratch):
    size = sum(math.prod(ref.shape) * jnp.dtype(ref.dtype).itemsize for ref in scratch)
    return pltpu.CompilerParams(vmem_limit_bytes=size + VMEM_SLACK)


def joined_shape(pieces):
    if len(pieces) == 1:
        return []
    count = sum(piece.shape[0] for piece in pieces)
    return [pltpu.VMEM((count,) + pieces[0].shape[1:], jnp.bfloat16)]


def project(sizes, meta, wave, pieces, count, width, spot, total=None, last=False, us=0):
    rows = wave.shape[0]
    operands = [wave, *pieces] + ([] if total is None else [total])
    scratch = joined_shape(pieces)
    scratch.append(pltpu.VMEM((2, sizes[1] // 2 + 1, rows, PAIR), jnp.bfloat16))
    if last:
        outs = count if rows // count % 16 == 0 else 1
        shapes = [jax.ShapeDtypeStruct((rows // outs, width), jnp.bfloat16)] * outs
        scratch = [pltpu.VMEM((rows, width), jnp.float32)] + scratch
    else:
        shapes = [jax.ShapeDtypeStruct((rows, width), jnp.float32)]
    result = pl.pallas_call(
        functools.partial(project_kernel, sizes, len(pieces), spot, total is None, last),
        grid_spec=pltpu.PrefetchScalarGridSpec(
            num_scalar_prefetch=1,
            grid=(1,),
            in_specs=[WHOLE] * len(operands),
            out_specs=[WHOLE] * len(shapes),
            scratch_shapes=scratch,
        ),
        out_shape=shapes,
        compiler_params=vmem(scratch),
        cost_estimate=cost(us),
    )(meta, *operands)
    return list(result) if last else result[0]


def spread(sizes, meta, applied, pieces, points, which):
    count = len(applied)
    applied = join_small(applied)
    rows = sum(block.shape[0] for block in applied)
    scratch = [pltpu.VMEM((points + TILE, rows), jnp.float32)] + joined_shape(pieces)
    result = pl.pallas_call(
        functools.partial(spread_kernel, sizes, len(applied), len(pieces), which),
        grid_spec=pltpu.PrefetchScalarGridSpec(
            num_scalar_prefetch=1,
            grid=(1,),
            in_specs=[WHOLE] * (len(applied) + len(pieces)),
            out_specs=[WHOLE] * len(applied),
            scratch_shapes=scratch,
        ),
        out_shape=[
            jax.ShapeDtypeStruct((block.shape[0], points), jnp.bfloat16) for block in applied
        ],
        compiler_params=vmem(scratch),
        cost_estimate=cost(0),
    )(meta, *applied, *pieces)
    return split_small(result, count)


def two_parts(values):
    high = values.astype(jnp.bfloat16)
    return high, (values - high.astype(jnp.float32)).astype(jnp.bfloat16)


def couple_kernel(high_ref, low_ref, *refs):
    parts, out_ref = refs[:-1], refs[-1]
    blocks, proj, unused = high_ref.shape
    for block in range(blocks):
        lanes = slice(block * proj, (block + 1) * proj)
        total = parts[0][:, lanes].astype(jnp.float32)
        for part in parts[1:]:
            total += part[:, lanes].astype(jnp.float32)
        high, low = two_parts(total)
        result = jnp.dot(high, high_ref[block], preferred_element_type=jnp.float32)
        result += jnp.dot(high, low_ref[block], preferred_element_type=jnp.float32)
        result += jnp.dot(low, high_ref[block], preferred_element_type=jnp.float32)
        out_ref[:, lanes] = result.astype(out_ref.dtype)


def couple(parts, high, low):
    return pl.pallas_call(
        couple_kernel,
        in_specs=[WHOLE] * (2 + len(parts)),
        out_specs=WHOLE,
        out_shape=jax.ShapeDtypeStruct(parts[0].shape, jnp.bfloat16),
        compiler_params=vmem([]),
        cost_estimate=cost(0),
    )(high, low, *parts)


def coupling_matrix(coupling):
    blocks, atoms, width, unused = coupling.shape
    proj = atoms * width
    wide = jnp.tile(coupling.reshape(blocks, proj, width), (1, 1, atoms))
    same = jnp.arange(proj)[:, None] // width == jnp.arange(proj)[None, :] // width
    return jnp.where(same[None], wide, 0.0)


def body(n_grid, wavefunctions, tile_segment, tile_block, tile_count, projectors, coupling):
    half = n_grid // 2
    bands, npts = wavefunctions.shape
    points = npts // n_grid
    tiles = projectors.shape[0]
    width = coupling.shape[0] * projectors.shape[2]
    index = lax.axis_index("grid")
    side, place = index // half, index % half
    group, core = lax.axis_index("groups"), lax.axis_index("band")
    partners = [(i, (i + half) % n_grid) for i in range(n_grid)]
    pools = [list(range(half)), list(range(half, n_grid))]
    swap = [(0, 1), (1, 0)]

    def exchange(blocks):
        return [blocks[0]] + [
            lax.ppermute(
                blocks[d], "grid", [(i, i // half * half + (i % half ^ d)) for i in range(n_grid)]
            )
            for d in range(1, half)
        ]

    def to_bricks(which):
        part = lax.dynamic_slice_in_dim(wavefunctions, which * half * points, half * points, 1)
        return lax.all_to_all(
            part, "grid", split_axis=1, concat_axis=0, tiled=True, axis_index_groups=pools
        )

    segments, blocks = points // TILE, coupling.shape[0]
    sizes = (tiles, segments, blocks)
    slots = jnp.arange(tiles, dtype=jnp.int32)
    starts = [tiles * sum(PARTS[:number]) // sum(PARTS) for number in range(len(PARTS) + 1)]
    held, range_of = slots, 0
    for start, end in zip(starts, starts[1:]):
        share = (end - start) // 4
        quarter, rest = (slots - start) // share, (slots - start) % share
        at = start + rest + share * ((quarter // 2 ^ group) + 2 * (quarter % 2 ^ core))
        held = jnp.where((slots >= start) & (slots < end), at, held)
    for first, end in RANGES[1:]:
        range_of += jnp.where(slots >= starts[first], 1, 0)

    own_wave = to_bricks(side)
    other_wave = to_bricks(1 - side)
    matrix = two_parts(coupling_matrix(coupling))

    arrived, pieces, across = [], [], None
    source = projectors
    for number, (start, end) in enumerate(zip(starts, starts[1:])):
        share = (end - start) // 4
        start += (2 * group + core) * share
        sent = lax.dynamic_slice_in_dim(source, start, share, 0)
        if number == 0:
            sent, source = lax.optimization_barrier((sent, source))
        if number > 0:
            sent = lax.optimization_barrier((sent, arrived[0] if number == 1 else shared))[0]
        arrived.append(lax.ppermute(sent, "grid", partners))
        if number == 0:
            numbers = jnp.stack([tile_segment, tile_block, jnp.broadcast_to(tile_count, (tiles,))])
            numbers = lax.optimization_barrier((numbers, arrived[0]))[0]
            others = lax.ppermute(numbers, "grid", partners)
            shared = (others, lax.ppermute(arrived[0], "groups", swap))

    absent = segments << bits(tiles)
    segment, block = (jnp.stack([numbers[i], others[i]]) for i in (0, 1))
    codes = jnp.stack([slots, held])
    codes += (segment + (block << bits(segments + 1))) << bits(tiles)
    live = slots < jnp.stack([numbers[2], others[2]])
    keys = block + blocks * jnp.stack([jnp.zeros_like(slots), range_of])
    meta = jnp.concatenate(
        [
            jnp.stack([place, numbers[2, 0], others[2, 0]]),
            group_lists(codes, keys, live, blocks, absent),
        ]
    )

    own_wave = lax.optimization_barrier((own_wave, arrived[1]))[0]
    own_spot = (OWN, 0, len(RANGES), 0)
    total = project(sizes, meta, own_wave, [projectors], half, width, own_spot, us=2)
    for number, mine in enumerate(arrived):
        sent = mine
        if number == 1:
            sent, across, matrix = lax.optimization_barrier((sent, across, matrix))
        if number == 2:
            sent, across, other_wave = lax.optimization_barrier((sent, across, other_wave))
        across = lax.ppermute(sent, "groups", swap) if number > 0 else shared[1]
        if number == 0:
            mine, across, total = lax.optimization_barrier((mine, across, total))
        pieces += [mine, across]
        pieces += [lax.ppermute(mine, "band", swap), lax.ppermute(across, "band", swap)]

    for number, (first, end) in enumerate(RANGES):
        last = end == len(PARTS)
        total = project(
            sizes,
            meta,
            other_wave,
            pieces[4 * first : 4 * end],
            half,
            width,
            (OTHER, number, number + 1, starts[first]),
            total,
            last=last,
            us=0 if last else 8,
        )
    if len(total) < half:
        total = [lax.dynamic_slice_in_dim(total[0], (place ^ d) * bands, bands, 0) for d in range(half)]

    applied = couple(exchange(total), *matrix)
    applied = exchange([applied] * half)

    result = jnp.zeros((bands, npts), jnp.bfloat16)
    for which, field in (
        (1 - side, spread(sizes, meta, applied, pieces, points, OTHER)),
        (side, spread(sizes, meta, applied, [projectors], points, OWN)),
    ):
        for d, block in enumerate(exchange(field)):
            start = (which * half + (place ^ d)) * points
            result = lax.dynamic_update_slice_in_dim(result, block, start, 1)
    return result


def solution(mesh):
    in_specs = (
        P(("groups", "grid", "band"), None),
        P("grid"),
        P("grid"),
        P("grid"),
        P("grid", None, None),
        P(),
    )
    out_specs = P(("groups", "grid", "band"), None)
    return jax.shard_map(
        functools.partial(body, mesh.shape["grid"]),
        mesh=mesh,
        in_specs=in_specs,
        out_specs=out_specs,
        check_vma=False,
    )
```

```python
import functools
import math

import jax
import jax.numpy as jnp
from jax import lax
from jax.experimental import pallas as pl
from jax.experimental.pallas import tpu as pltpu
from jax.sharding import PartitionSpec as P

TILE = 64
PAIR = 2 * TILE
GROUP = 4
UNROLL = 8
VMEM_SLACK = 10 * 1024 * 1024
PARTS = (18, 18, 12)
RANGES = ((0, 2), (2, 3))
OWN, OTHER = range(2)
BOUNDS = 3
STEPS = len(RANGES) + 1
LISTS = BOUNDS + 2 * STEPS


def bits(count):
    return max(1, (count - 1).bit_length())


def list_length(tiles, blocks):
    return tiles + len(RANGES) * ((GROUP - 1) * blocks + GROUP * UNROLL)


def group_lists(codes, keys, live, blocks, absent):
    n_lists, tiles = codes.shape
    n_keys = len(RANGES) * blocks
    order = jnp.arange(tiles, dtype=jnp.int32)
    key_range = jnp.arange(n_keys, dtype=jnp.int32)
    ranges = jnp.arange(STEPS, dtype=jnp.int32)
    mine = (keys[:, None, :] == key_range[None, :, None]) & live[:, None, :]
    groups = (jnp.sum(mine, axis=2, dtype=jnp.int32) + GROUP - 1) // GROUP
    in_range = key_range[:, None] // blocks == ranges[None, :]
    totals = jnp.sum(jnp.where(in_range, groups[:, :, None], 0), axis=1, dtype=jnp.int32)
    totals = (totals + UNROLL - 1) // UNROLL * UNROLL
    bounds = jnp.sum(
        jnp.where(ranges[:, None] < ranges[None, :], totals[:, :, None], 0), axis=1, dtype=jnp.int32
    )
    lower = (key_range[:, None] < key_range[None, :]) & (
        key_range[:, None] // blocks == key_range[None, :] // blocks
    )
    starts = jnp.sum(jnp.where(lower, groups[:, :, None], 0), axis=1, dtype=jnp.int32)
    starts += jnp.sum(jnp.where(in_range, bounds[:, None, :], 0), axis=2, dtype=jnp.int32)
    before = (
        (keys[:, :, None] == keys[:, None, :]) & live[:, :, None] & (order[:, None] < order[None, :])
    )
    entry = jnp.sum(before, axis=1, dtype=jnp.int32) + GROUP * jnp.sum(
        jnp.where(mine, starts[:, :, None], 0), axis=1, dtype=jnp.int32
    )
    entry = jnp.where(live, entry, -1)
    found = entry[:, :, None] == jnp.arange(list_length(tiles, blocks), dtype=jnp.int32)
    entries = absent + jnp.sum(
        jnp.where(found, codes[:, :, None] - absent, 0), axis=1, dtype=jnp.int32
    )
    return jnp.concatenate([bounds.reshape(-1), entries.reshape(-1)])


def group_loop(sizes, meta, values, proj, which, first, last, origin, product):
    tiles, segments, blocks = sizes
    begin, end = (meta[BOUNDS + STEPS * which + number] for number in (first, last))
    base = LISTS + which * list_length(tiles, blocks)

    def group(number):
        places = []
        for entry in range(GROUP):
            code = meta[base + GROUP * number + entry]
            index = jnp.maximum((code & ((1 << bits(tiles)) - 1)) - origin, 0)
            code = code >> bits(tiles)
            places.append((code & ((1 << bits(segments + 1)) - 1), values[index]))
            if entry == 0:
                block = code >> bits(segments + 1)
        lanes = pl.ds(pl.multiple_of(block * proj, proj), proj)
        return product(lanes, [at for at, tile in places], [tile for at, tile in places])

    def step(index, carry):
        sums = [group(begin + index * UNROLL + lane) for lane in range(UNROLL)]
        for additions in sums:
            for ref, rows, lanes, term in additions:
                ref[rows, lanes] += term
        return carry

    lax.fori_loop(0, (end - begin) // UNROLL, step, 0)


def join_pieces(meta, pieces, joined, first):
    end = 0
    for number, ref in enumerate(pieces):
        start, end = end, end + ref.shape[0]

        @pl.when(meta[2] > first + start - number % 4 * ref.shape[0])
        def copy(start=start, end=end, ref=ref):
            joined[start:end] = ref[...]


def rows_of(refs, lanes):
    return jnp.concatenate([ref[:, lanes] for ref in refs], axis=0)


def turn_waves(wave, turned, segments):
    for pair in range(segments // 2):
        values = wave[:, pair * PAIR : (pair + 1) * PAIR]
        turned[0, pair] = values
        turned[1, pair] = pltpu.roll(values.astype(jnp.float32), TILE, 1).astype(values.dtype)
    for way in range(2):
        turned[way, segments // 2] = jnp.zeros(turned.shape[2:], turned.dtype)


def project_kernel(sizes, n_pieces, spot, first, last, meta, wave, *refs):
    pieces, refs = refs[:n_pieces], refs[n_pieces:]
    turned, refs = refs[-1], refs[:-1]
    if not first:
        before, refs = refs[0], refs[1:]
    values = pieces[0]
    if n_pieces > 1:
        values, refs = refs[-1], refs[:-1]
        join_pieces(meta, pieces, values, spot[-1])
    total = refs[-1]
    total[...] = jnp.zeros_like(total) if first else before[...]
    every = slice(None)

    def product(lanes, segments, tiles):
        low = lax.broadcasted_iota(jnp.int32, turned.shape[2:], 1) < TILE
        waves = [
            jnp.where(
                low,
                turned[segments[at] & 1, segments[at] >> 1],
                turned[1 - (segments[at + 1] & 1), segments[at + 1] >> 1],
            )
            for at in range(0, GROUP, 2)
        ]
        term = jnp.dot(
            jnp.concatenate(waves, axis=1),
            jnp.concatenate(tiles, axis=0),
            preferred_element_type=jnp.float32,
        )
        return [(total, every, lanes, term)]

    @pl.when(meta[1 + spot[0]] > spot[-1])
    def loop():
        turn_waves(wave, turned, sizes[1])
        group_loop(sizes, meta, values, values.shape[2], *spot, product)

    if last:
        outs = refs[:-1]
        rows = outs[0].shape[0]
        for d, out in enumerate(outs):
            start = 0 if len(outs) == 1 else pl.multiple_of((meta[0] ^ d) * rows, rows)
            out[...] = total[pl.ds(start, rows), :].astype(out.dtype)


def spread_kernel(sizes, n_rows, n_pieces, which, meta, *refs):
    applied, refs = refs[:n_rows], refs[n_rows:]
    pieces, refs = refs[:n_pieces], refs[n_pieces:]
    values = pieces[0]
    if n_pieces > 1:
        values, refs = refs[-1], refs[:-1]
        join_pieces(meta, pieces, values, 0)
    outs, field = refs[:-1], refs[-1]
    field[...] = jnp.zeros_like(field)
    every = slice(None)

    def product(lanes, segments, tiles):
        terms = lax.dot_general(
            jnp.concatenate(tiles, axis=0),
            rows_of(applied, lanes),
            (((1,), (1,)), ((), ())),
            preferred_element_type=jnp.float32,
        )
        return [
            (
                field,
                pl.ds(pl.multiple_of(at * TILE, TILE), TILE),
                every,
                terms[number * TILE : (number + 1) * TILE],
            )
            for number, at in enumerate(segments)
        ]

    group_loop(sizes, meta, values, values.shape[2], which, 0, len(RANGES), 0, product)
    for pair in range(sizes[1] // 2):
        points = slice(pair * PAIR, (pair + 1) * PAIR)
        values, start = field[points, :].T, 0
        for out in outs:
            out[:, points] = values[start : start + out.shape[0]].astype(out.dtype)
            start += out.shape[0]


WHOLE = pl.BlockSpec(memory_space=pltpu.VMEM)


def cost(us):
    return pl.CostEstimate(flops=1 + us * 10**9, bytes_accessed=1, transcendentals=0)


def join_small(blocks):
    return blocks if blocks[0].shape[0] % 16 == 0 else [jnp.concatenate(blocks)]


def split_small(blocks, count):
    return blocks if len(blocks) == count else jnp.split(blocks[0], count)


def vmem(scratch):
    size = sum(math.prod(ref.shape) * jnp.dtype(ref.dtype).itemsize for ref in scratch)
    return pltpu.CompilerParams(vmem_limit_bytes=size + VMEM_SLACK)


def joined_shape(pieces):
    if len(pieces) == 1:
        return []
    count = sum(piece.shape[0] for piece in pieces)
    return [pltpu.VMEM((count,) + pieces[0].shape[1:], jnp.bfloat16)]


def project(sizes, meta, wave, pieces, count, width, spot, total=None, last=False, us=0):
    rows = wave.shape[0]
    operands = [wave, *pieces] + ([] if total is None else [total])
    scratch = joined_shape(pieces)
    scratch.append(pltpu.VMEM((2, sizes[1] // 2 + 1, rows, PAIR), jnp.bfloat16))
    if last:
        outs = count if rows // count % 16 == 0 else 1
        shapes = [jax.ShapeDtypeStruct((rows // outs, width), jnp.bfloat16)] * outs
        scratch = [pltpu.VMEM((rows, width), jnp.float32)] + scratch
    else:
        shapes = [jax.ShapeDtypeStruct((rows, width), jnp.float32)]
    result = pl.pallas_call(
        functools.partial(project_kernel, sizes, len(pieces), spot, total is None, last),
        grid_spec=pltpu.PrefetchScalarGridSpec(
            num_scalar_prefetch=1,
            grid=(1,),
            in_specs=[WHOLE] * len(operands),
            out_specs=[WHOLE] * len(shapes),
            scratch_shapes=scratch,
        ),
        out_shape=shapes,
        compiler_params=vmem(scratch),
        cost_estimate=cost(us),
    )(meta, *operands)
    return list(result) if last else result[0]


def spread(sizes, meta, applied, pieces, points, which):
    count = len(applied)
    applied = join_small(applied)
    rows = sum(block.shape[0] for block in applied)
    scratch = [pltpu.VMEM((points + TILE, rows), jnp.float32)] + joined_shape(pieces)
    result = pl.pallas_call(
        functools.partial(spread_kernel, sizes, len(applied), len(pieces), which),
        grid_spec=pltpu.PrefetchScalarGridSpec(
            num_scalar_prefetch=1,
            grid=(1,),
            in_specs=[WHOLE] * (len(applied) + len(pieces)),
            out_specs=[WHOLE] * len(applied),
            scratch_shapes=scratch,
        ),
        out_shape=[
            jax.ShapeDtypeStruct((block.shape[0], points), jnp.bfloat16) for block in applied
        ],
        compiler_params=vmem(scratch),
        cost_estimate=cost(0),
    )(meta, *applied, *pieces)
    return split_small(result, count)


def two_parts(values):
    high = values.astype(jnp.bfloat16)
    return high, (values - high.astype(jnp.float32)).astype(jnp.bfloat16)


def couple_kernel(high_ref, low_ref, *refs):
    parts, out_ref = refs[:-1], refs[-1]
    blocks, proj, unused = high_ref.shape
    for block in range(blocks):
        lanes = slice(block * proj, (block + 1) * proj)
        total = parts[0][:, lanes].astype(jnp.float32)
        for part in parts[1:]:
            total += part[:, lanes].astype(jnp.float32)
        high, low = two_parts(total)
        result = jnp.dot(high, high_ref[block], preferred_element_type=jnp.float32)
        result += jnp.dot(high, low_ref[block], preferred_element_type=jnp.float32)
        result += jnp.dot(low, high_ref[block], preferred_element_type=jnp.float32)
        out_ref[:, lanes] = result.astype(out_ref.dtype)


def couple(parts, high, low):
    return pl.pallas_call(
        couple_kernel,
        in_specs=[WHOLE] * (2 + len(parts)),
        out_specs=WHOLE,
        out_shape=jax.ShapeDtypeStruct(parts[0].shape, jnp.bfloat16),
        compiler_params=vmem([]),
        cost_estimate=cost(0),
    )(high, low, *parts)


def coupling_matrix(coupling):
    blocks, atoms, width, unused = coupling.shape
    proj = atoms * width
    wide = jnp.tile(coupling.reshape(blocks, proj, width), (1, 1, atoms))
    same = jnp.arange(proj)[:, None] // width == jnp.arange(proj)[None, :] // width
    return jnp.where(same[None], wide, 0.0)


def body(n_grid, wavefunctions, tile_segment, tile_block, tile_count, projectors, coupling):
    half = n_grid // 2
    bands, npts = wavefunctions.shape
    points = npts // n_grid
    tiles = projectors.shape[0]
    width = coupling.shape[0] * projectors.shape[2]
    index = lax.axis_index("grid")
    side, place = index // half, index % half
    group, core = lax.axis_index("groups"), lax.axis_index("band")
    partners = [(i, (i + half) % n_grid) for i in range(n_grid)]
    pools = [list(range(half)), list(range(half, n_grid))]
    swap = [(0, 1), (1, 0)]

    def exchange(blocks):
        return [blocks[0]] + [
            lax.ppermute(
                blocks[d], "grid", [(i, i // half * half + (i % half ^ d)) for i in range(n_grid)]
            )
            for d in range(1, half)
        ]

    def to_bricks(which):
        part = lax.dynamic_slice_in_dim(wavefunctions, which * half * points, half * points, 1)
        return lax.all_to_all(
            part, "grid", split_axis=1, concat_axis=0, tiled=True, axis_index_groups=pools
        )

    segments, blocks = points // TILE, coupling.shape[0]
    sizes = (tiles, segments, blocks)
    slots = jnp.arange(tiles, dtype=jnp.int32)
    starts = [tiles * sum(PARTS[:number]) // sum(PARTS) for number in range(len(PARTS) + 1)]
    held, range_of = slots, 0
    for start, end in zip(starts, starts[1:]):
        share = (end - start) // 4
        quarter, rest = (slots - start) // share, (slots - start) % share
        at = start + rest + share * ((quarter // 2 ^ group) + 2 * (quarter % 2 ^ core))
        held = jnp.where((slots >= start) & (slots < end), at, held)
    for first, end in RANGES[1:]:
        range_of += jnp.where(slots >= starts[first], 1, 0)

    own_wave = to_bricks(side)
    other_wave = to_bricks(1 - side)
    matrix = two_parts(coupling_matrix(coupling))

    arrived, pieces, across = [], [], None
    source = projectors
    for number, (start, end) in enumerate(zip(starts, starts[1:])):
        share = (end - start) // 4
        start += (2 * group + core) * share
        sent = lax.dynamic_slice_in_dim(source, start, share, 0)
        if number == 0:
            sent, source = lax.optimization_barrier((sent, source))
        if number > 0:
            sent = lax.optimization_barrier((sent, arrived[0] if number == 1 else shared))[0]
        arrived.append(lax.ppermute(sent, "grid", partners))
        if number == 0:
            numbers = jnp.stack([tile_segment, tile_block, jnp.broadcast_to(tile_count, (tiles,))])
            numbers = lax.optimization_barrier((numbers, arrived[0]))[0]
            others = lax.ppermute(numbers, "grid", partners)
            shared = (others, lax.ppermute(arrived[0], "groups", swap))

    absent = segments << bits(tiles)
    segment, block = (jnp.stack([numbers[i], others[i]]) for i in (0, 1))
    codes = jnp.stack([slots, held])
    codes += (segment + (block << bits(segments + 1))) << bits(tiles)
    live = slots < jnp.stack([numbers[2], others[2]])
    keys = block + blocks * jnp.stack([jnp.zeros_like(slots), range_of])
    meta = jnp.concatenate(
        [
            jnp.stack([place, numbers[2, 0], others[2, 0]]),
            group_lists(codes, keys, live, blocks, absent),
        ]
    )

    own_wave = lax.optimization_barrier((own_wave, arrived[-1]))[0]
    own_spot = (OWN, 0, len(RANGES), 0)
    total = project(sizes, meta, own_wave, [projectors], half, width, own_spot, us=10)
    for number, mine in enumerate(arrived):
        sent = mine
        if number == 1:
            sent, across, matrix = lax.optimization_barrier((sent, across, matrix))
        if number == 2:
            sent, across, other_wave = lax.optimization_barrier((sent, across, other_wave))
        across = lax.ppermute(sent, "groups", swap) if number > 0 else shared[1]
        pieces += [mine, across]
        pieces += [lax.ppermute(mine, "band", swap), lax.ppermute(across, "band", swap)]

    for number, (first, end) in enumerate(RANGES):
        last = end == len(PARTS)
        total = project(
            sizes,
            meta,
            other_wave,
            pieces[4 * first : 4 * end],
            half,
            width,
            (OTHER, number, number + 1, starts[first]),
            total,
            last=last,
            us=0 if last else 8,
        )
    if len(total) < half:
        total = [lax.dynamic_slice_in_dim(total[0], (place ^ d) * bands, bands, 0) for d in range(half)]

    applied = couple(exchange(total), *matrix)
    applied = exchange([applied] * half)

    result = jnp.zeros((bands, npts), jnp.bfloat16)
    for which, field in (
        (1 - side, spread(sizes, meta, applied, pieces, points, OTHER)),
        (side, spread(sizes, meta, applied, [projectors], points, OWN)),
    ):
        for d, block in enumerate(exchange(field)):
            start = (which * half + (place ^ d)) * points
            result = lax.dynamic_update_slice_in_dim(result, block, start, 1)
    return result


def solution(mesh):
    in_specs = (
        P(("groups", "grid", "band"), None),
        P("grid"),
        P("grid"),
        P("grid"),
        P("grid", None, None),
        P(),
    )
    out_specs = P(("groups", "grid", "band"), None)
    return jax.shard_map(
        functools.partial(body, mesh.shape["grid"]),
        mesh=mesh,
        in_specs=in_specs,
        out_specs=out_specs,
        check_vma=False,
    )
```
